128 devices in a mesh: fsdp: 8 (over x_lo, y), ctx: 16 (over z, x_hi, core).
Axes of the slice: x: 4 (x_hi: 2, x_lo: 2; x = x_hi * 2 + x_lo), y: 4, z: 4, core: 2. Of those that a mesh axis runs over, the one named last changes fastest.
Arguments:
- layer_input: float32 [8, 3072, 1024], P('fsdp', 'ctx'), may hold values from -4 to 4
- cotangent: float32 [8, 3072, 1024], P('fsdp', 'ctx'), may hold values from -1.25 to 1.25
- w_qkv: bfloat16 [1024, 3072], P('fsdp'), may hold values from -0.1875 to 0.1875
- b_q: bfloat16 [1024], P('fsdp'), may hold values from -4 to 4
- b_v: bfloat16 [1024], P('fsdp'), may hold values from -0.8984375 to 0.8984375
- w_out: bfloat16 [1024, 1024], P('fsdp'), may hold values from -2 to 2
- b_out: bfloat16 [1024], P('fsdp'), may hold values from -3 to 3
- g_attn: bfloat16 [1024], P('fsdp'), may hold values from 0.099609375 to 1.8984375
- beta_attn: bfloat16 [1024], P('fsdp'), may hold values from -3 to 3
- w_in: bfloat16 [1024, 4096], P('fsdp'), may hold values from -0.1875 to 0.1875
- b_in: bfloat16 [4096], P('fsdp'), may hold values from -3 to 3
- w_back: bfloat16 [4096, 1024], P('fsdp'), may hold values from -0.09375 to 0.09375
- b_back: bfloat16 [1024], P('fsdp'), may hold values from -3 to 3
- g_mlp: bfloat16 [1024], P('fsdp'), may hold values from 0.099609375 to 1.8984375
- beta_mlp: bfloat16 [1024], P('fsdp'), may hold values from -3 to 3
Outputs:
- output: float32 [8, 3072, 1024], P('fsdp', 'ctx')
- grad_input: float32 [8, 3072, 1024], P('fsdp', 'ctx')
- grad_w_qkv: float32 [1024, 3072], P('fsdp')
- grad_b_q: float32 [1024], P('fsdp')
- grad_b_v: float32 [1024], P('fsdp')
- grad_w_out: float32 [1024, 1024], P('fsdp')
- grad_b_out: float32 [1024], P('fsdp')
- grad_g_attn: float32 [1024], P('fsdp')
- grad_beta_attn: float32 [1024], P('fsdp')
- grad_w_in: float32 [1024, 4096], P('fsdp')
- grad_b_in: float32 [4096], P('fsdp')
- grad_w_back: float32 [4096, 1024], P('fsdp')
- grad_b_back: float32 [1024], P('fsdp')
- grad_g_mlp: float32 [1024], P('fsdp')
- grad_beta_mlp: float32 [1024], P('fsdp')
The draws below stay inside these ranges and needn't reach their ends.
All inputs are finite; a program needn't handle non-finite values.
Results may differ from the reference program's by a relative error of at most 0.025.
Values may be sent and summed in bfloat16 or wider, within the bound.
A program may use at most 192 MiB of HBM per device.

```python
import math
import jax
import jax.numpy as jnp
from jax import lax

D = 1024
HEADS = 16
HEAD_DIM = 64
FF = 4096
SEQS = 8
LEN = 3072


def draw_layer_input(key, part):
    base_key = jax.random.fold_in(key, 11)
    return jax.random.truncated_normal(base_key, -4.0, 4.0, (SEQS, LEN, D), jnp.float32)


def shard_levels(own_key, dims, cuts, smallest, top_value):
    def one(dim, shards_of):
        heights = jax.random.uniform(jax.random.fold_in(jax.random.fold_in(own_key, 6), dim), (shards_of,), jnp.float32, smallest / len(cuts), top_value / len(cuts))
        return jnp.repeat(jnp.exp(heights), dims[dim] // shards_of).reshape((-1,) + (1,) * (len(dims) - dim - 1))

    loudness = one(*cuts[0])
    for cut in cuts[1:]:
        loudness = loudness * one(*cut)
    return loudness


def centred(rng, shape, deviation, reach, pieces=(), dtype=jnp.bfloat16):
    result = jax.random.normal(rng, shape, jnp.float32) * deviation
    if len(pieces) > 0:
        result = shard_levels(rng, shape, pieces, -0.22, 0.18) * result
    return jnp.clip(result, min=-reach, max=reach).astype(dtype)


def setup_inputs(seed: int = 0) -> dict:
    seeds = jax.random.split(jax.random.key(seed), 16)
    layer_input = draw_layer_input(jax.random.fold_in(seeds[15], 71), 0)
    cotangent = centred(seeds[1], (SEQS, LEN, D), 0.25, 1.25, ((0, 8), (1, 16)), jnp.float32)
    w_qkv = centred(seeds[2], (D, 3 * D), D ** -0.5, 0.1875, ((0, 8),))
    b_q = centred(seeds[3], (D,), 1.0, 4.0, ((0, 8),))
    b_v = centred(seeds[4], (D,), 0.15, 0.8984375, ((0, 8),))
    w_out = centred(seeds[5], (D, D), (max(8, 16 * D // LEN)) ** -0.5, 2.0, ((0, 8),))
    b_out = centred(seeds[6], (D,), 0.5, 3.0, ((0, 8),))
    g_attn = jnp.clip(1.0 + 0.18 * jax.random.normal(seeds[7], (D,), jnp.float32), 0.099609375, 1.8984375).astype(jnp.bfloat16)
    beta_attn = centred(seeds[8], (D,), 0.5, 3.0, ((0, 8),))
    w_in = centred(seeds[9], (D, FF), D ** -0.5, 0.1875, ((0, 8),))
    b_in = centred(seeds[10], (FF,), 0.5, 3.0, ((0, 8),))
    w_back = centred(seeds[11], (FF, D), FF ** -0.5, 0.09375, ((0, 8),))
    b_back = centred(seeds[12], (D,), 0.5, 3.0, ((0, 8),))
    g_mlp = jnp.clip(1.0 + 0.18 * jax.random.normal(seeds[13], (D,), jnp.float32), 0.099609375, 1.8984375).astype(jnp.bfloat16)
    beta_mlp = centred(seeds[14], (D,), 0.5, 3.0, ((0, 8),))
    return dict(layer_input=layer_input, cotangent=cotangent, w_qkv=w_qkv, b_q=b_q, b_v=b_v, w_out=w_out, b_out=b_out, g_attn=g_attn, beta_attn=beta_attn, w_in=w_in, b_in=b_in, w_back=w_back, b_back=b_back, g_mlp=g_mlp, beta_mlp=beta_mlp)


EPSILON = 1e-05
ROOT_HALF = 0.7071067811865476
INV_ROOT_TWO_PI = 0.3989422804014327

def rounded(values):
    return lax.optimization_barrier(values.astype(jnp.bfloat16))

def widened(values):
    return values.astype(jnp.float32)

def layer_norm(hidden, gain, offset):
    center = hidden - lax.optimization_barrier(jnp.mean(hidden, axis=-1, keepdims=True))
    inverse = lax.rsqrt(lax.optimization_barrier(jnp.mean(center * center, axis=-1, keepdims=True)) + EPSILON)
    normed = center * inverse
    return (normed * gain + offset, normed, inverse)

def norm_back(upstream, normed, inverse, gain):
    scaled = upstream * gain
    return inverse * (scaled - lax.optimization_barrier(jnp.mean(scaled, axis=-1, keepdims=True)) - normed * lax.optimization_barrier(jnp.mean(scaled * normed, axis=-1, keepdims=True)))

def gelu_value(inputs):
    return 0.5 * inputs * (1.0 + jax.scipy.special.erf(inputs * ROOT_HALF))

def gelu_slope(inputs):
    return 0.5 * (1.0 + jax.scipy.special.erf(inputs * ROOT_HALF)) + inputs * jnp.exp(-0.5 * inputs * inputs) * INV_ROOT_TWO_PI

def reference(layer_input, cotangent, w_qkv, b_q, b_v, w_out, b_out, g_attn, beta_attn, w_in, b_in, w_back, b_back, g_mlp, beta_mlp):
    block_rows = min(512, LEN)
    block_count = LEN // block_rows
    scale = 1.0 / math.sqrt(HEAD_DIM)
    rows = layer_input.reshape(-1, D)
    rows_low = rows.astype(jnp.bfloat16)
    projected = jnp.dot(rows_low, w_qkv, preferred_element_type=jnp.float32)
    query = rounded((projected[:, :D] + widened(b_q)) * scale)
    keys = rounded(projected[:, D:2 * D])
    values = rounded(projected[:, 2 * D:] + widened(b_v))
    query_blocks = widened(query).reshape(SEQS, block_count, block_rows, HEADS, HEAD_DIM)
    key_seqs = widened(keys).reshape(SEQS, LEN, HEADS, HEAD_DIM)
    value_seqs = widened(values).reshape(SEQS, LEN, HEADS, HEAD_DIM)

    def forward_sequence(operands):
        query_seq, key_seq, value_seq = operands

        def forward_block(query_block):
            scores = jnp.einsum('qhd,khd->hqk', query_block, key_seq)
            highest = lax.optimization_barrier(jnp.max(scores, axis=-1, keepdims=True))
            log_total = highest[..., 0] + jnp.log(lax.optimization_barrier(jnp.sum(jnp.exp(scores - highest), axis=-1)))
            weights = widened(rounded(jnp.exp(scores - log_total[..., None])))
            return (jnp.einsum('hqk,khd->qhd', weights, value_seq), log_total)
        return lax.map(forward_block, query_seq)
    mixed_blocks, log_totals = lax.map(forward_sequence, (query_blocks, key_seqs, value_seqs))
    mixed = rounded(mixed_blocks.reshape(-1, D))
    first_sum = rows + jnp.dot(mixed, w_out, preferred_element_type=jnp.float32) + widened(b_out)
    first_out, first_normed, first_inverse = layer_norm(first_sum, widened(g_attn), widened(beta_attn))
    first_low = first_out.astype(jnp.bfloat16)
    pre_act = jnp.dot(first_low, w_in, preferred_element_type=jnp.float32) + widened(b_in)
    activated = gelu_value(pre_act).astype(jnp.bfloat16)
    second_sum = first_out + jnp.dot(activated, w_back, preferred_element_type=jnp.float32) + widened(b_back)
    output, second_normed, second_inverse = layer_norm(second_sum, widened(g_mlp), widened(beta_mlp))
    upstream = cotangent.reshape(-1, D)
    grad_g_mlp = lax.optimization_barrier(jnp.sum(upstream * second_normed, axis=0))
    grad_beta_mlp = lax.optimization_barrier(jnp.sum(upstream, axis=0))
    grad_second = norm_back(upstream, second_normed, second_inverse, widened(g_mlp))
    grad_b_back = lax.optimization_barrier(jnp.sum(grad_second, axis=0))
    grad_second_low = grad_second.astype(jnp.bfloat16)
    grad_w_back = jnp.dot(activated.T, grad_second_low, preferred_element_type=jnp.float32)
    grad_pre = jnp.dot(grad_second_low, w_back.T, preferred_element_type=jnp.float32) * gelu_slope(pre_act)
    grad_b_in = lax.optimization_barrier(jnp.sum(grad_pre, axis=0))
    grad_pre_low = grad_pre.astype(jnp.bfloat16)
    grad_w_in = jnp.dot(first_low.T, grad_pre_low, preferred_element_type=jnp.float32)
    grad_first_out = grad_second + jnp.dot(grad_pre_low, w_in.T, preferred_element_type=jnp.float32)
    grad_g_attn = lax.optimization_barrier(jnp.sum(grad_first_out * first_normed, axis=0))
    grad_beta_attn = lax.optimization_barrier(jnp.sum(grad_first_out, axis=0))
    grad_first = norm_back(grad_first_out, first_normed, first_inverse, widened(g_attn))
    grad_b_out = lax.optimization_barrier(jnp.sum(grad_first, axis=0))
    grad_first_low = grad_first.astype(jnp.bfloat16)
    grad_w_out = jnp.dot(mixed.T, grad_first_low, preferred_element_type=jnp.float32)
    grad_mixed = rounded(jnp.dot(grad_first_low, w_out.T, preferred_element_type=jnp.float32))
    delta = lax.optimization_barrier(jnp.sum((widened(grad_mixed) * widened(mixed)).reshape(SEQS, block_count, block_rows, HEADS, HEAD_DIM), axis=-1))
    delta = delta.transpose(0, 1, 3, 2)
    grad_mixed_blocks = widened(grad_mixed).reshape(SEQS, block_count, block_rows, HEADS, HEAD_DIM)

    def backward_sequence(operands):
        query_seq, key_seq, value_seq, grad_seq, log_seq, delta_seq = operands

        def backward_block(carry, block):
            grad_key_acc, grad_value_acc = carry
            query_block, grad_block, log_block, delta_block = block
            scores = jnp.einsum('qhd,khd->hqk', query_block, key_seq)
            prob = jnp.exp(scores - log_block[..., None])
            grad_value_acc = grad_value_acc + jnp.einsum('hqk,qhd->khd', widened(rounded(prob)), grad_block)
            grad_prob = jnp.einsum('qhd,khd->hqk', grad_block, value_seq)
            grad_scores = widened(rounded(prob * (grad_prob - delta_block[..., None])))
            grad_query_block = jnp.einsum('hqk,khd->qhd', grad_scores, key_seq)
            grad_key_acc = grad_key_acc + jnp.einsum('hqk,qhd->khd', grad_scores, query_block)
            return ((grad_key_acc, grad_value_acc), grad_query_block)
        empty = jnp.zeros((LEN, HEADS, HEAD_DIM), jnp.float32)
        (grad_key_seq, grad_value_seq), grad_query_seq = lax.scan(backward_block, (empty, empty), (query_seq, grad_seq, log_seq, delta_seq))
        return (grad_query_seq, grad_key_seq, grad_value_seq)
    grad_query, grad_keys, grad_values = lax.map(backward_sequence, (query_blocks, key_seqs, value_seqs, grad_mixed_blocks, log_totals, delta))
    grad_query = grad_query.reshape(-1, D) * scale
    grad_keys = grad_keys.reshape(-1, D)
    grad_values = grad_values.reshape(-1, D)
    grad_b_q = lax.optimization_barrier(jnp.sum(grad_query, axis=0))
    grad_b_v = lax.optimization_barrier(jnp.sum(grad_values, axis=0))
    grad_proj = jnp.concatenate([grad_query, grad_keys, grad_values], axis=1).astype(jnp.bfloat16)
    grad_w_qkv = jnp.dot(rows_low.T, grad_proj, preferred_element_type=jnp.float32)
    grad_input = grad_first + jnp.dot(grad_proj, w_qkv.T, preferred_element_type=jnp.float32)
    return (output.reshape(layer_input.shape), grad_input.reshape(layer_input.shape), grad_w_qkv, grad_b_q, grad_b_v, grad_w_out, grad_b_out, grad_g_attn, grad_beta_attn, grad_w_in, grad_b_in, grad_w_back, grad_b_back, grad_g_mlp, grad_beta_mlp)
```

```python
import functools
import math

import jax
import jax.numpy as jnp
from jax import lax
from jax.experimental import pallas as pl
from jax.experimental.pallas import tpu as pltpu
from jax.sharding import PartitionSpec as P

HEADS = 16
HEAD_DIM = 64
EPSILON = 1e-05
ROOT_HALF = 0.7071067811865476
INV_ROOT_TWO_PI = 0.3989422804014327
BF16 = jnp.bfloat16
F32 = jnp.float32
MESH = pl.DeviceIdType.MESH
UNITS = 12
MIB = 2**20


def place():
    fsdp, ctx = lax.axis_index("fsdp"), lax.axis_index("ctx")
    return (lax.rem(ctx // 2, 2) * 2 + fsdp // 4, lax.rem(fsdp, 4), ctx // 4, lax.rem(ctx, 2))


def device_at(x, y, z, core):
    x, y, z, core = (lax.rem(x + 4, 4), lax.rem(y + 4, 4), lax.rem(z + 4, 4), lax.rem(core, 2))
    return {"fsdp": lax.rem(x, 2) * 4 + y, "ctx": z * 4 + (x // 2) * 2 + core}


def greet(devices):
    barrier = pltpu.get_barrier_semaphore()
    for device in devices:
        pl.semaphore_signal(barrier, inc=1, device_id=device, device_id_type=MESH)
    pl.semaphore_wait(barrier, len(devices))


def remote(src, dst, send, recv, device):
    return pltpu.make_async_remote_copy(
        src_ref=src, dst_ref=dst, send_sem=send, recv_sem=recv, device_id=device, device_id_type=MESH
    )


GROUPS = 6


def gather_kernel(pk, small, full, smalls, own_sem, y_s, y_r, x_s, x_r, c_s, c_r, s_s, s_r):
    x, y, z, core = place()
    low = lax.rem(x, 2)
    shard = low * 4 + y
    per = UNITS // GROUPS
    half = per // 2
    rows = pl.ds(pl.multiple_of(core * 64, 64), 64)
    sibling = device_at(x, y, z, core + 1)
    ys = {d: device_at(x, y + d, z, core) for d in (1, 2, 3)}
    xs = [device_at(x + 1, y, z, core), device_at(x - 1, y, z, core)]
    across = {(a, d): device_at(x + a, y + d, z, core) for a in (0, 1) for d in range(4) if (a, d) != (0, 0)}
    greet([sibling] + xs + list(ys.values()) + [device_at(x - 1, y - d, z, core) for d in (1, 2, 3)])

    own = pltpu.make_async_copy(pk, full.at[:, shard], own_sem.at[0])
    own.start()
    own_small = pltpu.make_async_copy(small, smalls.at[shard], own_sem.at[1])
    own_small.start()
    small_copies = []
    for i, device in enumerate(across.values()):
        copy = remote(small, smalls.at[shard], s_s.at[i], s_r.at[i], device)
        copy.start()
        small_copies.append(copy)

    def y_copy(g, d):
        units = pl.ds(g * per, per)
        return remote(pk.at[units, rows], full.at[units, shard, rows], y_s.at[g, d - 1], y_r.at[g, d - 1], ys[d])

    def x_copy(g, e, way):
        units = pl.ds(g * per + way * half, half)
        block = low * 4 + lax.rem(y - e + 4, 4)
        src = pk.at[units, rows] if e == 0 else full.at[units, block, rows]
        return remote(src, full.at[units, block, rows], x_s.at[g, e, way], x_r.at[g, e, way], xs[way])

    def c_copy(g, which):
        if which < 3:
            block = low * 4 + lax.rem(y - which + 3, 4)
            units = pl.ds(g * per, per)
        else:
            e, way = (which - 3) // 2, (which - 3) % 2
            block = (1 - low) * 4 + lax.rem(y - e + 4, 4)
            units = pl.ds(g * per + way * half, half)
        ref = full.at[units, block, rows]
        return remote(ref, ref, c_s.at[g, which], c_r.at[g, which], sibling)

    def first(g, _):
        for d in (1, 3, 2):
            y_copy(g, d).start()
        for way in (0, 1):
            x_copy(g, 0, way).start()
        return 0

    def second(g, _):
        for d in (1, 3, 2):
            y_copy(g, d).wait_recv()
            for way in (0, 1):
                x_copy(g, d, way).start()
            c_copy(g, d - 1).start()
        for way in (0, 1):
            x_copy(g, 0, way).wait_recv()
            c_copy(g, 3 + way).start()
        return 0

    def third(g, _):
        for e in (1, 3, 2):
            for way in (0, 1):
                x_copy(g, e, way).wait_recv()
                c_copy(g, 3 + 2 * e + way).start()
        return 0

    def last(g, _):
        for d in (1, 2, 3):
            y_copy(g, d).wait_send()
        for e in range(4):
            for way in (0, 1):
                x_copy(g, e, way).wait_send()
        for which in range(11):
            c_copy(g, which).wait()
        return 0

    for body in (first, second, third, last):
        lax.fori_loop(0, GROUPS, body, 0)
    own.wait()
    own_small.wait()
    for copy in small_copies:
        copy.wait()


def gather(pk, small):
    any_space = pl.BlockSpec(memory_space=pl.ANY)
    dma = pltpu.SemaphoreType.DMA
    return pl.pallas_call(
        gather_kernel,
        out_shape=(
            jax.ShapeDtypeStruct((UNITS, 8, 128, 1024), BF16),
            jax.ShapeDtypeStruct((8, 16, 128), BF16),
        ),
        in_specs=[any_space, any_space],
        out_specs=(any_space, any_space),
        scratch_shapes=[
            dma((2,)),
            dma((GROUPS, 3)),
            dma((GROUPS, 3)),
            dma((GROUPS, 4, 2)),
            dma((GROUPS, 4, 2)),
            dma((GROUPS, 11)),
            dma((GROUPS, 11)),
            dma((7,)),
            dma((7,)),
        ],
        compiler_params=pltpu.CompilerParams(collective_id=1, has_side_effects=True),
        name="gather_params",
    )(pk, small)


BLOCK = 256


def peers():
    fsdp, me = lax.axis_index("fsdp"), lax.axis_index("ctx")
    return me, [(lax.rem(me + d, 16), {"fsdp": fsdp, "ctx": lax.rem(me + d, 16)}) for d in range(1, 16)]


def exchange(src, dst, me, others, sends, recvs, local):
    copies = []
    for i, (other, device) in enumerate(others):
        copy = remote(src.at[other], dst.at[me], sends.at[i], recvs.at[i], device)
        copy.start()
        copies.append(copy)
    mine = pltpu.make_async_copy(src.at[me], dst.at[me], local)
    mine.start()
    mine.wait()
    for copy in copies:
        copy.wait()


def flipped(value):
    return value.astype(F32).T.astype(BF16)


def dot(a, b):
    return jnp.dot(a, b, preferred_element_type=F32)


def forward_kernel(send, got, o_t, log_total, mixed, k_all, q_t, v_t, o_send, a_s, a_r, b_s, b_r, local):
    me, others = peers()
    greet([device for _, device in others])
    exchange(send, got, me, others, a_s, a_r, local.at[0])

    def unpack(j, _):
        rows = pl.ds(pl.multiple_of(j * 192, 64), 192)
        k_all[rows, :] = got[j, 0:192, 64:128]
        return 0

    lax.fori_loop(0, 16, unpack, 0)
    for j in range(16):
        span = slice(j * 192, (j + 1) * 192)
        both = got[j, 0:192, :].astype(F32).T
        q_t[:, span] = both[0:64].astype(BF16)
        pair = got[j, 192:288, :].astype(F32).T
        v_t[0:64, span] = jnp.concatenate([pair[0:64], pair[64:128]], axis=1).astype(BF16)
    v_t[64:80, :] = jnp.ones((16, 3072), BF16)

    def block(i, _):
        span = pl.ds(pl.multiple_of(i * BLOCK, BLOCK), BLOCK)
        scores = dot(k_all[...], q_t[:, span])
        highest = jnp.max(scores, axis=0, keepdims=True)
        weights = jnp.exp(scores - highest).astype(BF16)
        out = dot(v_t[...], weights)
        total = out[64:65]
        o_t[:, span] = (out[0:64] / total).astype(BF16)
        log_total[:, span] = highest + jnp.log(total)
        return 0

    lax.fori_loop(0, 3072 // BLOCK, block, 0)
    for j in range(16):
        part = o_t[:, j * 192 : (j + 1) * 192].astype(F32)
        stacked = jnp.concatenate([part[:, 0:96], part[:, 96:192]], axis=0)
        o_send[j] = stacked.T.astype(BF16)
    exchange(o_send, mixed, me, others, b_s, b_r, local.at[1])


def forward_attention(send):
    vmem = pl.BlockSpec(memory_space=pltpu.VMEM)
    dma = pltpu.SemaphoreType.DMA
    return pl.pallas_call(
        forward_kernel,
        out_shape=(
            jax.ShapeDtypeStruct((16, 288, 128), BF16),
            jax.ShapeDtypeStruct((64, 3072), BF16),
            jax.ShapeDtypeStruct((1, 3072), F32),
            jax.ShapeDtypeStruct((16, 96, 128), BF16),
        ),
        in_specs=[vmem],
        out_specs=(vmem, vmem, vmem, vmem),
        scratch_shapes=[
            pltpu.VMEM((3072, 64), BF16),
            pltpu.VMEM((64, 3072), BF16),
            pltpu.VMEM((80, 3072), BF16),
            pltpu.VMEM((16, 96, 128), BF16),
            dma((15,)),
            dma((15,)),
            dma((15,)),
            dma((15,)),
            dma((2,)),
        ],
        compiler_params=pltpu.CompilerParams(collective_id=2, has_side_effects=True, vmem_limit_bytes=50 * MIB),
        name="attention_forward",
    )(send)


def backward_kernel(send, got, o_t, log_total, back, do_got, k_all, v_all, q_all, q_t, k_t, do_all, do_t, delta,
                    dq_t, dk, dv, out_send, a_s, a_r, b_s, b_r, local):
    me, others = peers()
    greet([device for _, device in others])
    exchange(send, do_got, me, others, a_s, a_r, local.at[0])
    for j in range(16):
        span = slice(j * 192, (j + 1) * 192)
        q_all[span, :] = got[j, 0:192, 0:64]
        k_all[span, :] = got[j, 0:192, 64:128]
        v_all[j * 192 : j * 192 + 96, :] = got[j, 192:288, 0:64]
        v_all[j * 192 + 96 : j * 192 + 192, :] = got[j, 192:288, 64:128]
        do_all[j * 192 : j * 192 + 96, :] = do_got[j, :, 0:64]
        do_all[j * 192 + 96 : j * 192 + 192, :] = do_got[j, :, 64:128]
        both = got[j, 0:192, :].astype(F32).T
        q_t[:, span] = both[0:64].astype(BF16)
        k_t[:, span] = both[64:128].astype(BF16)
        pair = do_got[j].astype(F32).T
        flat = jnp.concatenate([pair[0:64], pair[64:128]], axis=1)
        do_t[:, span] = flat.astype(BF16)
        delta[:, span] = jnp.sum(flat * o_t[:, span].astype(F32), axis=0, keepdims=True)
    dk[...] = jnp.zeros_like(dk)
    dv[...] = jnp.zeros_like(dv)

    def block(i, _):
        span = pl.ds(pl.multiple_of(i * BLOCK, BLOCK), BLOCK)
        prob = jnp.exp(dot(k_all[...], q_t[:, span]) - log_total[:, span])
        grad_prob = dot(v_all[...], do_t[:, span])
        dv[...] += dot(prob.astype(BF16), do_all[span, :])
        grad_scores = (prob * (grad_prob - delta[:, span])).astype(BF16)
        dk[...] += dot(grad_scores, q_all[span, :])
        dq_t[:, span] = dot(k_t[...], grad_scores) * 0.125
        return 0

    lax.fori_loop(0, 3072 // BLOCK, block, 0)
    for j in range(16):
        span = slice(j * 192, (j + 1) * 192)
        dq = dq_t[:, span].T
        out_send[j, 0:192, :] = jnp.concatenate([dq, dk[span, :]], axis=1).astype(BF16)
        out_send[j, 192:288, :] = jnp.concatenate(
            [dv[j * 192 : j * 192 + 96, :], dv[j * 192 + 96 : j * 192 + 192, :]], axis=1
        ).astype(BF16)
    exchange(out_send, back, me, others, b_s, b_r, local.at[1])


def backward_attention(send, got, o_t, log_total):
    vmem = pl.BlockSpec(memory_space=pltpu.VMEM)
    dma = pltpu.SemaphoreType.DMA
    return pl.pallas_call(
        backward_kernel,
        out_shape=jax.ShapeDtypeStruct((16, 288, 128), BF16),
        in_specs=[vmem] * 4,
        out_specs=vmem,
        scratch_shapes=[
            pltpu.VMEM((16, 96, 128), BF16),
            pltpu.VMEM((3072, 64), BF16),
            pltpu.VMEM((3072, 64), BF16),
            pltpu.VMEM((3072, 64), BF16),
            pltpu.VMEM((64, 3072), BF16),
            pltpu.VMEM((64, 3072), BF16),
            pltpu.VMEM((3072, 64), BF16),
            pltpu.VMEM((64, 3072), BF16),
            pltpu.VMEM((1, 3072), F32),
            pltpu.VMEM((64, 3072), F32),
            pltpu.VMEM((3072, 64), F32),
            pltpu.VMEM((3072, 64), F32),
            pltpu.VMEM((16, 288, 128), BF16),
            dma((15,)),
            dma((15,)),
            dma((15,)),
            dma((15,)),
            dma((2,)),
        ],
        compiler_params=pltpu.CompilerParams(collective_id=3, has_side_effects=True, vmem_limit_bytes=50 * MIB),
        name="attention_backward",
    )(send, got, o_t, log_total)


def reduce_kernel(n, *refs):
    units = refs[:n]
    sm = refs[n]
    out, sm_out = refs[n + 1 : n + 3]
    (acc, near, a_buf, b_buf, c_buf, final, s0, s1, s2, s3, l_s, n_s, n_r, a_s, a_r, b_s, b_r, c_s, c_r,
     d_s, d_r, e_s, e_r, t_s, t_r) = refs[n + 3 :]
    per = n // 3
    x, y, z, core = place()
    low, high = lax.rem(x, 2), x // 2
    at = (x, y, z)
    sibling = device_at(x, y, z, core + 1)
    mine = pl.ds(pl.multiple_of(core * 512, 512), 512)
    theirs = pl.ds(pl.multiple_of((1 - core) * 512, 512), 512)

    def line(axis, d):
        to = list(at)
        to[axis] = lax.rem(to[axis] + d, 4)
        return to[axis], device_at(*to, core)

    lines = [line(axis, d)[1] for axis in range(3) for d in (1, 2, 3)]
    plane = [device_at(x + a, y, z + d, core) for a in (0, 2) for d in range(4) if (a, d) != (0, 0)]
    greet([sibling] + lines + [plane[i] for i in (4, 5, 6)])

    t_copies = [remote(sm, s0, t_s.at[0], t_r.at[0], sibling)]
    t_copies[0].start()

    loads, nears = [], []
    order = [p * per + i for i in range(per) for p in range(3)]
    for u in order:
        copy = remote(units[u].at[:, :, :, :, :, theirs], near.at[u], n_s.at[u], n_r.at[u], sibling)
        copy.start()
        load = pltpu.make_async_copy(units[u].at[:, :, :, :, :, mine], acc.at[u], l_s.at[u])
        load.start()
        nears.append(copy)
        loads.append(load)
    for u, copy, load in zip(order, nears, loads):
        load.wait()
        copy.wait_recv()

        def pair(i, _, u=u):
            a, b = i // 4, lax.rem(i, 4)
            acc[u, a, b] = (acc[u, a, b].astype(F32) + near[u, a, b].astype(F32)).astype(BF16)
            return 0

        lax.fori_loop(0, 8, pair, 0)

    def part(ref, p):
        return ref.at[pl.ds(p * per, per)]

    def first_piece(p, c):
        whole = part(acc, p)
        if p == 0:
            return whole.at[:, lax.rem(c, 2), :, :, c // 2]
        if p == 1:
            return whole.at[:, :, c]
        return whole.at[:, :, :, c]

    def second_piece(p, ref, c):
        if p == 0:
            return ref.at[:, c]
        if p == 1:
            return ref.at[:, :, c]
        return ref.at[:, lax.rem(c, 2), :, c // 2]

    def third_piece(p, ref, c):
        if p == 0:
            return ref.at[:, c]
        if p == 1:
            return ref.at[:, lax.rem(c, 2), c // 2]
        return ref.at[:, c]

    def scatter(stage, pieces, bufs, sends, recvs):
        copies = []
        for d in (1, 3, 2):
            for p in range(3):
                axis = (p + stage) % 3
                c, device = line(axis, d)
                copy = remote(pieces[p](c), bufs[p].at[d - 1], sends.at[p, d - 1], recvs.at[p, d - 1], device)
                copy.start()
                copies.append(copy)
        return copies

    def add_up(stage, pieces, bufs):
        for p in range(3):
            axis = (p + stage) % 3
            own = pieces[p](at[axis])
            buf = bufs[p]

            def one(i, _, own=own, buf=buf):
                own[i] = (
                    own[i].astype(F32) + buf[0, i].astype(F32) + buf[1, i].astype(F32) + buf[2, i].astype(F32)
                ).astype(BF16)
                return 0

            lax.fori_loop(0, per, one, 0)

    a_bufs = list(a_buf)
    firsts = [functools.partial(first_piece, p) for p in range(3)]
    a_copies = scatter(0, firsts, a_bufs, a_s, a_r)

    def settle(buf, parts):
        total = parts[0]
        for other in parts[1:]:
            total = total + other
        return total

    t_copies[0].wait()
    s0[...] = s0[...] + sm[...]

    def small_stage(stage, axis, piece, buf):
        copies = []
        me = at[axis]
        for d in (1, 2, 3):
            c, device = line(axis, d)
            slot = 1 + 3 * stage + d - 1
            copies.append(remote(piece(c), buf.at[me], t_s.at[slot], t_r.at[slot], device))
            copies[-1].start()
        own = pltpu.make_async_copy(piece(me), buf.at[me], l_s.at[n + stage])
        own.start()
        own.wait()
        for copy in copies:
            copy.wait()

    small_stage(0, 1, lambda c: s0.at[:, c], s1)
    s0[:, 0] = s1[0] + s1[1] + s1[2] + s1[3]
    small_stage(1, 0, lambda c: s0.at[lax.rem(c, 2), 0], s2)
    s0[0, 1] = s2[0] + s2[1] + s2[2] + s2[3]
    small_stage(2, 2, lambda c: s0.at[0, 1], s3)
    sm_out[...] = s3[0] + s3[1] + s3[2] + s3[3]

    for copy in a_copies:
        copy.wait()
    add_up(0, firsts, a_bufs)

    def of(p, k):
        return firsts[p](at[p]) if k == 1 else second_piece(p, firsts[p](at[p]), at[(p + 1) % 3])

    seconds = [lambda c, p=p: second_piece(p, of(p, 1), c) for p in range(3)]
    b_bufs = list(b_buf)
    b_copies = scatter(1, seconds, b_bufs, b_s, b_r)
    for copy in b_copies:
        copy.wait()
    add_up(1, seconds, b_bufs)
    thirds = [lambda c, p=p: third_piece(p, of(p, 2), c) for p in range(3)]
    c_bufs = [c_buf.at[p] for p in range(3)]
    c_copies = scatter(2, thirds, c_bufs, c_s, c_r)
    for copy in c_copies:
        copy.wait()
    for p in range(3):
        own = thirds[p](at[(p + 2) % 3])
        for i in range(per):
            final[p * per + i] = (
                own[i].astype(F32)
                + c_buf[p, 0, i].astype(F32)
                + c_buf[p, 1, i].astype(F32)
                + c_buf[p, 2, i].astype(F32)
            ).astype(BF16)

    d_copies = []
    for i, device in enumerate(plane):
        copy = remote(final, out.at[:, z, high, :, mine], d_s.at[i], d_r.at[i], device)
        copy.start()
        d_copies.append(copy)
    own = pltpu.make_async_copy(final, out.at[:, z, high, :, mine], l_s.at[n + 3])
    own.start()
    own.wait()
    e_copies = [remote(final, out.at[:, z, high, :, mine], e_s.at[0], e_r.at[0], sibling)]
    e_copies[0].start()
    i = 0
    for a in (0, 2):
        for d in range(4):
            if (a, d) == (0, 0):
                continue
            d_copies[i].wait_recv()
            ref = out.at[:, lax.rem(z - d + 4, 4), lax.rem(high + a // 2, 2), :, mine]
            copy = remote(ref, ref, e_s.at[1 + i], e_r.at[1 + i], sibling)
            copy.start()
            e_copies.append(copy)
            i += 1
    for copy in nears + d_copies:
        copy.wait_send()
    for copy in e_copies:
        copy.wait()


def reduce(units, sm):
    n = len(units)
    per = n // 3
    any_space = pl.BlockSpec(memory_space=pl.ANY)
    vmem = pl.BlockSpec(memory_space=pltpu.VMEM)
    dma = pltpu.SemaphoreType.DMA
    return pl.pallas_call(
        functools.partial(reduce_kernel, n),
        out_shape=(
            jax.ShapeDtypeStruct((n, 4, 2, 16, 1024), BF16),
            jax.ShapeDtypeStruct((16, 128), F32),
        ),
        in_specs=[any_space] * n + [vmem],
        out_specs=(vmem, vmem),
        scratch_shapes=[
            pltpu.VMEM((n, 2, 4, 4, 2, 16, 512), BF16),
            pltpu.VMEM((n, 2, 4, 4, 2, 16, 512), BF16),
            (
                pltpu.VMEM((3, per, 4, 4, 16, 512), BF16),
                pltpu.VMEM((3, per, 2, 4, 2, 16, 512), BF16),
                pltpu.VMEM((3, per, 2, 4, 2, 16, 512), BF16),
            ),
            (
                pltpu.VMEM((3, per, 4, 16, 512), BF16),
                pltpu.VMEM((3, per, 2, 2, 16, 512), BF16),
                pltpu.VMEM((3, per, 4, 16, 512), BF16),
            ),
            pltpu.VMEM((3, 3, per, 16, 512), BF16),
            pltpu.VMEM((n, 16, 512), BF16),
            pltpu.VMEM((2, 4, 16, 128), F32),
            pltpu.VMEM((4, 2, 16, 128), F32),
            pltpu.VMEM((4, 16, 128), F32),
            pltpu.VMEM((4, 16, 128), F32),
            dma((n + 4,)),
            dma((n,)),
            dma((n,)),
            dma((3, 3)),
            dma((3, 3)),
            dma((3, 3)),
            dma((3, 3)),
            dma((3, 3)),
            dma((3, 3)),
            dma((7,)),
            dma((7,)),
            dma((8,)),
            dma((8,)),
            dma((10,)),
            dma((10,)),
        ],
        compiler_params=pltpu.CompilerParams(collective_id=4, has_side_effects=True, vmem_limit_bytes=58 * MIB),
        name="reduce_gradients",
    )(*[unit.reshape(2, 4, 4, 2, 16, 1024) for unit in units], sm)


def widened(values):
    return values.astype(F32)


def layer_norm(hidden, gain, offset):
    center = hidden - jnp.mean(hidden, axis=-1, keepdims=True)
    inverse = lax.rsqrt(jnp.mean(center * center, axis=-1, keepdims=True) + EPSILON)
    normed = center * inverse
    return (normed * gain + offset, normed, inverse)


def norm_back(upstream, normed, inverse, gain):
    scaled = upstream * gain
    return inverse * (
        scaled
        - jnp.mean(scaled, axis=-1, keepdims=True)
        - normed * jnp.mean(scaled * normed, axis=-1, keepdims=True)
    )


def gelu_value(inputs):
    return 0.5 * inputs * (1.0 + jax.scipy.special.erf(inputs * ROOT_HALF))


def gelu_slope(inputs):
    return (
        0.5 * (1.0 + jax.scipy.special.erf(inputs * ROOT_HALF))
        + inputs * jnp.exp(-0.5 * inputs * inputs) * INV_ROOT_TWO_PI
    )


def by_head(value):
    return value.reshape(-1, HEADS, HEAD_DIM).transpose(1, 0, 2)


def folded(value):
    half = value.shape[1] // 2
    return jnp.concatenate([value[:, :half], value[:, half:]], axis=2)


def unfolded(value):
    return jnp.concatenate([value[:, :, :HEAD_DIM], value[:, :, HEAD_DIM:]], axis=1)


def by_token(value):
    return value.transpose(1, 0, 2).reshape(-1, HEADS * HEAD_DIM)


def dot_nt(a, b):
    return lax.dot_general(a, b, (((1,), (1,)), ((), ())), preferred_element_type=F32)


def dot_tn(a, b):
    return lax.dot_general(a, b, (((0,), (0,)), ((), ())), preferred_element_type=F32)


def shards(layer_input, cotangent, w_qkv, b_q, b_v, w_out, b_out, g_attn, beta_attn, w_in, b_in, w_back, b_back,
           g_mlp, beta_mlp):
    width = layer_input.shape[-1]
    scale = 1.0 / math.sqrt(HEAD_DIM)
    in_units = w_in.reshape(128, 8, 4, 128).transpose(2, 0, 1, 3).reshape(4, 128, width)
    pk = jnp.concatenate(
        [w_qkv.reshape(128, 3, width).transpose(1, 0, 2), w_out[None], in_units, w_back.reshape(4, 128, width)]
    )
    small = jnp.concatenate(
        [jnp.stack([b_q, b_v, b_out, g_attn, beta_attn, b_back, g_mlp, beta_mlp]), b_in.reshape(4, 128),
         jnp.zeros((4, 128), BF16)]
    )
    full, smalls = gather(pk, small)
    full = full.reshape(UNITS, width, width)
    smalls = widened(smalls.transpose(1, 0, 2).reshape(16, width))
    bq, bv, bout, gattn, battn, bback, gmlp, bmlp = (smalls[i] for i in range(8))
    bin_ = [smalls[8 + j] for j in range(4)]

    rows = layer_input.reshape(-1, width)
    rows_low = rows.astype(BF16)
    query = ((dot(rows_low, full[0]) + bq) * scale).astype(BF16)
    keys = dot(rows_low, full[1]).astype(BF16)
    values = (dot(rows_low, full[2]) + bv).astype(BF16)
    send = jnp.concatenate(
        [jnp.concatenate([by_head(query), by_head(keys)], axis=2), folded(by_head(values))], axis=1
    )
    got, o_t, log_total, mixed_got = forward_attention(send)
    mixed = by_token(unfolded(mixed_got))

    first_sum = rows + dot(mixed, full[3]) + bout
    first_out, first_normed, first_inverse = layer_norm(first_sum, gattn, battn)
    first_low = first_out.astype(BF16)
    pre_act = [dot(first_low, full[4 + j]) + bin_[j] for j in range(4)]
    activated = [gelu_value(value).astype(BF16) for value in pre_act]
    second_sum = first_out + bback
    for j in range(4):
        second_sum = second_sum + dot(activated[j], full[8 + j])
    output, second_normed, second_inverse = layer_norm(second_sum, gmlp, bmlp)

    upstream = cotangent.reshape(-1, width)
    grad_g_mlp = jnp.sum(upstream * second_normed, axis=0)
    grad_beta_mlp = jnp.sum(upstream, axis=0)
    grad_second = norm_back(upstream, second_normed, second_inverse, gmlp)
    grad_b_back = jnp.sum(grad_second, axis=0)
    grad_second_low = grad_second.astype(BF16)
    grad_w_back = [dot_tn(activated[j], grad_second_low).astype(BF16) for j in range(4)]
    grad_pre = [dot_nt(grad_second_low, full[8 + j]) * gelu_slope(pre_act[j]) for j in range(4)]
    grad_b_in = [jnp.sum(value, axis=0) for value in grad_pre]
    grad_pre_low = [value.astype(BF16) for value in grad_pre]
    grad_w_in = [dot_tn(first_low, grad_pre_low[j]).astype(BF16) for j in range(4)]
    grad_first_out = grad_second
    for j in range(4):
        grad_first_out = grad_first_out + dot_nt(grad_pre_low[j], full[4 + j])
    grad_g_attn = jnp.sum(grad_first_out * first_normed, axis=0)
    grad_beta_attn = jnp.sum(grad_first_out, axis=0)
    grad_first = norm_back(grad_first_out, first_normed, first_inverse, gattn)
    grad_b_out = jnp.sum(grad_first, axis=0)
    grad_first_low = grad_first.astype(BF16)
    grad_w_out = dot_tn(mixed, grad_first_low).astype(BF16)
    grad_mixed = dot_nt(grad_first_low, full[3]).astype(BF16)

    back = backward_attention(folded(by_head(grad_mixed)), got, o_t, log_total)
    grad_query = by_token(back[:, :192, :HEAD_DIM])
    grad_keys = by_token(back[:, :192, HEAD_DIM:])
    grad_values = by_token(unfolded(back[:, 192:]))
    grad_b_q = jnp.sum(widened(grad_query), axis=0)
    grad_b_v = jnp.sum(widened(grad_values), axis=0)
    grad_w_qkv = [dot_tn(rows_low, value).astype(BF16) for value in (grad_query, grad_keys, grad_values)]
    grad_input = grad_first
    for i, value in enumerate((grad_query, grad_keys, grad_values)):
        grad_input = grad_input + dot_nt(value, full[i])

    sm = jnp.stack(
        [grad_b_q, grad_b_v, grad_b_out, grad_g_attn, grad_beta_attn, grad_b_back, grad_g_mlp, grad_beta_mlp]
        + grad_b_in
        + [jnp.zeros((width,), F32)] * 4
    )
    sm = sm.reshape(16, 8, 128).transpose(1, 0, 2).reshape(2, 4, 16, 128)
    owned, own_small = reduce(grad_w_qkv + [grad_w_out] + grad_w_in + grad_w_back, sm)
    owned = widened(owned.reshape(UNITS, 128, width))
    o_qkv = owned[0:3].transpose(1, 0, 2).reshape(128, 3 * width)
    o_in = owned[4:8].reshape(4, 128, 8, 128).transpose(1, 2, 0, 3).reshape(128, 4 * width)
    o_back = owned[8:12].reshape(512, width)
    return (
        output.reshape(layer_input.shape),
        grad_input.reshape(layer_input.shape),
        o_qkv,
        own_small[0],
        own_small[1],
        owned[3],
        own_small[2],
        own_small[3],
        own_small[4],
        o_in,
        own_small[8:12].reshape(512),
        o_back,
        own_small[5],
        own_small[6],
        own_small[7],
    )


def solution(mesh):
    big, mat, vec = P("fsdp", "ctx", None), P("fsdp", None), P("fsdp")
    params = (mat, vec, vec, mat, vec, vec, vec, mat, vec, mat, vec, vec, vec)
    return jax.shard_map(
        shards, mesh=mesh, in_specs=(big, big) + params, out_specs=(big, big) + params, check_vma=False
    )
```

```python
import jax
import jax.numpy as jnp
from jax import lax
from jax.experimental import pallas as pl
from jax.experimental.pallas import tpu as pltpu
from jax.sharding import PartitionSpec as P

EPSILON = 1e-05
ROOT_HALF = 0.7071067811865476
INV_ROOT_TWO_PI = 0.3989422804014327
BF16 = jnp.bfloat16
F32 = jnp.float32
MESH = pl.DeviceIdType.MESH
MIB = 2**20


def place():
    fsdp, ctx = lax.axis_index("fsdp"), lax.axis_index("ctx")
    return (lax.rem(ctx // 2, 2) * 2 + fsdp // 4, lax.rem(fsdp, 4), ctx // 4, lax.rem(ctx, 2))


def device_at(x, y, z, core):
    x, y, z, core = (lax.rem(x + 4, 4), lax.rem(y + 4, 4), lax.rem(z + 4, 4), lax.rem(core, 2))
    return {"fsdp": lax.rem(x, 2) * 4 + y, "ctx": z * 4 + (x // 2) * 2 + core}


def greet(devices):
    barrier = pltpu.get_barrier_semaphore()
    for device in devices:
        pl.semaphore_signal(barrier, inc=1, device_id=device, device_id_type=MESH)
    pl.semaphore_wait(barrier, len(devices))


def remote(src, dst, send, recv, device):
    return pltpu.make_async_remote_copy(
        src_ref=src, dst_ref=dst, send_sem=send, recv_sem=recv, device_id=device, device_id_type=MESH
    )


BLOCK = 256
TOKENS = 192
LENGTH = 3072
DMA = pltpu.SemaphoreType.DMA


def peers():
    fsdp, me = lax.axis_index("fsdp"), lax.axis_index("ctx")
    return me, [(lax.rem(me + d, 16), {"fsdp": fsdp, "ctx": lax.rem(me + d, 16)}) for d in range(1, 16)]


def exchange(src, dst, me, others, sends, recvs, local):
    copies = []
    for i, (other, device) in enumerate(others):
        copy = remote(src.at[other], dst.at[me], sends.at[i], recvs.at[i], device)
        copy.start()
        copies.append(copy)
    mine = pltpu.make_async_copy(src.at[me], dst.at[me], local)
    mine.start()
    return copies + [mine]


def wait_all(copies):
    for copy in copies:
        copy.wait()


def dot(a, b):
    return jnp.dot(a, b, preferred_element_type=F32)


def dot_nt(a, b):
    return lax.dot_general(a, b, (((1,), (1,)), ((), ())), preferred_element_type=F32)


def dot_tn(a, b):
    return lax.dot_general(a, b, (((0,), (0,)), ((), ())), preferred_element_type=F32)


def beside(a, b):
    return jnp.concatenate([a, b], axis=1)


def block_span(i, size):
    return pl.ds(pl.multiple_of(i * size, size), size)


CHUNKS = ((0, 0, 32), (0, 32, 32), (1, 0, 64), (2, 0, 32), (2, 32, 32), (3, 0, 128), (3, 128, 128))
SHARD_ROWS = (128, 128, 128, 512)


def forward_kernel(x_in, small, w_qkv, w_out, w_in, w_back,
                   rows_low, got, o_t, log_total, mixed, smalls, g_qkv, g_out, g_in, g_back,
                   qkv_v, send, proj, k_all, q_t, v_t, o_send, o_got,
                   y_s, y_r, x_s, x_r, c_s, c_r, s_s, s_r, a_s, a_r, b_s, b_r, local):
    x, y, z, core = place()
    me, others = peers()
    low = lax.rem(x, 2)
    shard = low * 4 + y
    sibling = device_at(x, y, z, core + 1)
    ys = {d: device_at(x, y + d, z, core) for d in (1, 2, 3)}
    xs = [device_at(x + 1, y, z, core), device_at(x - 1, y, z, core)]
    greet([device for _, device in others] + list(ys.values()) + xs
          + [device_at(x - 1, y - d, z, core) for d in (1, 2, 3)])

    sources, fulls = (w_qkv, w_out, w_in, w_back), (qkv_v, g_out, g_in, g_back)
    pending, locals_ = [], []

    def begin(copy):
        copy.start()
        pending.append(copy)
        return copy

    smalls_in = []
    for i, (a, d) in enumerate([(a, d) for a in (0, 1) for d in range(4) if (a, d) != (0, 0)]):
        smalls_in.append(begin(remote(small, smalls.at[shard], s_s.at[i], s_r.at[i], device_at(x + a, y + d, z, core))))
    own = pltpu.make_async_copy(small, smalls.at[shard], local.at[0])
    own.start()
    own.wait()

    def keep_own(array):
        rows = SHARD_ROWS[array]
        copy = pltpu.make_async_copy(
            sources[array], fulls[array].at[block_span(shard, rows)], local.at[1 + array]
        )
        copy.start()
        locals_.append(copy)

    def rows_of(c, block, way=None):
        array, first, count = CHUNKS[c]
        rows = SHARD_ROWS[array]
        start = block * rows + core * (rows // 2) + first
        if way is not None:
            count = count // 2
            start = start + way * count
        return array, pl.ds(pl.multiple_of(start, 16), count)

    y_in, x_in_copies, c_in = {}, {}, {}

    def block_at(e, far):
        side = 1 - low if far else low
        return side * 4 + lax.rem(y - e + 4, 4)

    def y_start(c):
        array, src = rows_of(c, 0)
        dst = rows_of(c, shard)[1]
        for d in (1, 3, 2):
            y_in[c, d] = begin(
                remote(sources[array].at[src], fulls[array].at[dst], y_s.at[c, d - 1], y_r.at[c, d - 1], ys[d])
            )
        for way in (0, 1):
            src = rows_of(c, 0, way)[1]
            dst = rows_of(c, shard, way)[1]
            x_in_copies[c, 0, way] = begin(
                remote(sources[array].at[src], fulls[array].at[dst], x_s.at[c, 0, way], x_r.at[c, 0, way], xs[way])
            )

    def to_sibling(c, which, rows):
        array = CHUNKS[c][0]
        ref = fulls[array].at[rows]
        c_in[c, which] = begin(remote(ref, ref, c_s.at[c, which], c_r.at[c, which], sibling))

    def x_start(c):
        for d in (1, 3, 2):
            y_in[c, d].wait_recv()
            for way in (0, 1):
                array, rows = rows_of(c, block_at(d, False), way)
                ref = fulls[array].at[rows]
                x_in_copies[c, d, way] = begin(
                    remote(ref, ref, x_s.at[c, d, way], x_r.at[c, d, way], xs[way])
                )
            to_sibling(c, d - 1, rows_of(c, block_at(d, False))[1])

    def share(c):
        for e in (0, 1, 3, 2):
            for way in (0, 1):
                x_in_copies[c, e, way].wait_recv()
                to_sibling(c, 3 + 2 * e + way, rows_of(c, block_at(e, True), way)[1])

    def settle(c):
        for which in range(11):
            c_in[c, which].wait_recv()

    y_start(0)
    keep_own(0)
    rows_low[...] = x_in[...].astype(BF16)
    x_start(0)
    y_start(1)
    x_start(1)
    y_start(2)
    share(0)
    share(1)
    x_start(2)
    y_start(3)
    settle(0)
    settle(1)
    wait_all(locals_)
    locals_.clear()
    for copy in smalls_in:
        copy.wait_recv()
    keep = pltpu.make_async_copy(qkv_v, g_qkv, local.at[5])
    keep.start()
    for array in (1, 2, 3):
        keep_own(array)

    bias = smalls[...].astype(F32)
    bq = jnp.concatenate([bias[f, 0:1, :] for f in range(8)], axis=1)
    bv = jnp.concatenate([bias[f, 1:2, :] for f in range(8)], axis=1)
    low_rows = rows_low[...]
    proj[:, 0:1024] = (dot(low_rows, qkv_v[:, 0:1024]) + bq) * 0.125
    proj[:, 1024:2048] = dot(low_rows, qkv_v[:, 1024:2048])
    proj[:, 2048:3072] = dot(low_rows, qkv_v[:, 2048:3072]) + bv
    for h in range(16):
        q_cols = slice(64 * h, 64 * h + 64)
        k_cols = slice(1024 + 64 * h, 1024 + 64 * h + 64)
        v_cols = slice(2048 + 64 * h, 2048 + 64 * h + 64)
        send[h, 0:192, :] = beside(proj[:, q_cols], proj[:, k_cols]).astype(BF16)
        send[h, 192:288, :] = beside(proj[0:96, v_cols], proj[96:192, v_cols]).astype(BF16)
    copies = exchange(send, got, me, others, a_s, a_r, local.at[6])
    x_start(3)
    y_start(4)
    share(2)
    wait_all(copies)

    def unpack(j, _):
        k_all[pl.ds(pl.multiple_of(j * 192, 64), 192), :] = got[j, 0:192, 64:128]
        return 0

    lax.fori_loop(0, 16, unpack, 0)
    for j in range(16):
        span = slice(j * 192, (j + 1) * 192)
        both = got[j, 0:192, :].astype(F32).T
        q_t[:, span] = both[0:64].astype(BF16)
        pair = got[j, 192:288, :].astype(F32).T
        v_t[0:64, span] = beside(pair[0:64], pair[64:128]).astype(BF16)
    v_t[64:80, :] = jnp.ones((16, LENGTH), BF16)

    def block(i, _):
        span = block_span(i, BLOCK)
        scores = dot(k_all[...], q_t[:, span])
        highest = jnp.max(scores, axis=0, keepdims=True)
        weights = jnp.exp(scores - highest).astype(BF16)
        out = dot(v_t[...], weights)
        total = out[64:65]
        o_t[:, span] = (out[0:64] / total).astype(BF16)
        log_total[:, span] = highest + jnp.log(total)
        return 0

    x_start(4)
    y_start(5)
    lax.fori_loop(0, 3, block, 0)
    share(3)
    x_start(5)
    y_start(6)
    lax.fori_loop(3, 6, block, 0)
    share(4)
    lax.fori_loop(6, 9, block, 0)
    x_start(6)
    share(5)
    lax.fori_loop(9, 12, block, 0)
    for j in range(16):
        part = o_t[:, j * 192 : (j + 1) * 192].astype(F32)
        o_send[j] = jnp.concatenate([part[:, 0:96], part[:, 96:192]], axis=0).T.astype(BF16)
    copies = exchange(o_send, o_got, me, others, b_s, b_r, local.at[7])
    share(6)
    wait_all(copies)
    for p in range(8):
        a, b = o_got[2 * p].astype(F32), o_got[2 * p + 1].astype(F32)
        span = slice(128 * p, 128 * p + 128)
        mixed[0:96, span] = beside(a[:, 0:64], b[:, 0:64]).astype(BF16)
        mixed[96:192, span] = beside(a[:, 64:128], b[:, 64:128]).astype(BF16)
    for c in range(2, len(CHUNKS)):
        settle(c)
    for copy in pending:
        copy.wait_send()
    wait_all(locals_)
    keep.wait()


def forward(x_in, small, w_qkv, w_out, w_in, w_back):
    vmem, far = pl.BlockSpec(memory_space=pltpu.VMEM), pl.BlockSpec(memory_space=pl.ANY)
    n = len(CHUNKS)
    shape = jax.ShapeDtypeStruct
    return pl.pallas_call(
        forward_kernel,
        out_shape=(
            shape((TOKENS, 1024), BF16),
            shape((16, 288, 128), BF16),
            shape((64, LENGTH), BF16),
            shape((1, LENGTH), F32),
            shape((TOKENS, 1024), BF16),
            shape((8, 16, 128), BF16),
            shape((1024, 3072), BF16),
            shape((1024, 1024), BF16),
            shape((1024, 4096), BF16),
            shape((4096, 1024), BF16),
        ),
        in_specs=[vmem, vmem, far, far, far, far],
        out_specs=(vmem,) * 6 + (far,) * 4,
        scratch_shapes=[
            pltpu.VMEM((1024, 3072), BF16),
            pltpu.VMEM((16, 288, 128), BF16),
            pltpu.VMEM((TOKENS, 3072), F32),
            pltpu.VMEM((LENGTH, 64), BF16),
            pltpu.VMEM((64, LENGTH), BF16),
            pltpu.VMEM((80, LENGTH), BF16),
            pltpu.VMEM((16, 96, 128), BF16),
            pltpu.VMEM((16, 96, 128), BF16),
            DMA((n, 3)), DMA((n, 3)),
            DMA((n, 4, 2)), DMA((n, 4, 2)),
            DMA((n, 11)), DMA((n, 11)),
            DMA((7,)), DMA((7,)),
            DMA((15,)), DMA((15,)),
            DMA((15,)), DMA((15,)),
            DMA((8,)),
        ],
        compiler_params=pltpu.CompilerParams(collective_id=1, has_side_effects=True, vmem_limit_bytes=50 * MIB),
        name="forward_attention",
    )(x_in, small, w_qkv, w_out, w_in, w_back)


class Sum:
    def __init__(self, acc, first, per, bufs, final, out, sems, at, mine, pending):
        self.acc, self.first, self.per, self.bufs, self.final, self.out = acc, first, per, bufs, final, out
        self.sems, self.at, self.mine, self.pending = sems, at, mine, pending
        self.copies = {}

    def line(self, axis, d):
        to = list(self.at[:3])
        to[axis] = lax.rem(to[axis] + d, 4)
        return to[axis], device_at(*to, self.at[3])

    def piece(self, stage, p, c):
        at = self.at
        if stage == 0:
            whole = self.acc.at[pl.ds(self.first + p * self.per, self.per)]
            if p == 0:
                return whole.at[:, lax.rem(c, 2), :, :, c // 2]
            return whole.at[:, :, c] if p == 1 else whole.at[:, :, :, c]
        ref = self.piece(stage - 1, p, at[(p + stage - 1) % 3])
        if stage == 1:
            if p == 0:
                return ref.at[:, c]
            if p == 1:
                return ref.at[:, :, c]
            return ref.at[:, lax.rem(c, 2), :, c // 2]
        if p == 1:
            return ref.at[:, lax.rem(c, 2), c // 2]
        return ref.at[:, c]

    def start(self, stage, p):
        axis = (p + stage) % 3
        for d in (1, 3, 2):
            c, device = self.line(axis, d)
            sends, recvs = self.sems[2 * stage : 2 * stage + 2]
            copy = remote(
                self.piece(stage, p, c), self.bufs[stage][p].at[d - 1], sends.at[p, d - 1], recvs.at[p, d - 1], device
            )
            copy.start()
            self.copies[stage, p, d] = copy
            self.pending.append(copy)

    def finish(self, stage, p):
        for d in (1, 3, 2):
            self.copies[stage, p, d].wait_recv()
        own = self.piece(stage, p, self.at[(p + stage) % 3])
        buf = self.bufs[stage][p]
        target = self.final.at[pl.ds(p * self.per, self.per)] if stage == 2 else own
        for i in range(self.per):
            total = own[i].astype(F32) + buf[0, i].astype(F32) + buf[1, i].astype(F32) + buf[2, i].astype(F32)
            target[i] = total.astype(BF16)

    def spread(self, sibling, local):
        x, y, z, core = self.at
        high = x // 2
        sends, recvs, near_sends, near_recvs = self.sems[6:10]
        mine = self.out.at[pl.ds(self.first, 3 * self.per), z, high, :, self.mine]
        self.landed = []
        steps = [(a, d) for a in (0, 2) for d in range(4) if (a, d) != (0, 0)]
        for i, (a, d) in enumerate(steps):
            copy = remote(self.final, mine, sends.at[i], recvs.at[i], device_at(x + a, y, z + d, core))
            copy.start()
            self.landed.append(copy)
            self.pending.append(copy)
        self.steps = steps
        own = pltpu.make_async_copy(self.final, mine, local)
        own.start()
        copy = remote(self.final, mine, near_sends.at[0], near_recvs.at[0], sibling)
        copy.start()
        self.near = [copy]
        own.wait()

    def forward(self, sibling):
        x, y, z, core = self.at
        near_sends, near_recvs = self.sems[8:10]
        for i, (a, d) in enumerate(self.steps):
            self.landed[i].wait_recv()
            ref = self.out.at[
                pl.ds(self.first, 3 * self.per), lax.rem(z - d + 4, 4), lax.rem(x // 2 + a // 2, 2), :, self.mine
            ]
            copy = remote(ref, ref, near_sends.at[1 + i], near_recvs.at[1 + i], sibling)
            copy.start()
            self.near.append(copy)

    def end(self):
        wait_all(self.near)

    @staticmethod
    def scratch(per):
        def bufs(*shapes):
            return tuple(pltpu.VMEM((3, per) + shape + (16, 512), BF16) for shape in shapes)

        return (
            (bufs((4, 4), (2, 4, 2), (2, 4, 2)), bufs((4,), (2, 2), (4,)), bufs((), (), ())),
            pltpu.VMEM((3 * per, 16, 512), BF16),
            (DMA((3, 3)),) * 6 + (DMA((7,)),) * 2 + (DMA((8,)),) * 2,
        )


def backward_kernel(gm, got, o_t, log_total, rows_low, grad_first, sm_in,
                    first_low, mixed, act, gs, gfl, gp, g_qkv,
                    grad_input, out, sm_out,
                    sm, back, send, do_got, k_all, v_all, q_all, q_t, k_t, do_all, do_t, delta, dq_t, dk, dv,
                    lhs, rhs, lhs2, rhs2, gproj, acc, sum_a, sum_b, s0, s1, s2, s3,
                    a_s, a_r, b_s, b_r, n_s, n_r, t_s, t_r, local):
    x, y, z, core = at = place()
    me, others = peers()
    sibling = device_at(x, y, z, core + 1)
    greet([device for _, device in others] + [device_at(x, y + d, z, core) for d in (1, 2, 3)]
          + [device_at(x + d, y, z, core) for d in (1, 3)])
    pending = []
    mine = block_span(core, 512)

    for h in range(16):
        part = gm[:, 64 * h : 64 * h + 64].astype(F32)
        send[h, 0:96, :] = beside(part[0:96], part[96:192]).astype(BF16)
    a_copies = exchange(send.at[:, 0:96], do_got, me, others, a_s, a_r, local.at[0])

    near = []
    upper, lower = pl.ds(0, TOKENS), pl.ds(TOKENS, TOKENS)
    moves = [
        (rows_low, None, lhs2, 0, 1024),
        (mixed, None, lhs, 1024, 1024),
        (gfl, 512, rhs, 512, 512),
        (first_low, None, lhs, 0, 1024),
        (gp, 2048, rhs, 1024, 2048),
        (act, None, lhs, 2048, 4096),
        (gs, 512, rhs, 0, 512),
    ]
    for i, (src, cols, dst, first, count) in enumerate(moves):
        own = src if cols is None else src.at[:, block_span(core, cols)]
        other = src if cols is None else src.at[:, block_span(1 - core, cols)]
        span = pl.ds(first, count)
        copy = remote(other, dst.at[lower, span], n_s.at[i], n_r.at[i], sibling)
        copy.start()
        keep = pltpu.make_async_copy(own, dst.at[upper, span], local.at[1 + i])
        keep.start()
        near.append((copy, keep))
        pending.append(copy)

    for j in range(16):
        span = slice(j * 192, (j + 1) * 192)
        q_all[span, :] = got[j, 0:192, 0:64]
        k_all[span, :] = got[j, 0:192, 64:128]
        v_all[j * 192 : j * 192 + 96, :] = got[j, 192:288, 0:64]
        v_all[j * 192 + 96 : j * 192 + 192, :] = got[j, 192:288, 64:128]
        both = got[j, 0:192, :].astype(F32).T
        q_t[:, span] = both[0:64].astype(BF16)
        k_t[:, span] = both[64:128].astype(BF16)
    dk[...] = jnp.zeros_like(dk)
    dv[...] = jnp.zeros_like(dv)

    sum1 = Sum(acc, 0, 3, sum_a[0], sum_a[1], out, sum_a[2], at, mine, pending)
    sum2 = Sum(acc, 9, 1, sum_b[0], sum_b[1], out, sum_b[2], at, mine, pending)

    def arrive(*which):
        for i in which:
            near[i][0].wait_recv()
            near[i][1].wait()

    def product(unit, left, first, right, column):
        for side in range(2):
            value = dot_tn(left[:, first + 512 * side : first + 512 * side + 512], right[:, column : column + 512])
            acc[unit, side] = value.astype(BF16).reshape(4, 4, 2, 16, 512)

    arrive(1, 2)
    product(0, lhs, 1024, rhs, 512)
    arrive(3, 4)
    for j in range(2):
        product(1 + j, lhs, 0, rhs, 1024 + 512 * j)
    sum1.start(0, 0)
    for j in range(2, 4):
        product(1 + j, lhs, 0, rhs, 1024 + 512 * j)
    arrive(5, 6)
    for f in range(8):
        value = dot_tn(lhs[:, 2048 + 512 * f : 2560 + 512 * f], rhs[:, 0:512]).astype(BF16)
        acc[5:9, f // 4, f % 4] = value.reshape(4, 4, 2, 16, 512)
    sum1.start(0, 1)
    sum1.start(0, 2)

    wait_all(a_copies)
    for j in range(16):
        span = slice(j * 192, (j + 1) * 192)
        do_all[j * 192 : j * 192 + 96, :] = do_got[j, :, 0:64]
        do_all[j * 192 + 96 : j * 192 + 192, :] = do_got[j, :, 64:128]
        pair = do_got[j].astype(F32).T
        flat = beside(pair[0:64], pair[64:128])
        do_t[:, span] = flat.astype(BF16)
        delta[:, span] = jnp.sum(flat * o_t[:, span].astype(F32), axis=0, keepdims=True)

    def block(i, _):
        span = block_span(i, BLOCK)
        prob = jnp.exp(dot(k_all[...], q_t[:, span]) - log_total[:, span])
        grad_prob = dot(v_all[...], do_t[:, span])
        dv[...] += dot(prob.astype(BF16), do_all[span, :])
        grad_scores = (prob * (grad_prob - delta[:, span])).astype(BF16)
        dk[...] += dot(grad_scores, q_all[span, :])
        dq_t[:, span] = dot(k_t[...], grad_scores) * 0.125
        return 0

    lax.fori_loop(0, 9, block, 0)
    sum1.finish(0, 0)
    sum1.start(1, 0)
    lax.fori_loop(9, 12, block, 0)
    for j in range(16):
        span = slice(j * 192, (j + 1) * 192)
        send[j, 0:192, :] = beside(dq_t[:, span].T, dk[span, :]).astype(BF16)
        send[j, 192:288, :] = beside(
            dv[j * 192 : j * 192 + 96, :], dv[j * 192 + 96 : j * 192 + 192, :]
        ).astype(BF16)
    b_copies = exchange(send, back, me, others, b_s, b_r, local.at[0])
    for p in (1, 2):
        sum1.finish(0, p)
        sum1.start(1, p)
    for p in range(3):
        sum1.finish(1, p)
        sum1.start(2, p)
    wait_all(b_copies)
    for p in range(8):
        a, b = back[2 * p].astype(F32), back[2 * p + 1].astype(F32)
        span = slice(128 * p, 128 * p + 128)
        for i, part in enumerate((slice(0, 64), slice(64, 128))):
            cols = slice(1024 * i + 128 * p, 1024 * i + 128 * p + 128)
            gproj[:, cols] = beside(a[0:192, part], b[0:192, part]).astype(BF16)
            gproj[96 * i : 96 * i + 96, 2048 + 128 * p : 2176 + 128 * p] = beside(
                a[192:288, part], b[192:288, part]
            ).astype(BF16)
    near2 = []
    for i in range(3):
        span = pl.ds(512 * i, 512)

        def cols(half, i=i):
            return pl.ds(pl.multiple_of(1024 * i + 512 * half, 512), 512)

        copy = remote(gproj.at[:, cols(1 - core)], rhs2.at[lower, span], n_s.at[7 + i], n_r.at[7 + i], sibling)
        copy.start()
        keep = pltpu.make_async_copy(gproj.at[:, cols(core)], rhs2.at[upper, span], local.at[8 + i])
        keep.start()
        near2.append((copy, keep))
        pending.append(copy)
    sm[...] = sm_in[...]
    for i, first in ((0, 0), (1, 2048)):
        total = jnp.sum(gproj[:, first : first + 1024].astype(F32), axis=0, keepdims=True)
        for f in range(8):
            sm[f // 4, f % 4, i : i + 1, :] = total[:, 128 * f : 128 * f + 128]
    t_copy = remote(sm, s0, t_s.at[0], t_r.at[0], sibling)
    t_copy.start()
    pending.append(t_copy)
    arrive(0)
    for i in range(3):
        near2[i][0].wait_recv()
        near2[i][1].wait()
        product(9 + i, lhs2, 0, rhs2, 512 * i)
        sum2.start(0, i)
    t_copy.wait()
    s0[...] = s0[...] + sm[...]

    def small_start(stage, axis, piece, buf):
        copies = []
        for d in (1, 2, 3):
            c, device = sum1.line(axis, d)
            slot = 1 + 3 * stage + d - 1
            copies.append(remote(piece(c), buf.at[at[axis]], t_s.at[slot], t_r.at[slot], device))
            copies[-1].start()
        own = pltpu.make_async_copy(piece(at[axis]), buf.at[at[axis]], local.at[11 + stage])
        own.start()
        return copies + [own]

    small = small_start(0, 1, lambda c: s0.at[:, c], s1)
    for p in range(3):
        sum1.finish(2, p)
    sum1.spread(sibling, local.at[14])
    grads = gproj[...]
    grad_input[...] = grad_first[...] + dot_nt(grads, g_qkv[...])
    wait_all(small)
    s0[:, 0] = s1[0] + s1[1] + s1[2] + s1[3]
    small = small_start(1, 0, lambda c: s0.at[lax.rem(c, 2), 0], s2)
    for p in range(3):
        sum2.finish(0, p)
        sum2.start(1, p)
    wait_all(small)
    s0[0, 1] = s2[0] + s2[1] + s2[2] + s2[3]
    small = small_start(2, 2, lambda c: s0.at[0, 1], s3)
    for p in range(3):
        sum2.finish(1, p)
        sum2.start(2, p)
    wait_all(small)
    sm_out[...] = s3[0] + s3[1] + s3[2] + s3[3]
    for p in range(3):
        sum2.finish(2, p)
    sum2.spread(sibling, local.at[15])
    sum1.forward(sibling)
    sum2.forward(sibling)
    sum1.end()
    sum2.end()
    for copy in pending:
        if copy is not t_copy:
            copy.wait_send()


def backward(gm, got, o_t, log_total, rows_low, grad_first, sm, first_low, mixed, act, gs, gfl, gp, g_qkv):
    vmem, far = pl.BlockSpec(memory_space=pltpu.VMEM), pl.BlockSpec(memory_space=pl.ANY)
    shape = jax.ShapeDtypeStruct
    return pl.pallas_call(
        backward_kernel,
        out_shape=(
            shape((TOKENS, 1024), F32),
            shape((12, 4, 2, 16, 1024), BF16),
            shape((16, 128), F32),
        ),
        in_specs=[vmem] * 7 + [far] * 6 + [vmem],
        out_specs=(vmem, vmem, vmem),
        scratch_shapes=[
            pltpu.VMEM((2, 4, 16, 128), F32),
            pltpu.VMEM((16, 288, 128), BF16),
            pltpu.VMEM((16, 288, 128), BF16),
            pltpu.VMEM((16, 96, 128), BF16),
            pltpu.VMEM((LENGTH, 64), BF16),
            pltpu.VMEM((LENGTH, 64), BF16),
            pltpu.VMEM((LENGTH, 64), BF16),
            pltpu.VMEM((64, LENGTH), BF16),
            pltpu.VMEM((64, LENGTH), BF16),
            pltpu.VMEM((LENGTH, 64), BF16),
            pltpu.VMEM((64, LENGTH), BF16),
            pltpu.VMEM((1, LENGTH), F32),
            pltpu.VMEM((64, LENGTH), F32),
            pltpu.VMEM((LENGTH, 64), F32),
            pltpu.VMEM((LENGTH, 64), F32),
            pltpu.VMEM((2 * TOKENS, 6144), BF16),
            pltpu.VMEM((2 * TOKENS, 3072), BF16),
            pltpu.VMEM((2 * TOKENS, 1024), BF16),
            pltpu.VMEM((2 * TOKENS, 1536), BF16),
            pltpu.VMEM((TOKENS, 3072), BF16),
            pltpu.VMEM((12, 2, 4, 4, 2, 16, 512), BF16),
            Sum.scratch(3),
            Sum.scratch(1),
            pltpu.VMEM((2, 4, 16, 128), F32),
            pltpu.VMEM((4, 2, 16, 128), F32),
            pltpu.VMEM((4, 16, 128), F32),
            pltpu.VMEM((4, 16, 128), F32),
            DMA((15,)), DMA((15,)),
            DMA((15,)), DMA((15,)),
            DMA((10,)), DMA((10,)),
            DMA((10,)), DMA((10,)),
            DMA((16,)),
        ],
        compiler_params=pltpu.CompilerParams(collective_id=2, has_side_effects=True, vmem_limit_bytes=62 * MIB),
        name="backward_attention",
    )(gm, got, o_t, log_total, rows_low, grad_first, sm, first_low, mixed, act, gs, gfl, gp, g_qkv)


def unpack_kernel(out, o_qkv, o_out, o_in, o_back):
    def unit(u):
        return out[u].reshape(128, 1024).astype(F32)

    o_out[...] = unit(0)
    for j in range(4):
        value = unit(1 + j)
        o_in[:, 512 * j : 512 * j + 512] = value[:, 0:512]
        o_in[:, 2048 + 512 * j : 2560 + 512 * j] = value[:, 512:1024]
        o_back[128 * j : 128 * j + 128, :] = unit(5 + j)
    for i in range(3):
        o_qkv[:, 1024 * i : 1024 * i + 1024] = unit(9 + i)


def unpack(out):
    shape = jax.ShapeDtypeStruct
    vmem = pl.BlockSpec(memory_space=pltpu.VMEM)
    return pl.pallas_call(
        unpack_kernel,
        out_shape=(shape((128, 3072), F32), shape((128, 1024), F32), shape((128, 4096), F32), shape((512, 1024), F32)),
        in_specs=[vmem],
        out_specs=(vmem,) * 4,
        compiler_params=pltpu.CompilerParams(vmem_limit_bytes=30 * MIB),
        name="unpack_gradients",
    )(out)


def widened(values):
    return values.astype(F32)


def layer_norm(hidden, gain, offset):
    center = hidden - jnp.mean(hidden, axis=-1, keepdims=True)
    inverse = lax.rsqrt(jnp.mean(center * center, axis=-1, keepdims=True) + EPSILON)
    normed = center * inverse
    return (normed * gain + offset, normed, inverse)


def norm_back(upstream, normed, inverse, gain):
    scaled = upstream * gain
    return inverse * (
        scaled
        - jnp.mean(scaled, axis=-1, keepdims=True)
        - normed * jnp.mean(scaled * normed, axis=-1, keepdims=True)
    )


def gelu_value(inputs):
    return 0.5 * inputs * (1.0 + jax.scipy.special.erf(inputs * ROOT_HALF))


def gelu_slope(inputs):
    return (
        0.5 * (1.0 + jax.scipy.special.erf(inputs * ROOT_HALF))
        + inputs * jnp.exp(-0.5 * inputs * inputs) * INV_ROOT_TWO_PI
    )


def shards(layer_input, cotangent, w_qkv, b_q, b_v, w_out, b_out, g_attn, beta_attn, w_in, b_in, w_back, b_back,
           g_mlp, beta_mlp):
    width = layer_input.shape[-1]
    small = jnp.concatenate(
        [jnp.stack([b_q, b_v, b_out, g_attn, beta_attn, b_back, g_mlp, beta_mlp]), b_in.reshape(4, 128),
         jnp.zeros((4, 128), BF16)]
    )
    rows = layer_input.reshape(-1, width)
    rows_low, got, o_t, log_total, mixed, smalls, g_qkv, g_out, g_in, g_back = forward(
        rows, small, w_qkv, w_out, w_in, w_back
    )
    smalls = widened(smalls)
    _, _, bout, gattn, battn, bback, gmlp, bmlp = (smalls[:, i].reshape(width) for i in range(8))
    bin_ = smalls[:, 8:12].reshape(4 * width)

    first_sum = rows + dot(mixed, g_out) + bout
    first_out, first_normed, first_inverse = layer_norm(first_sum, gattn, battn)
    first_low = first_out.astype(BF16)
    pre_act = dot(first_low, g_in) + bin_
    activated = gelu_value(pre_act).astype(BF16)
    second_sum = first_out + dot(activated, g_back) + bback
    output, second_normed, second_inverse = layer_norm(second_sum, gmlp, bmlp)

    upstream = cotangent.reshape(-1, width)
    grad_g_mlp = jnp.sum(upstream * second_normed, axis=0)
    grad_beta_mlp = jnp.sum(upstream, axis=0)
    grad_second = norm_back(upstream, second_normed, second_inverse, gmlp)
    grad_b_back = jnp.sum(grad_second, axis=0)
    grad_second_low = grad_second.astype(BF16)
    grad_pre = dot_nt(grad_second_low, g_back) * gelu_slope(pre_act)
    grad_b_in = jnp.sum(grad_pre, axis=0)
    grad_pre_low = grad_pre.astype(BF16)
    grad_first_out = grad_second + dot_nt(grad_pre_low, g_in)
    grad_g_attn = jnp.sum(grad_first_out * first_normed, axis=0)
    grad_beta_attn = jnp.sum(grad_first_out, axis=0)
    grad_first = norm_back(grad_first_out, first_normed, first_inverse, gattn)
    grad_b_out = jnp.sum(grad_first, axis=0)
    grad_first_low = grad_first.astype(BF16)
    grad_mixed = dot_nt(grad_first_low, g_out).astype(BF16)

    blank = jnp.zeros((width,), F32)
    sm = jnp.stack(
        [blank, blank, grad_b_out, grad_g_attn, grad_beta_attn, grad_b_back, grad_g_mlp, grad_beta_mlp]
    )
    sm = jnp.concatenate(
        [sm.reshape(8, 8, 128).transpose(1, 0, 2), grad_b_in.reshape(8, 4, 128), jnp.zeros((8, 4, 128), F32)], axis=1
    ).reshape(2, 4, 16, 128)
    grad_input, owned, own_small = backward(
        grad_mixed, got, o_t, log_total, rows_low, grad_first, sm, first_low, mixed, activated, grad_second_low,
        grad_first_low, grad_pre_low, g_qkv
    )
    o_qkv, o_out, o_in, o_back = unpack(owned)
    return (
        output.reshape(layer_input.shape),
        grad_input.reshape(layer_input.shape),
        o_qkv,
        own_small[0],
        own_small[1],
        o_out,
        own_small[2],
        own_small[3],
        own_small[4],
        o_in,
        own_small[8:12].reshape(512),
        o_back,
        own_small[5],
        own_small[6],
        own_small[7],
    )


def solution(mesh):
    big, mat, vec = P("fsdp", "ctx", None), P("fsdp", None), P("fsdp")
    params = (mat, vec, vec, mat, vec, vec, vec, mat, vec, mat, vec, vec, vec)
    return jax.shard_map(
        shards, mesh=mesh, in_specs=(big, big) + params, out_specs=(big, big) + params, check_vma=False
    )
```

```python
import jax
import jax.numpy as jnp
from jax import lax
from jax.experimental import pallas as pl
from jax.experimental.pallas import tpu as pltpu
from jax.sharding import PartitionSpec as P

EPSILON = 1e-05
ROOT_HALF = 0.7071067811865476
INV_ROOT_TWO_PI = 0.3989422804014327
BF16 = jnp.bfloat16
F32 = jnp.float32
MESH = pl.DeviceIdType.MESH
MIB = 2**20


def place():
    fsdp, ctx = lax.axis_index("fsdp"), lax.axis_index("ctx")
    return (lax.rem(ctx // 2, 2) * 2 + fsdp // 4, lax.rem(fsdp, 4), ctx // 4, lax.rem(ctx, 2))


def device_at(x, y, z, core):
    x, y, z, core = (lax.rem(x + 4, 4), lax.rem(y + 4, 4), lax.rem(z + 4, 4), lax.rem(core, 2))
    return {"fsdp": lax.rem(x, 2) * 4 + y, "ctx": z * 4 + (x // 2) * 2 + core}


def greet(devices):
    barrier = pltpu.get_barrier_semaphore()
    for device in devices:
        pl.semaphore_signal(barrier, inc=1, device_id=device, device_id_type=MESH)
    pl.semaphore_wait(barrier, len(devices))


def remote(src, dst, send, recv, device):
    return pltpu.make_async_remote_copy(
        src_ref=src, dst_ref=dst, send_sem=send, recv_sem=recv, device_id=device, device_id_type=MESH
    )


BLOCK = 256
TOKENS = 192
LENGTH = 3072
DMA = pltpu.SemaphoreType.DMA


def peers():
    fsdp, me = lax.axis_index("fsdp"), lax.axis_index("ctx")
    return me, [(lax.rem(me + d, 16), {"fsdp": fsdp, "ctx": lax.rem(me + d, 16)}) for d in range(1, 16)]


def exchange(src, dst, me, others, sends, recvs, local):
    copies = []
    for i, (other, device) in enumerate(others):
        copy = remote(src.at[other], dst.at[me], sends.at[i], recvs.at[i], device)
        copy.start()
        copies.append(copy)
    mine = pltpu.make_async_copy(src.at[me], dst.at[me], local)
    mine.start()
    return copies + [mine]


def wait_all(copies):
    for copy in copies:
        copy.wait()


def dot(a, b):
    return jnp.dot(a, b, preferred_element_type=F32)


def dot_nt(a, b):
    return lax.dot_general(a, b, (((1,), (1,)), ((), ())), preferred_element_type=F32)


def dot_tn(a, b):
    return lax.dot_general(a, b, (((0,), (0,)), ((), ())), preferred_element_type=F32)


def beside(a, b):
    return jnp.concatenate([a, b], axis=1)


def flipped(value):
    return value.astype(F32).T.astype(BF16)


def block_span(i, size):
    return pl.ds(pl.multiple_of(i * size, size), size)


class Gather:
    def __init__(self, sources, fulls, chunks, sems, at, pending):
        self.sources, self.fulls, self.chunks, self.pending = sources, fulls, chunks, pending
        self.sems = sems
        x, y, z, core = at
        self.y, self.core, self.low = y, core, lax.rem(x, 2)
        self.up, self.down = device_at(x, y + 1, z, core), device_at(x, y - 1, z, core)
        self.xs = [device_at(x + 1, y, z, core), device_at(x - 1, y, z, core)]
        self.sibling = device_at(x, y, z, core + 1)
        self.copies = {}

    def shard_rows(self, array):
        return self.sources[array].shape[0]

    def rows(self, c, block, way=None):
        array, first, count = self.chunks[c]
        rows = self.shard_rows(array)
        start = block * rows + self.core * (rows // 2) + first
        if way is not None:
            count = count // 2
            start = start + way * count
        return pl.ds(pl.multiple_of(start, 16), count)

    def block(self, e, far=False):
        side = 1 - self.low if far else self.low
        return side * 4 + lax.rem(self.y - e + 4, 4)

    def own(self, array, local):
        rows = self.shard_rows(array)
        copy = pltpu.make_async_copy(
            self.sources[array], self.fulls[array].at[block_span(self.block(0), rows)], local
        )
        copy.start()
        return copy

    def go(self, key, kind, c, slot, src, rows, device):
        full = self.fulls[self.chunks[c][0]]
        sends, recvs = self.sems[2 * kind : 2 * kind + 2]
        copy = remote(full.at[rows] if src is None else src, full.at[rows], sends.at[c, slot], recvs.at[c, slot], device)
        copy.start()
        self.copies[key, c, slot] = copy
        self.pending.append(copy)

    def start(self, c):
        source = self.sources[self.chunks[c][0]]
        mine = self.block(0)
        self.go("y", 0, c, 0, source.at[self.rows(c, 0)], self.rows(c, mine), self.up)
        self.go("y", 0, c, 1, source.at[self.rows(c, 0)], self.rows(c, mine), self.down)
        for way in (0, 1):
            self.go("x", 1, c, way, source.at[self.rows(c, 0, way)], self.rows(c, mine, way), self.xs[way])

    def along_x(self, c, e, way):
        self.go("x", 1, c, 2 * e + way, None, self.rows(c, self.block(e), way), self.xs[way])

    def to_core(self, c, slot, rows):
        self.go("c", 2, c, slot, None, rows, self.sibling)

    def relay(self, c):
        for slot, e, device in ((0, 1, self.up), (1, 3, self.down)):
            self.copies["y", c, slot].wait_recv()
            self.go("y", 0, c, 2 + slot, None, self.rows(c, self.block(e), slot), device)
            for way in (0, 1):
                self.along_x(c, e, way)
            self.to_core(c, slot, self.rows(c, self.block(e)))

    def last(self, c):
        for way in (0, 1):
            self.copies["y", c, 2 + way].wait_recv()
            self.along_x(c, 2, way)
        self.to_core(c, 2, self.rows(c, self.block(2)))

    def share(self, c):
        for e in (0, 1, 3, 2):
            for way in (0, 1):
                self.copies["x", c, 2 * e + way].wait_recv()
                self.to_core(c, 3 + 2 * e + way, self.rows(c, self.block(e, True), way))

    def settle(self, c):
        for slot in range(11):
            self.copies["c", c, slot].wait_recv()

    @staticmethod
    def scratch(n):
        return (DMA((n, 4)),) * 2 + (DMA((n, 8)),) * 2 + (DMA((n, 11)),) * 2


CHUNKS = ((0, 0, 64), (1, 0, 32), (1, 32, 32), (2, 0, 128), (2, 128, 128))


def forward_kernel(x_in, small, w_qkv, w_out, w_in, w_back,
                   q_all, k_all, v_all, q_t, k_t, o_t, log_total, mixed, smalls, x_out, g_out, g_in, g_back, g_qkv,
                   x_all, tiles, w_got, w_head, v_t, o_send, o_got,
                   g_sems, q_s, q_r, s_s, s_r, h_s, h_r, n_s, n_r, b_s, b_r, local):
    x, y, z, core = place()
    me, others = peers()
    low, high = lax.rem(x, 2), x // 2
    shard = low * 4 + y
    sibling = device_at(x, y, z, core + 1)
    pending, locals_ = [], []

    def begin(copy):
        copy.start()
        pending.append(copy)
        return copy

    def keep(src, dst, slot):
        copy = pltpu.make_async_copy(src, dst, local.at[slot])
        copy.start()
        return copy

    tile_copies = [
        keep(w_qkv.at[:, block_span(8 * i + me // 2, 128)], tiles.at[i], i) for i in range(3)
    ]
    x_all[me] = x_in[...].astype(BF16)
    across = [
        (lax.rem(low + a, 2), d) for a in (0, 1) for d in range(4) if (a, d) != (0, 0)
    ]
    across = [device_at(high * 2 + a, y + d, z, core) for a, d in across]
    greet([device for _, device in others] + across + [device_at(high * 2 - 1 + 3 * low, y, z, core)])

    def index(dz, dh, dk=0):
        return lax.rem(z + dz + 4, 4) * 4 + lax.rem(high + dh, 2) * 2 + lax.rem(core + dk, 2)

    up, down = device_at(x, y, z + 1, core), device_at(x, y, z - 1, core)
    first_half, second_half = pl.ds(0, 96), pl.ds(96, 96)

    def pass_on(slot, block, device, rows=None):
        ref = x_all.at[block] if rows is None else x_all.at[block, rows]
        return begin(remote(ref, ref, h_s.at[slot], h_r.at[slot], device))

    def share_rows(slot, block):
        ref = x_all.at[block]
        return begin(remote(ref, ref, n_s.at[slot], n_r.at[slot], sibling))

    moves = {1: pass_on(1, me, up), 2: pass_on(2, me, down), 0: pass_on(0, me, device_at(x + 2, y, z, core))}
    nears = [share_rows(7, me)]

    odd = lax.rem(me, 2) == 1
    for copy in tile_copies:
        copy.wait()

    def column_half(value):
        return jnp.where(odd, value[:, 64:128], value[:, 0:64])

    parts = [column_half(tiles[i].astype(F32)) for i in range(3)]
    w_got[shard, 0:128, :] = beside(parts[0], parts[1]).astype(BF16)
    w_got[shard, 128:192, :] = beside(parts[2][0:64], parts[2][64:128]).astype(BF16)
    w_got[shard, 192:208, :] = small[...]
    head_copies = []
    for i, device in enumerate(across):
        ref = w_got.at[shard]
        head_copies.append(begin(remote(ref, ref, s_s.at[i], s_r.at[i], device)))

    whole = Gather((w_out, w_in, w_back), (g_out, g_in, g_back), CHUNKS, g_sems, (x, y, z, core), pending)
    for c in range(3):
        whole.start(c)
    for array in range(3):
        locals_.append(whole.own(array, local.at[3 + array]))

    quarter = w_qkv.at[pl.ds(pl.multiple_of(core * 64 + z * 16, 16), 16)]
    xs = [device_at(x + 1, y, z, core), device_at(x - 1, y, z, core)]
    ys = [device_at(x, y + 1, z, core), device_at(x, y - 1, z, core), device_at(x, y + 2, z, core)]
    q_moves = {}

    def q_go(slot, src, dst, device):
        q_moves[slot] = begin(remote(src, dst, q_s.at[slot], q_r.at[slot], device))

    def q_block(e):
        return g_qkv.at[low * 4 + lax.rem(y - e + 4, 4)]

    q_own = keep(quarter, q_block(0), 9)
    for slot in range(3):
        q_go(slot, quarter, q_block(0), ys[slot])
    q_go(3, quarter, q_block(0), xs[0])

    def q_along_x():
        for slot, e in ((0, 1), (1, 3), (2, 2)):
            q_moves[slot].wait_recv()
            q_go(3 + e, q_block(e), q_block(e), xs[e % 2])

    for copy in head_copies:
        copy.wait_recv()
    for f in range(8):
        span = slice(128 * f, 128 * f + 128)
        w_head[span, 0:128] = w_got[f, 0:128, :]
        w_head[128 * f : 128 * f + 64, 128:192] = w_got[f, 128:192, 0:64]
        w_head[128 * f + 64 : 128 * f + 128, 128:192] = w_got[f, 128:192, 64:128]
        smalls[f] = w_got[f, 192:208, :]
    bias = w_got[me // 2, 192:208, :].astype(F32)
    bias = jnp.concatenate(
        [column_half(bias[0:1]), jnp.zeros((1, 64), F32), column_half(bias[1:2])], axis=1
    )
    scale = jnp.where(lax.broadcasted_iota(jnp.int32, (1, 192), 1) < 64, 0.125, 1.0)

    def project(block):
        value = ((dot(x_all[block], w_head[:, 0:192]) + bias) * scale).astype(BF16)
        rows = pl.ds(pl.multiple_of(block * TOKENS, 64), TOKENS)
        q_all[rows, :] = value[:, 0:64]
        k_all[rows, :] = value[:, 64:128]
        v_all[rows, :] = value[:, 128:192]

    project(me)
    moves[1].wait_recv()
    moves[4] = pass_on(4, index(-1, 0), up, first_half)
    moves[2].wait_recv()
    moves[5] = pass_on(5, index(1, 0), down, second_half)
    moves[0].wait_recv()
    moves[6] = pass_on(6, index(0, 1), up)
    moves[7] = pass_on(7, index(0, 1), down)
    nears += [share_rows(0, index(-1, 0)), share_rows(1, index(1, 0)), share_rows(2, index(0, 1))]
    whole.relay(0)
    whole.start(3)
    project(index(-1, 0))
    project(index(1, 0))
    project(index(0, 1))
    nears[0].wait_recv()
    project(index(0, 0, 1))
    q_along_x()
    whole.relay(1)
    whole.start(4)
    whole.last(0)
    moves[4].wait_recv()
    moves[5].wait_recv()
    nears.append(share_rows(3, index(2, 0)))
    project(index(2, 0))
    moves[6].wait_recv()
    moves[8] = pass_on(8, index(-1, 1), up, first_half)
    moves[7].wait_recv()
    moves[9] = pass_on(9, index(1, 1), down, second_half)
    nears += [share_rows(4, index(-1, 1)), share_rows(5, index(1, 1))]
    whole.relay(2)
    whole.last(1)
    whole.share(0)
    for i, spot in enumerate(((-1, 0), (1, 0), (0, 1), (2, 0))):
        nears[1 + i].wait_recv()
        project(index(*spot, 1))
    project(index(-1, 1))
    project(index(1, 1))
    for i, spot in enumerate(((-1, 1), (1, 1))):
        nears[5 + i].wait_recv()
        project(index(*spot, 1))
    moves[8].wait_recv()
    moves[9].wait_recv()
    nears.append(share_rows(6, index(2, 1)))
    project(index(2, 1))
    nears[7].wait_recv()
    project(index(2, 1, 1))
    kept = keep(x_all, x_out, 7)
    whole.relay(3)
    whole.last(2)
    whole.share(1)

    for i in range(LENGTH // BLOCK):
        span = slice(BLOCK * i, BLOCK * i + BLOCK)
        q_t[:, span] = flipped(q_all[span, :])
        k_t[:, span] = flipped(k_all[span, :])
        v_t[0:64, span] = flipped(v_all[span, :])
    v_t[64:80, :] = jnp.ones((16, LENGTH), BF16)

    def block(i, _):
        span = block_span(i, BLOCK)
        scores = dot(k_all[...], q_t[:, span])
        highest = jnp.max(scores, axis=0, keepdims=True)
        weights = jnp.exp(scores - highest).astype(BF16)
        out = dot(v_t[...], weights)
        total = out[64:65]
        o_t[:, span] = (out[0:64] / total).astype(BF16)
        log_total[:, span] = highest + jnp.log(total)
        return 0

    whole.relay(4)
    whole.last(3)
    lax.fori_loop(0, 4, block, 0)
    whole.last(4)
    whole.share(2)
    lax.fori_loop(4, 8, block, 0)
    whole.share(3)
    lax.fori_loop(8, 12, block, 0)
    for j in range(16):
        part = o_t[:, j * 192 : (j + 1) * 192].astype(F32)
        o_send[j] = jnp.concatenate([part[:, 0:96], part[:, 96:192]], axis=0).T.astype(BF16)
    copies = exchange(o_send, o_got, me, others, b_s, b_r, local.at[8])
    whole.share(4)
    wait_all(copies)
    for p in range(8):
        a, b = o_got[2 * p].astype(F32), o_got[2 * p + 1].astype(F32)
        span = slice(128 * p, 128 * p + 128)
        mixed[0:96, span] = beside(a[:, 0:64], b[:, 0:64]).astype(BF16)
        mixed[96:192, span] = beside(a[:, 64:128], b[:, 64:128]).astype(BF16)
    for c in range(len(CHUNKS)):
        whole.settle(c)
    q_own.wait()
    for slot in range(3, 7):
        q_moves[slot].wait_recv()
    for copy in pending:
        copy.wait_send()
    wait_all(locals_)
    kept.wait()


def forward(x_in, small, w_qkv, w_out, w_in, w_back):
    vmem, far = pl.BlockSpec(memory_space=pltpu.VMEM), pl.BlockSpec(memory_space=pl.ANY)
    n = len(CHUNKS)
    shape = jax.ShapeDtypeStruct
    return pl.pallas_call(
        forward_kernel,
        out_shape=(
            shape((LENGTH, 64), BF16),
            shape((LENGTH, 64), BF16),
            shape((LENGTH, 64), BF16),
            shape((64, LENGTH), BF16),
            shape((64, LENGTH), BF16),
            shape((64, LENGTH), BF16),
            shape((1, LENGTH), F32),
            shape((TOKENS, 1024), BF16),
            shape((8, 16, 128), BF16),
            shape((16, TOKENS, 1024), BF16),
            shape((1024, 1024), BF16),
            shape((1024, 4096), BF16),
            shape((4096, 1024), BF16),
            shape((8, 16, 3072), BF16),
        ),
        in_specs=[vmem] * 6,
        out_specs=(vmem,) * 9 + (far,) * 5,
        scratch_shapes=[
            pltpu.VMEM((16, TOKENS, 1024), BF16),
            pltpu.VMEM((3, 128, 128), BF16),
            pltpu.VMEM((8, 208, 128), BF16),
            pltpu.VMEM((1024, 256), BF16),
            pltpu.VMEM((80, LENGTH), BF16),
            pltpu.VMEM((16, 96, 128), BF16),
            pltpu.VMEM((16, 96, 128), BF16),
            Gather.scratch(n),
            DMA((7,)), DMA((7,)),
            DMA((7,)), DMA((7,)),
            DMA((10,)), DMA((10,)),
            DMA((8,)), DMA((8,)),
            DMA((15,)), DMA((15,)),
            DMA((10,)),
        ],
        compiler_params=pltpu.CompilerParams(collective_id=1, has_side_effects=True, vmem_limit_bytes=60 * MIB),
        name="forward_attention",
    )(x_in, small, w_qkv, w_out, w_in, w_back)


TURNS = (2, 1, 0, 1, 0, 1, 2, 1, 0)
PIECES = (((4, 4), (2, 4, 2), (2, 4, 2)), ((4,), (2, 2), (4,)), ((), (), ()))


class Sum:
    def __init__(self, acc, bufs, final, out, sems, at, pending):
        self.acc, self.bufs, self.final, self.out = acc, bufs, final, out
        self.sems, self.at, self.pending = sems, at, pending
        self.mine = block_span(at[3], 512)
        self.sibling = device_at(*at[:3], at[3] + 1)
        self.copies = {}

    def line(self, axis, d):
        to = list(self.at[:3])
        to[axis] = lax.rem(to[axis] + d, 4)
        return to[axis], device_at(*to, self.at[3])

    def piece(self, stage, u, c):
        turn = TURNS[u]
        if stage == 0:
            ref = self.acc.at[u]
            if turn == 0:
                return ref.at[lax.rem(c, 2), :, :, c // 2]
            return ref.at[:, c] if turn == 1 else ref.at[:, :, c]
        ref = self.piece(stage - 1, u, self.at[(turn + stage - 1) % 3])
        if (turn + stage) % 3 == 0:
            return ref.at[lax.rem(c, 2), c // 2] if turn == 1 else ref.at[lax.rem(c, 2), :, c // 2]
        return ref.at[:, c] if turn == 1 else ref.at[c]

    def buffer(self, stage, u):
        turn = TURNS[u]
        return self.bufs[stage][turn].at[TURNS[:u].count(turn)]

    def start(self, stage, *units):
        sends, recvs = self.sems[2 * stage : 2 * stage + 2]
        for u in units:
            axis = (TURNS[u] + stage) % 3
            for d in (1, 3, 2):
                c, device = self.line(axis, d)
                copy = remote(
                    self.piece(stage, u, c),
                    self.buffer(stage, u).at[d - 1],
                    sends.at[u, d - 1],
                    recvs.at[u, d - 1],
                    device,
                )
                copy.start()
                self.copies[stage, u, d] = copy
                self.pending.append(copy)

    def finish(self, stage, *units):
        for u in units:
            for d in (1, 3, 2):
                self.copies[stage, u, d].wait_recv()
            own = self.piece(stage, u, self.at[(TURNS[u] + stage) % 3])
            buf = self.buffer(stage, u)
            total = own[...].astype(F32) + buf[0].astype(F32) + buf[1].astype(F32) + buf[2].astype(F32)
            if stage == 2:
                self.final[u] = total.astype(BF16)
            else:
                own[...] = total.astype(BF16)
                self.start(stage + 1, u)

    def go(self, key, slot, src, dst, device):
        sends, recvs = self.sems[6:8] if key == "far" else self.sems[8:10]
        copy = remote(src, dst, sends.at[slot], recvs.at[slot], device)
        copy.start()
        self.copies[key, slot] = copy
        self.pending.append(copy)

    def spot(self, dz, dh):
        x, y, z, core = self.at
        return self.out.at[:, lax.rem(z + dz, 4), lax.rem(x // 2 + dh, 2), :, self.mine]

    def spread(self, local):
        mine = self.spot(0, 0)
        self.go("far", 0, self.final, mine, self.line(0, 2)[1])
        for d in (1, 3, 2):
            self.go("far", d, self.final, mine, self.line(2, d)[1])
        self.go("near", 0, self.final, mine, self.sibling)
        own = pltpu.make_async_copy(self.final, mine, local)
        own.start()
        own.wait()

    def relay(self):
        self.copies["far", 0].wait_recv()
        ref = self.spot(0, 1)
        for d in (1, 3, 2):
            self.go("far", 3 + d, ref, ref, self.line(2, d)[1])
        self.go("near", 1, ref, ref, self.sibling)

    def share(self):
        for dh in (0, 1):
            for d in (1, 3, 2):
                self.copies["far", 3 * dh + d].wait_recv()
                ref = self.spot(4 - d, dh)
                self.go("near", 1 + 3 * dh + d, ref, ref, self.sibling)

    def end(self):
        for slot in range(8):
            self.copies["near", slot].wait_recv()

    @staticmethod
    def scratch():
        bufs = tuple(
            tuple(
                pltpu.VMEM((TURNS.count(turn), 3) + shapes[turn] + (16, 512), BF16) for turn in range(3)
            )
            for shapes in PIECES
        )
        n = len(TURNS)
        return (
            bufs,
            pltpu.VMEM((n, 16, 512), BF16),
            (DMA((n, 3)),) * 6 + (DMA((7,)),) * 2 + (DMA((8,)),) * 2,
        )


def backward_kernel(gm, q_all, k_all, v_all, q_t, k_t, o_t, log_total, grad_first, sm_in,
                    x_far, first_low, mixed, act, gs, gfl, gp, *rest):
    quarters, rest = rest[:4], rest[4:]
    backward_body(gm, q_all, k_all, v_all, q_t, k_t, o_t, log_total, grad_first, sm_in, x_far, first_low, mixed, act, gs,
                  gfl, gp, quarters, *rest)


def backward_body(gm, q_all, k_all, v_all, q_t, k_t, o_t, log_total, grad_first, sm_in,
                    x_far, first_low, mixed, act, gs, gfl, gp, quarters,
                    grad_input, out, qkv_out, sm_out,
                    x_all, g_qkv, sm, back, send, do_got, do_all, do_t, delta, dq_t, dk, dv,
                    lhs, rhs, gproj, head_t, head_send, head_got, head_sum, acc, sum_a, s0, s1, s2, s3,
                    a_s, a_r, b_s, b_r, n_s, n_r, t_s, t_r, h_s, h_r, p_s, p_r, q_s, q_r, local):
    x, y, z, core = at = place()
    me, others = peers()
    low = lax.rem(x, 2)
    shard = low * 4 + y
    sibling = device_at(x, y, z, core + 1)
    pending = []

    def keep(src, dst, slot):
        copy = pltpu.make_async_copy(src, dst, local.at[slot])
        copy.start()
        return copy

    for h in range(16):
        part = gm[:, 64 * h : 64 * h + 64].astype(F32)
        send[h, 0:96, :] = beside(part[0:96], part[96:192]).astype(BF16)
    across = [(a, d) for a in (0, 1) for d in range(4) if (a, d) != (0, 0)]
    across = [
        (lax.rem(low + a, 2) * 4 + lax.rem(y + d, 4), device_at(x // 2 * 2 + lax.rem(low + a, 2), y + d, z, core))
        for a, d in across
    ]
    greet([device for _, device in others] + [device for _, device in across]
          + [device_at(x // 2 * 2 - 1 + 3 * low, y, z, core)])
    a_copies = exchange(send.at[:, 0:96], do_got, me, others, a_s, a_r, local.at[0])

    near = []
    upper, lower = pl.ds(0, TOKENS), pl.ds(TOKENS, TOKENS)
    moves = [
        (mixed, None, lhs, 1024, 1024),
        (gfl, 512, rhs, 512, 512),
        (first_low, None, lhs, 0, 1024),
        (gp, 2048, rhs, 1024, 2048),
        (act, None, lhs, 2048, 4096),
        (gs, 512, rhs, 0, 512),
    ]
    for i, (src, cols, dst, first, count) in enumerate(moves):
        own = src if cols is None else src.at[:, block_span(core, cols)]
        other = src if cols is None else src.at[:, block_span(1 - core, cols)]
        span = pl.ds(first, count)
        copy = remote(other, dst.at[lower, span], n_s.at[i], n_r.at[i], sibling)
        copy.start()
        near.append((copy, keep(own, dst.at[upper, span], 1 + i)))
        pending.append(copy)
    x_copy = keep(x_far, x_all, 7)
    g_copies = []
    for i, quarter in enumerate(quarters):
        ref = g_qkv.at[:, core, lax.rem(z - i + 4, 4)]
        copy = remote(quarter, ref, q_s.at[i], q_r.at[i], sibling)
        copy.start()
        g_copies += [copy, keep(quarter, ref, 15 + i)]
    dk[...] = jnp.zeros_like(dk)
    dv[...] = jnp.zeros_like(dv)
    sums = Sum(acc, sum_a[0], sum_a[1], out, sum_a[2], at, pending)

    def arrive(*which):
        for i in which:
            near[i][0].wait_recv()
            near[i][1].wait()

    def product(unit, first, column):
        for side in range(2):
            value = dot_tn(lhs[:, first + 512 * side : first + 512 * side + 512], rhs[:, column : column + 512])
            acc[unit, side] = value.astype(BF16).reshape(4, 4, 2, 16, 512)
        sums.start(0, unit)

    arrive(0, 1)
    product(0, 1024, 512)
    arrive(2, 3)
    for j in range(4):
        product(1 + j, 0, 1024 + 512 * j)
    arrive(4, 5)
    for j in range(4):
        for side in range(2):
            left = jnp.concatenate(
                [lhs[:, 2048 + 512 * f + 128 * j : 2176 + 512 * f + 128 * j] for f in range(4 * side, 4 * side + 4)],
                axis=1,
            )
            acc[5 + j, side] = dot_tn(left, rhs[:, 0:512]).astype(BF16).reshape(4, 4, 2, 16, 512)
        sums.start(0, 5 + j)

    wait_all(a_copies)
    for j in range(16):
        span = slice(j * 192, (j + 1) * 192)
        do_all[j * 192 : j * 192 + 96, :] = do_got[j, :, 0:64]
        do_all[j * 192 + 96 : j * 192 + 192, :] = do_got[j, :, 64:128]
        pair = do_got[j].astype(F32).T
        flat = beside(pair[0:64], pair[64:128])
        do_t[:, span] = flat.astype(BF16)
        delta[:, span] = jnp.sum(flat * o_t[:, span].astype(F32), axis=0, keepdims=True)

    def block(i, _):
        span = block_span(i, BLOCK)
        prob = jnp.exp(dot(k_all[...], q_t[:, span]) - log_total[:, span])
        grad_prob = dot(v_all[...], do_t[:, span])
        dv[...] += dot(prob.astype(BF16), do_all[span, :])
        grad_scores = (prob * (grad_prob - delta[:, span])).astype(BF16)
        dk[...] += dot(grad_scores, q_all[span, :])
        dq_t[:, span] = dot(k_t[...], grad_scores) * 0.125
        return 0

    lax.fori_loop(0, 5, block, 0)
    sums.finish(0, 0, 1)
    lax.fori_loop(5, 9, block, 0)
    sums.finish(0, 2, 3)
    lax.fori_loop(9, 12, block, 0)
    sum_q = jnp.zeros((1, 64), F32)
    for j in range(16):
        span = slice(j * 192, (j + 1) * 192)
        dq = dq_t[:, span].T
        sum_q = sum_q + jnp.sum(dq, axis=0, keepdims=True)
        send[j, 0:192, :] = beside(dq, dk[span, :]).astype(BF16)
        send[j, 192:288, :] = beside(
            dv[j * 192 : j * 192 + 96, :], dv[j * 192 + 96 : j * 192 + 192, :]
        ).astype(BF16)
    b_copies = exchange(send, back, me, others, b_s, b_r, local.at[0])
    sums.finish(0, 4, 5)

    for i in range(LENGTH // BLOCK):
        span = slice(BLOCK * i, BLOCK * i + BLOCK)
        head_t[0:64, span] = dq_t[:, span].astype(BF16)
        head_t[64:128, span] = dk[span, :].T.astype(BF16)
        head_t[128:192, span] = dv[span, :].T.astype(BF16)
    x_copy.wait()
    head = dot(head_t[...], x_all[...].reshape(LENGTH, 1024))
    for f in range(8):
        head_send[f] = head[:, 128 * f : 128 * f + 128].astype(BF16)
    head_copies = []
    for i, (to, device) in enumerate(across):
        copy = remote(head_send.at[to], head_got.at[shard], h_s.at[i], h_r.at[i], device)
        copy.start()
        head_copies.append(copy)
    head_copies.append(keep(head_send.at[shard], head_got.at[shard], 9))

    sm[...] = sm_in[...]
    odd = lax.rem(me, 2) == 1
    blank = jnp.zeros((1, 64), F32)
    owner = me // 2
    for i, value in enumerate((sum_q, jnp.sum(dv[...], axis=0, keepdims=True))):
        sm[owner // 4, lax.rem(owner, 4), i : i + 1, :] = jnp.where(odd, beside(blank, value), beside(value, blank))
    t_copy = remote(sm, s0, t_s.at[0], t_r.at[0], sibling)
    t_copy.start()

    def small_start(stage, axis, piece, buf):
        copies = []
        for d in (1, 2, 3):
            c, device = sums.line(axis, d)
            slot = 1 + 3 * stage + d - 1
            copies.append(remote(piece(c), buf.at[at[axis]], t_s.at[slot], t_r.at[slot], device))
            copies[-1].start()
        return copies + [keep(piece(at[axis]), buf.at[at[axis]], 10 + stage)]

    sums.finish(0, 6, 7, 8)
    sums.finish(1, 0, 1, 2, 3)
    t_copy.wait()
    s0[...] = s0[...] + sm[...]
    small = small_start(0, 1, lambda c: s0.at[:, c], s1)
    wait_all(head_copies)
    total = head_got[0].astype(F32)
    for f in range(1, 8):
        total = total + head_got[f].astype(F32)
    head_sum[...] = total.astype(BF16)
    p_copies = [keep(head_sum, qkv_out.at[me], 13)]
    for i, (_, device) in enumerate(others):
        copy = remote(head_sum, qkv_out.at[me], p_s.at[i], p_r.at[i], device)
        copy.start()
        p_copies.append(copy)
    sums.finish(1, 4, 5, 6, 7, 8)
    wait_all(small)
    s0[:, 0] = s1[0] + s1[1] + s1[2] + s1[3]
    small = small_start(1, 0, lambda c: s0.at[lax.rem(c, 2), 0], s2)
    sums.finish(2, *range(9))
    sums.spread(local.at[14])
    wait_all(b_copies)
    for p in range(8):
        a, b = back[2 * p].astype(F32), back[2 * p + 1].astype(F32)
        for i, part in enumerate((slice(0, 64), slice(64, 128))):
            cols = slice(1024 * i + 128 * p, 1024 * i + 128 * p + 128)
            gproj[:, cols] = beside(a[0:192, part], b[0:192, part]).astype(BF16)
            gproj[96 * i : 96 * i + 96, 2048 + 128 * p : 2176 + 128 * p] = beside(
                a[192:288, part], b[192:288, part]
            ).astype(BF16)
    sums.relay()
    wait_all(small)
    s0[0, 1] = s2[0] + s2[1] + s2[2] + s2[3]
    small = small_start(2, 2, lambda c: s0.at[0, 1], s3)
    wait_all(g_copies)
    grad_input[...] = grad_first[...] + dot_nt(gproj[...], g_qkv[...].reshape(1024, 3072))
    wait_all(small)
    sm_out[...] = s3[0] + s3[1] + s3[2] + s3[3]
    sums.share()
    wait_all(p_copies)
    sums.end()
    for copy in pending:
        copy.wait_send()


def backward(gm, q_all, k_all, v_all, q_t, k_t, o_t, log_total, grad_first, sm,
             x_far, first_low, mixed, act, gs, gfl, gp, *quarters):
    vmem, far = pl.BlockSpec(memory_space=pltpu.VMEM), pl.BlockSpec(memory_space=pl.ANY)
    shape = jax.ShapeDtypeStruct
    return pl.pallas_call(
        backward_kernel,
        out_shape=(
            shape((TOKENS, 1024), F32),
            shape((9, 4, 2, 16, 1024), BF16),
            shape((16, 192, 128), BF16),
            shape((16, 128), F32),
        ),
        in_specs=[vmem] * 10 + [far] * 11,
        out_specs=(vmem,) * 4,
        scratch_shapes=[
            pltpu.VMEM((16, TOKENS, 1024), BF16),
            pltpu.VMEM((8, 2, 4, 16, 3072), BF16),
            pltpu.VMEM((2, 4, 16, 128), F32),
            pltpu.VMEM((16, 288, 128), BF16),
            pltpu.VMEM((16, 288, 128), BF16),
            pltpu.VMEM((16, 96, 128), BF16),
            pltpu.VMEM((LENGTH, 64), BF16),
            pltpu.VMEM((64, LENGTH), BF16),
            pltpu.VMEM((1, LENGTH), F32),
            pltpu.VMEM((64, LENGTH), F32),
            pltpu.VMEM((LENGTH, 64), F32),
            pltpu.VMEM((LENGTH, 64), F32),
            pltpu.VMEM((2 * TOKENS, 6144), BF16),
            pltpu.VMEM((2 * TOKENS, 3072), BF16),
            pltpu.VMEM((TOKENS, 3072), BF16),
            pltpu.VMEM((192, LENGTH), BF16),
            pltpu.VMEM((8, 192, 128), BF16),
            pltpu.VMEM((8, 192, 128), BF16),
            pltpu.VMEM((192, 128), BF16),
            pltpu.VMEM((9, 2, 4, 4, 2, 16, 512), BF16),
            Sum.scratch(),
            pltpu.VMEM((2, 4, 16, 128), F32),
            pltpu.VMEM((4, 2, 16, 128), F32),
            pltpu.VMEM((4, 16, 128), F32),
            pltpu.VMEM((4, 16, 128), F32),
            DMA((15,)), DMA((15,)),
            DMA((15,)), DMA((15,)),
            DMA((6,)), DMA((6,)),
            DMA((10,)), DMA((10,)),
            DMA((7,)), DMA((7,)),
            DMA((15,)), DMA((15,)),
            DMA((4,)), DMA((4,)),
            DMA((19,)),
        ],
        compiler_params=pltpu.CompilerParams(collective_id=2, has_side_effects=True, vmem_limit_bytes=62 * MIB),
        name="backward_attention",
    )(gm, q_all, k_all, v_all, q_t, k_t, o_t, log_total, grad_first, sm,
      x_far, first_low, mixed, act, gs, gfl, gp, *quarters)


def unpack_kernel(out, heads, o_qkv, o_out, o_in, o_back):
    def unit(u):
        return out[u].reshape(128, 1024).astype(F32)

    o_out[...] = unit(0)
    for j in range(4):
        value = unit(1 + j)
        o_in[:, 512 * j : 512 * j + 512] = value[:, 0:512]
        o_in[:, 2048 + 512 * j : 2560 + 512 * j] = value[:, 512:1024]
        o_back[128 * j : 128 * j + 128, :] = unit(5 + j)
    for i in range(3):
        part = slice(64 * i, 64 * i + 64)
        for p in range(8):
            both = jnp.concatenate([heads[2 * p, part, :], heads[2 * p + 1, part, :]], axis=0)
            o_qkv[:, 1024 * i + 128 * p : 1024 * i + 128 * p + 128] = both.astype(F32).T


def unpack(out, heads):
    shape = jax.ShapeDtypeStruct
    vmem = pl.BlockSpec(memory_space=pltpu.VMEM)
    return pl.pallas_call(
        unpack_kernel,
        out_shape=(shape((128, 3072), F32), shape((128, 1024), F32), shape((128, 4096), F32), shape((512, 1024), F32)),
        in_specs=[vmem, vmem],
        out_specs=(vmem,) * 4,
        compiler_params=pltpu.CompilerParams(vmem_limit_bytes=30 * MIB),
        name="unpack_gradients",
    )(out, heads)


def widened(values):
    return values.astype(F32)


def layer_norm(hidden, gain, offset):
    center = hidden - jnp.mean(hidden, axis=-1, keepdims=True)
    inverse = lax.rsqrt(jnp.mean(center * center, axis=-1, keepdims=True) + EPSILON)
    normed = center * inverse
    return (normed * gain + offset, normed, inverse)


def norm_back(upstream, normed, inverse, gain):
    scaled = upstream * gain
    return inverse * (
        scaled
        - jnp.mean(scaled, axis=-1, keepdims=True)
        - normed * jnp.mean(scaled * normed, axis=-1, keepdims=True)
    )


def gelu_value(inputs):
    return 0.5 * inputs * (1.0 + jax.scipy.special.erf(inputs * ROOT_HALF))


def gelu_slope(inputs):
    return (
        0.5 * (1.0 + jax.scipy.special.erf(inputs * ROOT_HALF))
        + inputs * jnp.exp(-0.5 * inputs * inputs) * INV_ROOT_TWO_PI
    )


def shards(layer_input, cotangent, w_qkv, b_q, b_v, w_out, b_out, g_attn, beta_attn, w_in, b_in, w_back, b_back,
           g_mlp, beta_mlp):
    width = layer_input.shape[-1]
    small = jnp.concatenate(
        [jnp.stack([b_q, b_v, b_out, g_attn, beta_attn, b_back, g_mlp, beta_mlp]), b_in.reshape(4, 128),
         jnp.zeros((4, 128), BF16)]
    )
    rows = layer_input.reshape(-1, width)
    (q_all, k_all, v_all, q_t, k_t, o_t, log_total, mixed, smalls, x_all, g_out, g_in, g_back, g_qkv) = forward(
        rows, small, w_qkv, w_out, w_in, w_back
    )
    quarters = [g_qkv] + [
        lax.ppermute(g_qkv, "ctx", [(i, (i + 4 * d) % 16) for i in range(16)]) for d in (1, 2, 3)
    ]
    smalls = widened(smalls)
    _, _, bout, gattn, battn, bback, gmlp, bmlp = (smalls[:, i].reshape(width) for i in range(8))
    bin_ = smalls[:, 8:12].reshape(4 * width)

    first_sum = rows + dot(mixed, g_out) + bout
    first_out, first_normed, first_inverse = layer_norm(first_sum, gattn, battn)
    first_low = first_out.astype(BF16)
    pre_act = dot(first_low, g_in) + bin_
    activated = gelu_value(pre_act).astype(BF16)
    second_sum = first_out + dot(activated, g_back) + bback
    output, second_normed, second_inverse = layer_norm(second_sum, gmlp, bmlp)

    upstream = cotangent.reshape(-1, width)
    grad_g_mlp = jnp.sum(upstream * second_normed, axis=0)
    grad_beta_mlp = jnp.sum(upstream, axis=0)
    grad_second = norm_back(upstream, second_normed, second_inverse, gmlp)
    grad_b_back = jnp.sum(grad_second, axis=0)
    grad_second_low = grad_second.astype(BF16)
    grad_pre = dot_nt(grad_second_low, g_back) * gelu_slope(pre_act)
    grad_b_in = jnp.sum(grad_pre, axis=0)
    grad_pre_low = grad_pre.astype(BF16)
    grad_first_out = grad_second + dot_nt(grad_pre_low, g_in)
    grad_g_attn = jnp.sum(grad_first_out * first_normed, axis=0)
    grad_beta_attn = jnp.sum(grad_first_out, axis=0)
    grad_first = norm_back(grad_first_out, first_normed, first_inverse, gattn)
    grad_b_out = jnp.sum(grad_first, axis=0)
    grad_first_low = grad_first.astype(BF16)
    grad_mixed = dot_nt(grad_first_low, g_out).astype(BF16)

    blank = jnp.zeros((width,), F32)
    sm = jnp.stack(
        [blank, blank, grad_b_out, grad_g_attn, grad_beta_attn, grad_b_back, grad_g_mlp, grad_beta_mlp]
    )
    sm = jnp.concatenate(
        [sm.reshape(8, 8, 128).transpose(1, 0, 2), grad_b_in.reshape(8, 4, 128), jnp.zeros((8, 4, 128), F32)], axis=1
    ).reshape(2, 4, 16, 128)
    grad_input, owned, heads, own_small = backward(
        grad_mixed, q_all, k_all, v_all, q_t, k_t, o_t, log_total, grad_first, sm,
        x_all, first_low, mixed, activated, grad_second_low, grad_first_low, grad_pre_low, *quarters
    )
    o_qkv, o_out, o_in, o_back = unpack(owned, heads)
    return (
        output.reshape(layer_input.shape),
        grad_input.reshape(layer_input.shape),
        o_qkv,
        own_small[0],
        own_small[1],
        o_out,
        own_small[2],
        own_small[3],
        own_small[4],
        o_in,
        own_small[8:12].reshape(512),
        o_back,
        own_small[5],
        own_small[6],
        own_small[7],
    )


def solution(mesh):
    big, mat, vec = P("fsdp", "ctx", None), P("fsdp", None), P("fsdp")
    params = (mat, vec, vec, mat, vec, vec, vec, mat, vec, mat, vec, vec, vec)
    return jax.shard_map(
        shards, mesh=mesh, in_specs=(big, big) + params, out_specs=(big, big) + params, check_vma=False
    )
```

```python
import jax
import jax.numpy as jnp
from jax import lax
from jax.experimental import pallas as pl
from jax.experimental.pallas import tpu as pltpu
from jax.sharding import PartitionSpec as P

EPSILON = 1e-05
ROOT_HALF = 0.7071067811865476
INV_ROOT_TWO_PI = 0.3989422804014327
BF16 = jnp.bfloat16
F32 = jnp.float32
MESH = pl.DeviceIdType.MESH
MIB = 2**20


def place():
    fsdp, ctx = lax.axis_index("fsdp"), lax.axis_index("ctx")
    return (lax.rem(ctx // 2, 2) * 2 + fsdp // 4, lax.rem(fsdp, 4), ctx // 4, lax.rem(ctx, 2))


def device_at(x, y, z, core):
    x, y, z, core = (lax.rem(x + 4, 4), lax.rem(y + 4, 4), lax.rem(z + 4, 4), lax.rem(core, 2))
    return {"fsdp": lax.rem(x, 2) * 4 + y, "ctx": z * 4 + (x // 2) * 2 + core}


def greet(devices):
    barrier = pltpu.get_barrier_semaphore()
    for device in devices:
        pl.semaphore_signal(barrier, inc=1, device_id=device, device_id_type=MESH)
    pl.semaphore_wait(barrier, len(devices))


def remote(src, dst, send, recv, device):
    return pltpu.make_async_remote_copy(
        src_ref=src, dst_ref=dst, send_sem=send, recv_sem=recv, device_id=device, device_id_type=MESH
    )


BLOCK = 256
TOKENS = 192
LENGTH = 3072
DMA = pltpu.SemaphoreType.DMA


def peers():
    fsdp, me = lax.axis_index("fsdp"), lax.axis_index("ctx")
    return me, [(lax.rem(me + d, 16), {"fsdp": fsdp, "ctx": lax.rem(me + d, 16)}) for d in range(1, 16)]


def exchange(src, dst, me, others, sends, recvs, local):
    copies = []
    for i, (other, device) in enumerate(others):
        copy = remote(src.at[other], dst.at[me], sends.at[i], recvs.at[i], device)
        copy.start()
        copies.append(copy)
    mine = pltpu.make_async_copy(src.at[me], dst.at[me], local)
    mine.start()
    return copies + [mine]


def wait_all(copies):
    for copy in copies:
        copy.wait()


def dot(a, b):
    return jnp.dot(a, b, preferred_element_type=F32)


def dot_nt(a, b):
    return lax.dot_general(a, b, (((1,), (1,)), ((), ())), preferred_element_type=F32)


def dot_tn(a, b):
    return lax.dot_general(a, b, (((0,), (0,)), ((), ())), preferred_element_type=F32)


def beside(a, b):
    return jnp.concatenate([a, b], axis=1)


def flipped(value):
    return value.astype(F32).T.astype(BF16)


def block_span(i, size):
    return pl.ds(pl.multiple_of(i * size, size), size)


class Gather:
    def __init__(self, sources, fulls, chunks, sems, at, pending):
        self.sources, self.fulls, self.chunks, self.pending = sources, fulls, chunks, pending
        self.sems = sems
        x, y, z, core = at
        self.y, self.core, self.low = y, core, lax.rem(x, 2)
        self.up, self.down = device_at(x, y + 1, z, core), device_at(x, y - 1, z, core)
        self.xs = [device_at(x + 1, y, z, core), device_at(x - 1, y, z, core)]
        self.sibling = device_at(x, y, z, core + 1)
        self.copies = {}

    def shard_rows(self, array):
        return self.sources[array].shape[0]

    def rows(self, c, block, way=None):
        array, first, count = self.chunks[c]
        rows = self.shard_rows(array)
        start = block * rows + self.core * (rows // 2) + first
        if way is not None:
            count = count // 2
            start = start + way * count
        return pl.ds(pl.multiple_of(start, 16), count)

    def block(self, e, far=False):
        side = 1 - self.low if far else self.low
        return side * 4 + lax.rem(self.y - e + 4, 4)

    def own(self, array, local):
        rows = self.shard_rows(array)
        copy = pltpu.make_async_copy(
            self.sources[array], self.fulls[array].at[block_span(self.block(0), rows)], local
        )
        copy.start()
        return copy

    def go(self, key, kind, c, slot, src, rows, device):
        full = self.fulls[self.chunks[c][0]]
        sends, recvs = self.sems[2 * kind : 2 * kind + 2]
        copy = remote(full.at[rows] if src is None else src, full.at[rows], sends.at[c, slot], recvs.at[c, slot], device)
        copy.start()
        self.copies[key, c, slot] = copy
        self.pending.append(copy)

    def start(self, c):
        source = self.sources[self.chunks[c][0]]
        mine = self.block(0)
        self.go("y", 0, c, 0, source.at[self.rows(c, 0)], self.rows(c, mine), self.up)
        self.go("y", 0, c, 1, source.at[self.rows(c, 0)], self.rows(c, mine), self.down)

    def start_x(self, c):
        source = self.sources[self.chunks[c][0]]
        mine = self.block(0)
        for way in (0, 1):
            self.go("x", 1, c, way, source.at[self.rows(c, 0, way)], self.rows(c, mine, way), self.xs[way])

    def along_x(self, c, e, way):
        self.go("x", 1, c, 2 * e + way, None, self.rows(c, self.block(e), way), self.xs[way])

    def to_core(self, c, slot, rows):
        self.go("c", 2, c, slot, None, rows, self.sibling)

    def relay(self, c):
        for slot, e, device in ((0, 1, self.up), (1, 3, self.down)):
            self.copies["y", c, slot].wait_recv()
            self.go("y", 0, c, 2 + slot, None, self.rows(c, self.block(e), slot), device)
            for way in (0, 1):
                self.along_x(c, e, way)
            self.to_core(c, slot, self.rows(c, self.block(e)))

    def last(self, c):
        for way in (0, 1):
            self.copies["y", c, 2 + way].wait_recv()
            self.along_x(c, 2, way)
        self.to_core(c, 2, self.rows(c, self.block(2)))

    def share(self, c):
        for e in (0, 1, 3, 2):
            for way in (0, 1):
                self.copies["x", c, 2 * e + way].wait_recv()
                self.to_core(c, 3 + 2 * e + way, self.rows(c, self.block(e, True), way))

    def settle(self, c):
        for slot in range(11):
            self.copies["c", c, slot].wait_recv()

    @staticmethod
    def scratch(n):
        return (DMA((n, 4)),) * 2 + (DMA((n, 8)),) * 2 + (DMA((n, 11)),) * 2


class PlaneGather:
    def __init__(self, source, full, sems, at, pending):
        x, y, z, core = at
        self.full, self.sems, self.at, self.pending = full, sems, at, pending
        self.source = source.at[pl.ds(pl.multiple_of(core * 64 + z * 16, 16), 16)]
        self.xs = [device_at(x + 1, y, z, core), device_at(x - 1, y, z, core)]
        self.ys = [device_at(x, y + 1, z, core), device_at(x, y - 1, z, core), device_at(x, y + 2, z, core)]
        self.zs = [device_at(x, y, z + 1, core), device_at(x, y, z - 1, core)]
        self.sibling = device_at(x, y, z, core + 1)
        self.moves = {}

    def go(self, slot, src, dst, device):
        copy = remote(src, dst, self.sems[0].at[slot], self.sems[1].at[slot], device)
        copy.start()
        self.moves[slot] = copy
        self.pending.append(copy)

    def block(self, e):
        x, y, z, core = self.at
        return self.full.at[lax.rem(x, 2) * 4 + lax.rem(y - e + 4, 4), core, z]

    def start(self, local):
        self.own = pltpu.make_async_copy(self.source, self.block(0), local)
        self.own.start()
        for slot in range(3):
            self.go(slot, self.source, self.block(0), self.ys[slot])
        self.go(3, self.source, self.block(0), self.xs[0])

    def along_x(self):
        for slot, e in ((0, 1), (1, 3), (2, 2)):
            self.moves[slot].wait_recv()
            self.go(3 + e, self.block(e), self.block(e), self.xs[e % 2])

    def along_z(self):
        _, _, z, core = self.at
        self.own.wait()
        for slot in range(3, 7):
            self.moves[slot].wait_recv()
        ref = self.full.at[:, core, z]
        for slot in range(2):
            self.go(7 + slot, ref, ref, self.zs[slot])
        self.go(10, ref, ref, self.sibling)

    def relay(self):
        _, _, z, core = self.at
        for slot, d in ((0, 3), (1, 1)):
            self.moves[7 + slot].wait_recv()
            ref = self.full.at[pl.ds(4 * slot, 4), core, lax.rem(z + d, 4)]
            self.go(9 + 5 * slot, ref, ref, self.zs[slot])
            ref = self.full.at[:, core, lax.rem(z + d, 4)]
            self.go(11 + slot, ref, ref, self.sibling)

    def to_core(self):
        _, _, z, core = self.at
        for slot in (9, 14):
            self.moves[slot].wait_recv()
        ref = self.full.at[:, core, lax.rem(z + 2, 4)]
        self.go(13, ref, ref, self.sibling)

    def settle(self):
        for slot in range(10, 14):
            self.moves[slot].wait_recv()

    @staticmethod
    def scratch():
        return (DMA((15,)),) * 2


CHUNKS = ((0, 0, 64), (1, 0, 32), (1, 32, 32), (2, 0, 128), (2, 128, 128))


def forward_kernel(x_in, small, w_qkv, w_out, w_in, w_back,
                   q_all, k_all, v_all, q_t, k_t, o_t, log_total, mixed, smalls, x_out, g_out, g_in, g_back, g_qkv,
                   x_all, tiles, w_got, w_head, v_t, o_send, o_got, scores_a, scores_b, high_a, high_b,
                   g_sems, q_sems, s_s, s_r, h_s, h_r, n_s, n_r, b_s, b_r, local):
    x, y, z, core = place()
    me, others = peers()
    low, high = lax.rem(x, 2), x // 2
    shard = low * 4 + y
    sibling = device_at(x, y, z, core + 1)
    pending, locals_ = [], []

    def begin(copy):
        copy.start()
        pending.append(copy)
        return copy

    def keep(src, dst, slot):
        copy = pltpu.make_async_copy(src, dst, local.at[slot])
        copy.start()
        return copy

    tile_copies = [
        keep(w_qkv.at[:, block_span(8 * i + me // 2, 128)], tiles.at[i], i) for i in range(3)
    ]
    x_all[me] = x_in[...].astype(BF16)
    across = [
        (lax.rem(low + a, 2), d) for a in (0, 1) for d in range(4) if (a, d) != (0, 0)
    ]
    across = [device_at(high * 2 + a, y + d, z, core) for a, d in across]
    greet([device for _, device in others] + across + [device_at(high * 2 - 1 + 3 * low, y, z, core)])

    def index(dz, dh, dk=0):
        return lax.rem(z + dz + 4, 4) * 4 + lax.rem(high + dh, 2) * 2 + lax.rem(core + dk, 2)

    up, down = device_at(x, y, z + 1, core), device_at(x, y, z - 1, core)
    first_half, second_half = pl.ds(0, 96), pl.ds(96, 96)

    def pass_on(slot, block, device, rows=None):
        ref = x_all.at[block] if rows is None else x_all.at[block, rows]
        return begin(remote(ref, ref, h_s.at[slot], h_r.at[slot], device))

    def share_rows(slot, block):
        ref = x_all.at[block]
        return begin(remote(ref, ref, n_s.at[slot], n_r.at[slot], sibling))

    moves = {1: pass_on(1, me, up), 2: pass_on(2, me, down), 0: pass_on(0, me, device_at(x + 2, y, z, core))}
    nears = [share_rows(7, me)]

    odd = lax.rem(me, 2) == 1
    for copy in tile_copies:
        copy.wait()

    def column_half(value):
        return jnp.where(odd, value[:, 64:128], value[:, 0:64])

    parts = [column_half(tiles[i].astype(F32)) for i in range(3)]
    w_got[shard, 0:128, :] = beside(parts[0], parts[1]).astype(BF16)
    w_got[shard, 128:192, :] = beside(parts[2][0:64], parts[2][64:128]).astype(BF16)
    w_got[shard, 192:208, :] = small[...]
    head_copies = []
    for i, device in enumerate(across):
        ref = w_got.at[shard]
        head_copies.append(begin(remote(ref, ref, s_s.at[i], s_r.at[i], device)))

    whole = Gather((w_out, w_in, w_back), (g_out, g_in, g_back), CHUNKS, g_sems, (x, y, z, core), pending)
    plane = PlaneGather(w_qkv, g_qkv, q_sems, (x, y, z, core), pending)
    plane.start(local.at[3])
    for c in range(2):
        whole.start(c)
    for array in range(3):
        locals_.append(whole.own(array, local.at[4 + array]))

    for copy in head_copies:
        copy.wait_recv()
    for f in range(8):
        span = slice(128 * f, 128 * f + 128)
        w_head[span, 0:128] = w_got[f, 0:128, :]
        w_head[128 * f : 128 * f + 64, 128:192] = w_got[f, 128:192, 0:64]
        w_head[128 * f + 64 : 128 * f + 128, 128:192] = w_got[f, 128:192, 64:128]
        smalls[f] = w_got[f, 192:208, :]
    bias = w_got[me // 2, 192:208, :].astype(F32)
    bias = jnp.concatenate(
        [column_half(bias[0:1]), jnp.zeros((1, 64), F32), column_half(bias[1:2])], axis=1
    )
    scale = jnp.where(lax.broadcasted_iota(jnp.int32, (1, 192), 1) < 64, 0.125, 1.0)

    def project(block):
        value = ((dot(x_all[block], w_head[:, 0:192]) + bias) * scale).astype(BF16)
        rows = pl.ds(pl.multiple_of(block * TOKENS, 64), TOKENS)
        q_all[rows, :] = value[:, 0:64]
        k_all[rows, :] = value[:, 64:128]
        v_all[rows, :] = value[:, 128:192]

    project(me)
    moves[1].wait_recv()
    moves[4] = pass_on(4, index(-1, 0), up, first_half)
    moves[2].wait_recv()
    moves[5] = pass_on(5, index(1, 0), down, second_half)
    moves[0].wait_recv()
    moves[6] = pass_on(6, index(0, 1), up)
    moves[7] = pass_on(7, index(0, 1), down)
    nears += [share_rows(0, index(-1, 0)), share_rows(1, index(1, 0)), share_rows(2, index(0, 1))]
    for c in range(2):
        whole.start_x(c)
    plane.along_x()
    project(index(-1, 0))
    project(index(1, 0))
    project(index(0, 1))
    nears[0].wait_recv()
    project(index(0, 0, 1))
    whole.relay(0)
    whole.start(2)
    whole.start_x(2)
    moves[4].wait_recv()
    moves[5].wait_recv()
    nears.append(share_rows(3, index(2, 0)))
    project(index(2, 0))
    moves[6].wait_recv()
    moves[8] = pass_on(8, index(-1, 1), up, first_half)
    moves[7].wait_recv()
    moves[9] = pass_on(9, index(1, 1), down, second_half)
    nears += [share_rows(4, index(-1, 1)), share_rows(5, index(1, 1))]
    plane.along_z()
    whole.relay(1)
    whole.start(3)
    whole.start_x(3)
    whole.last(0)
    for i, spot in enumerate(((-1, 0), (1, 0), (0, 1), (2, 0))):
        nears[1 + i].wait_recv()
        project(index(*spot, 1))
    project(index(-1, 1))
    project(index(1, 1))
    for i, spot in enumerate(((-1, 1), (1, 1))):
        nears[5 + i].wait_recv()
        project(index(*spot, 1))
    moves[8].wait_recv()
    moves[9].wait_recv()
    nears.append(share_rows(6, index(2, 1)))
    project(index(2, 1))
    nears[7].wait_recv()
    project(index(2, 1, 1))
    kept = keep(x_all, x_out, 7)
    whole.relay(2)
    whole.last(1)
    whole.start(4)
    whole.start_x(4)
    whole.share(0)
    plane.relay()

    for i in range(LENGTH // BLOCK):
        span = slice(BLOCK * i, BLOCK * i + BLOCK)
        q_t[:, span] = flipped(q_all[span, :])
        k_t[:, span] = flipped(k_all[span, :])
        v_t[0:64, span] = flipped(v_all[span, :])
    v_t[64:80, :] = jnp.ones((16, LENGTH), BF16)

    def make_scores(i, scores, highest):
        value = dot(k_all[...], q_t[:, block_span(i, BLOCK)])
        scores[...] = value
        highest[...] = jnp.max(value, axis=0, keepdims=True)

    def mix(i, scores, highest):
        span = block_span(i, BLOCK)
        out = dot(v_t[...], jnp.exp(scores[...] - highest[...]).astype(BF16))
        total = out[64:65]
        o_t[:, span] = (out[0:64] / total).astype(BF16)
        log_total[:, span] = highest[...] + jnp.log(total)

    def two_blocks(i, _):
        make_scores(2 * i + 1, scores_b, high_b)
        mix(2 * i, scores_a, high_a)
        make_scores(jnp.minimum(2 * i + 2, LENGTH // BLOCK - 1), scores_a, high_a)
        mix(2 * i + 1, scores_b, high_b)
        return 0

    make_scores(0, scores_a, high_a)
    lax.fori_loop(0, 1, two_blocks, 0)
    whole.relay(3)
    whole.last(2)
    whole.share(1)
    lax.fori_loop(1, 2, two_blocks, 0)
    whole.relay(4)
    whole.last(3)
    whole.share(2)
    lax.fori_loop(2, 4, two_blocks, 0)
    plane.to_core()
    whole.last(4)
    whole.share(3)
    lax.fori_loop(4, 6, two_blocks, 0)
    for j in range(16):
        part = o_t[:, j * 192 : (j + 1) * 192].astype(F32)
        o_send[j] = jnp.concatenate([part[:, 0:96], part[:, 96:192]], axis=0).T.astype(BF16)
    copies = exchange(o_send, o_got, me, others, b_s, b_r, local.at[8])
    whole.share(4)
    wait_all(copies)
    for p in range(8):
        a, b = o_got[2 * p].astype(F32), o_got[2 * p + 1].astype(F32)
        span = slice(128 * p, 128 * p + 128)
        mixed[0:96, span] = beside(a[:, 0:64], b[:, 0:64]).astype(BF16)
        mixed[96:192, span] = beside(a[:, 64:128], b[:, 64:128]).astype(BF16)
    for c in range(len(CHUNKS)):
        whole.settle(c)
    plane.settle()
    for copy in pending:
        copy.wait_send()
    wait_all(locals_)
    kept.wait()


def forward(x_in, small, w_qkv, w_out, w_in, w_back):
    vmem, far = pl.BlockSpec(memory_space=pltpu.VMEM), pl.BlockSpec(memory_space=pl.ANY)
    n = len(CHUNKS)
    shape = jax.ShapeDtypeStruct
    return pl.pallas_call(
        forward_kernel,
        out_shape=(
            shape((LENGTH, 64), BF16),
            shape((LENGTH, 64), BF16),
            shape((LENGTH, 64), BF16),
            shape((64, LENGTH), BF16),
            shape((64, LENGTH), BF16),
            shape((64, LENGTH), BF16),
            shape((1, LENGTH), F32),
            shape((TOKENS, 1024), BF16),
            shape((8, 16, 128), BF16),
            shape((16, TOKENS, 1024), BF16),
            shape((1024, 1024), BF16),
            shape((1024, 4096), BF16),
            shape((4096, 1024), BF16),
            shape((8, 2, 4, 16, 3072), BF16),
        ),
        in_specs=[vmem] * 6,
        out_specs=(vmem,) * 9 + (far,) * 5,
        scratch_shapes=[
            pltpu.VMEM((16, TOKENS, 1024), BF16),
            pltpu.VMEM((3, 128, 128), BF16),
            pltpu.VMEM((8, 208, 128), BF16),
            pltpu.VMEM((1024, 256), BF16),
            pltpu.VMEM((80, LENGTH), BF16),
            pltpu.VMEM((16, 96, 128), BF16),
            pltpu.VMEM((16, 96, 128), BF16),
            pltpu.VMEM((LENGTH, BLOCK), F32),
            pltpu.VMEM((LENGTH, BLOCK), F32),
            pltpu.VMEM((1, BLOCK), F32),
            pltpu.VMEM((1, BLOCK), F32),
            Gather.scratch(n),
            PlaneGather.scratch(),
            DMA((7,)), DMA((7,)),
            DMA((10,)), DMA((10,)),
            DMA((8,)), DMA((8,)),
            DMA((15,)), DMA((15,)),
            DMA((10,)),
        ],
        compiler_params=pltpu.CompilerParams(collective_id=1, has_side_effects=True, vmem_limit_bytes=60 * MIB),
        name="forward_attention",
    )(x_in, small, w_qkv, w_out, w_in, w_back)


TURNS = (2, 1, 0, 1, 0, 1, 2, 1, 0)
PIECES = (((4, 4), (2, 4, 2), (2, 4, 2)), ((4,), (2, 2), (4,)), ((), (), ()))


class Sum:
    def __init__(self, acc, bufs, final, out, sems, at, pending):
        self.acc, self.bufs, self.final, self.out = acc, bufs, final, out
        self.sems, self.at, self.pending = sems, at, pending
        self.mine = block_span(at[3], 512)
        self.sibling = device_at(*at[:3], at[3] + 1)
        self.copies = {}

    def line(self, axis, d):
        to = list(self.at[:3])
        to[axis] = lax.rem(to[axis] + d, 4)
        return to[axis], device_at(*to, self.at[3])

    def piece(self, stage, u, c):
        turn = TURNS[u]
        if stage == 0:
            ref = self.acc.at[u]
            if turn == 0:
                return ref.at[lax.rem(c, 2), :, :, c // 2]
            return ref.at[:, c] if turn == 1 else ref.at[:, :, c]
        ref = self.piece(stage - 1, u, self.at[(turn + stage - 1) % 3])
        if (turn + stage) % 3 == 0:
            return ref.at[lax.rem(c, 2), c // 2] if turn == 1 else ref.at[lax.rem(c, 2), :, c // 2]
        return ref.at[:, c] if turn == 1 else ref.at[c]

    def buffer(self, stage, u):
        turn = TURNS[u]
        return self.bufs[stage][turn].at[TURNS[:u].count(turn)]

    def start(self, stage, *units):
        sends, recvs = self.sems[2 * stage : 2 * stage + 2]
        for u in units:
            axis = (TURNS[u] + stage) % 3
            for d in (1, 3, 2):
                c, device = self.line(axis, d)
                copy = remote(
                    self.piece(stage, u, c),
                    self.buffer(stage, u).at[d - 1],
                    sends.at[u, d - 1],
                    recvs.at[u, d - 1],
                    device,
                )
                copy.start()
                self.copies[stage, u, d] = copy
                self.pending.append(copy)

    def finish(self, stage, *units):
        for u in units:
            for d in (1, 3, 2):
                self.copies[stage, u, d].wait_recv()
            own = self.piece(stage, u, self.at[(TURNS[u] + stage) % 3])
            buf = self.buffer(stage, u)
            total = own[...].astype(F32) + buf[0].astype(F32) + buf[1].astype(F32) + buf[2].astype(F32)
            if stage == 2:
                self.final[u] = total.astype(BF16)
            else:
                own[...] = total.astype(BF16)
                self.start(stage + 1, u)

    def go(self, key, slot, src, dst, device):
        sends, recvs = self.sems[6:8] if key == "far" else self.sems[8:10]
        copy = remote(src, dst, sends.at[slot], recvs.at[slot], device)
        copy.start()
        self.copies[key, slot] = copy
        self.pending.append(copy)

    def spot(self, dz, dh):
        x, y, z, core = self.at
        return self.out.at[:, lax.rem(z + dz, 4), lax.rem(x // 2 + dh, 2), :, self.mine]

    def spread(self, local):
        mine = self.spot(0, 0)
        self.go("far", 0, self.final, mine, self.line(0, 2)[1])
        for d in (1, 3, 2):
            self.go("far", d, self.final, mine, self.line(2, d)[1])
        self.go("near", 0, self.final, mine, self.sibling)
        own = pltpu.make_async_copy(self.final, mine, local)
        own.start()
        own.wait()

    def relay(self):
        self.copies["far", 0].wait_recv()
        ref = self.spot(0, 1)
        for d in (1, 3, 2):
            self.go("far", 3 + d, ref, ref, self.line(2, d)[1])
        self.go("near", 1, ref, ref, self.sibling)

    def share(self):
        for dh in (0, 1):
            for d in (1, 3, 2):
                self.copies["far", 3 * dh + d].wait_recv()
                ref = self.spot(4 - d, dh)
                self.go("near", 1 + 3 * dh + d, ref, ref, self.sibling)

    def end(self):
        for slot in range(8):
            self.copies["near", slot].wait_recv()

    @staticmethod
    def scratch():
        bufs = tuple(
            tuple(
                pltpu.VMEM((TURNS.count(turn), 3) + shapes[turn] + (16, 512), BF16) for turn in range(3)
            )
            for shapes in PIECES
        )
        n = len(TURNS)
        return (
            bufs,
            pltpu.VMEM((n, 16, 512), BF16),
            (DMA((n, 3)),) * 6 + (DMA((7,)),) * 2 + (DMA((8,)),) * 2,
        )


def backward_kernel(gm, q_all, k_all, v_all, q_t, k_t, o_t, log_total, grad_first, sm_in,
                    x_far, first_low, mixed, act, gs, gfl, gp, g_far,
                    grad_input, out, qkv_out, sm_out,
                    x_all, g_qkv, sm, back, send, do_got, do_all, do_t, delta, dq_t, dk, dv,
                    lhs, rhs, gproj, head_t, head_send, head_got, head_sum, acc, sum_a, s0, s1, s2, s3,
                    a_s, a_r, b_s, b_r, n_s, n_r, t_s, t_r, h_s, h_r, p_s, p_r, local):
    x, y, z, core = at = place()
    me, others = peers()
    low = lax.rem(x, 2)
    shard = low * 4 + y
    sibling = device_at(x, y, z, core + 1)
    pending = []

    def keep(src, dst, slot):
        copy = pltpu.make_async_copy(src, dst, local.at[slot])
        copy.start()
        return copy

    for h in range(16):
        part = gm[:, 64 * h : 64 * h + 64].astype(F32)
        send[h, 0:96, :] = beside(part[0:96], part[96:192]).astype(BF16)
    across = [(a, d) for a in (0, 1) for d in range(4) if (a, d) != (0, 0)]
    across = [
        (lax.rem(low + a, 2) * 4 + lax.rem(y + d, 4), device_at(x // 2 * 2 + lax.rem(low + a, 2), y + d, z, core))
        for a, d in across
    ]
    greet([device for _, device in others] + [device for _, device in across]
          + [device_at(x // 2 * 2 - 1 + 3 * low, y, z, core)])
    a_copies = exchange(send.at[:, 0:96], do_got, me, others, a_s, a_r, local.at[0])

    near = []
    upper, lower = pl.ds(0, TOKENS), pl.ds(TOKENS, TOKENS)
    moves = [
        (mixed, None, lhs, 1024, 1024),
        (gfl, 512, rhs, 512, 512),
        (first_low, None, lhs, 0, 1024),
        (gp, 2048, rhs, 1024, 2048),
        (act, None, lhs, 2048, 4096),
        (gs, 512, rhs, 0, 512),
    ]
    for i, (src, cols, dst, first, count) in enumerate(moves):
        own = src if cols is None else src.at[:, block_span(core, cols)]
        other = src if cols is None else src.at[:, block_span(1 - core, cols)]
        span = pl.ds(first, count)
        copy = remote(other, dst.at[lower, span], n_s.at[i], n_r.at[i], sibling)
        copy.start()
        near.append((copy, keep(own, dst.at[upper, span], 1 + i)))
        pending.append(copy)
    x_copy = keep(x_far, x_all, 7)
    g_copy = keep(g_far, g_qkv, 8)
    dk[...] = jnp.zeros_like(dk)
    dv[...] = jnp.zeros_like(dv)
    sums = Sum(acc, sum_a[0], sum_a[1], out, sum_a[2], at, pending)

    def arrive(*which):
        for i in which:
            near[i][0].wait_recv()
            near[i][1].wait()

    def product(unit, first, column):
        for side in range(2):
            value = dot_tn(lhs[:, first + 512 * side : first + 512 * side + 512], rhs[:, column : column + 512])
            acc[unit, side] = value.astype(BF16).reshape(4, 4, 2, 16, 512)
        sums.start(0, unit)

    arrive(0, 1)
    product(0, 1024, 512)
    arrive(2, 3)
    for j in range(4):
        product(1 + j, 0, 1024 + 512 * j)
    arrive(4, 5)
    for j in range(4):
        for side in range(2):
            left = jnp.concatenate(
                [lhs[:, 2048 + 512 * f + 128 * j : 2176 + 512 * f + 128 * j] for f in range(4 * side, 4 * side + 4)],
                axis=1,
            )
            acc[5 + j, side] = dot_tn(left, rhs[:, 0:512]).astype(BF16).reshape(4, 4, 2, 16, 512)
        sums.start(0, 5 + j)

    wait_all(a_copies)
    for j in range(16):
        span = slice(j * 192, (j + 1) * 192)
        do_all[j * 192 : j * 192 + 96, :] = do_got[j, :, 0:64]
        do_all[j * 192 + 96 : j * 192 + 192, :] = do_got[j, :, 64:128]
        pair = do_got[j].astype(F32).T
        flat = beside(pair[0:64], pair[64:128])
        do_t[:, span] = flat.astype(BF16)
        delta[:, span] = jnp.sum(flat * o_t[:, span].astype(F32), axis=0, keepdims=True)

    def block(i, _):
        span = block_span(i, BLOCK)
        prob = jnp.exp(dot(k_all[...], q_t[:, span]) - log_total[:, span])
        grad_prob = dot(v_all[...], do_t[:, span])
        dv[...] += dot(prob.astype(BF16), do_all[span, :])
        grad_scores = (prob * (grad_prob - delta[:, span])).astype(BF16)
        dk[...] += dot(grad_scores, q_all[span, :])
        dq_t[:, span] = dot(k_t[...], grad_scores) * 0.125
        return 0

    lax.fori_loop(0, 5, block, 0)
    sums.finish(0, 0, 1)
    lax.fori_loop(5, 9, block, 0)
    sums.finish(0, 2, 3)
    lax.fori_loop(9, 12, block, 0)
    sum_q = jnp.zeros((1, 64), F32)
    for j in range(16):
        span = slice(j * 192, (j + 1) * 192)
        dq = dq_t[:, span].T
        sum_q = sum_q + jnp.sum(dq, axis=0, keepdims=True)
        send[j, 0:192, :] = beside(dq, dk[span, :]).astype(BF16)
        send[j, 192:288, :] = beside(
            dv[j * 192 : j * 192 + 96, :], dv[j * 192 + 96 : j * 192 + 192, :]
        ).astype(BF16)
    b_copies = exchange(send, back, me, others, b_s, b_r, local.at[0])
    sums.finish(0, 4, 5)

    for i in range(LENGTH // BLOCK):
        span = slice(BLOCK * i, BLOCK * i + BLOCK)
        head_t[0:64, span] = dq_t[:, span].astype(BF16)
        head_t[64:128, span] = dk[span, :].T.astype(BF16)
        head_t[128:192, span] = dv[span, :].T.astype(BF16)
    x_copy.wait()
    head = dot(head_t[...], x_all[...].reshape(LENGTH, 1024))
    for f in range(8):
        head_send[f] = head[:, 128 * f : 128 * f + 128].astype(BF16)
    head_copies = []
    for i, (to, device) in enumerate(across):
        copy = remote(head_send.at[to], head_got.at[shard], h_s.at[i], h_r.at[i], device)
        copy.start()
        head_copies.append(copy)
    head_copies.append(keep(head_send.at[shard], head_got.at[shard], 9))

    sm[...] = sm_in[...]
    odd = lax.rem(me, 2) == 1
    blank = jnp.zeros((1, 64), F32)
    owner = me // 2
    for i, value in enumerate((sum_q, jnp.sum(dv[...], axis=0, keepdims=True))):
        sm[owner // 4, lax.rem(owner, 4), i : i + 1, :] = jnp.where(odd, beside(blank, value), beside(value, blank))
    t_copy = remote(sm, s0, t_s.at[0], t_r.at[0], sibling)
    t_copy.start()

    def small_start(stage, axis, piece, buf):
        copies = []
        for d in (1, 2, 3):
            c, device = sums.line(axis, d)
            slot = 1 + 3 * stage + d - 1
            copies.append(remote(piece(c), buf.at[at[axis]], t_s.at[slot], t_r.at[slot], device))
            copies[-1].start()
        return copies + [keep(piece(at[axis]), buf.at[at[axis]], 10 + stage)]

    sums.finish(0, 6, 7, 8)
    sums.finish(1, 0, 1, 2, 3)
    t_copy.wait()
    s0[...] = s0[...] + sm[...]
    small = small_start(0, 1, lambda c: s0.at[:, c], s1)
    wait_all(head_copies)
    total = head_got[0].astype(F32)
    for f in range(1, 8):
        total = total + head_got[f].astype(F32)
    head_sum[...] = total.astype(BF16)
    p_copies = [keep(head_sum, qkv_out.at[me], 13)]
    for i, (_, device) in enumerate(others):
        copy = remote(head_sum, qkv_out.at[me], p_s.at[i], p_r.at[i], device)
        copy.start()
        p_copies.append(copy)
    sums.finish(1, 4, 5, 6, 7, 8)
    wait_all(small)
    s0[:, 0] = s1[0] + s1[1] + s1[2] + s1[3]
    small = small_start(1, 0, lambda c: s0.at[lax.rem(c, 2), 0], s2)
    sums.finish(2, *range(9))
    sums.spread(local.at[14])
    wait_all(b_copies)
    for p in range(8):
        a, b = back[2 * p].astype(F32), back[2 * p + 1].astype(F32)
        for i, part in enumerate((slice(0, 64), slice(64, 128))):
            cols = slice(1024 * i + 128 * p, 1024 * i + 128 * p + 128)
            gproj[:, cols] = beside(a[0:192, part], b[0:192, part]).astype(BF16)
            gproj[96 * i : 96 * i + 96, 2048 + 128 * p : 2176 + 128 * p] = beside(
                a[192:288, part], b[192:288, part]
            ).astype(BF16)
    sums.relay()
    wait_all(small)
    s0[0, 1] = s2[0] + s2[1] + s2[2] + s2[3]
    small = small_start(2, 2, lambda c: s0.at[0, 1], s3)
    g_copy.wait()
    grad_input[...] = grad_first[...] + dot_nt(gproj[...], g_qkv[...])
    wait_all(small)
    sm_out[...] = s3[0] + s3[1] + s3[2] + s3[3]
    sums.share()
    wait_all(p_copies)
    sums.end()
    for copy in pending:
        copy.wait_send()


def backward(gm, q_all, k_all, v_all, q_t, k_t, o_t, log_total, grad_first, sm,
             x_far, first_low, mixed, act, gs, gfl, gp, g_far):
    vmem, far = pl.BlockSpec(memory_space=pltpu.VMEM), pl.BlockSpec(memory_space=pl.ANY)
    shape = jax.ShapeDtypeStruct
    return pl.pallas_call(
        backward_kernel,
        out_shape=(
            shape((TOKENS, 1024), F32),
            shape((9, 4, 2, 16, 1024), BF16),
            shape((16, 192, 128), BF16),
            shape((16, 128), F32),
        ),
        in_specs=[vmem] * 10 + [far] * 8,
        out_specs=(vmem,) * 4,
        scratch_shapes=[
            pltpu.VMEM((16, TOKENS, 1024), BF16),
            pltpu.VMEM((1024, 3072), BF16),
            pltpu.VMEM((2, 4, 16, 128), F32),
            pltpu.VMEM((16, 288, 128), BF16),
            pltpu.VMEM((16, 288, 128), BF16),
            pltpu.VMEM((16, 96, 128), BF16),
            pltpu.VMEM((LENGTH, 64), BF16),
            pltpu.VMEM((64, LENGTH), BF16),
            pltpu.VMEM((1, LENGTH), F32),
            pltpu.VMEM((64, LENGTH), F32),
            pltpu.VMEM((LENGTH, 64), F32),
            pltpu.VMEM((LENGTH, 64), F32),
            pltpu.VMEM((2 * TOKENS, 6144), BF16),
            pltpu.VMEM((2 * TOKENS, 3072), BF16),
            pltpu.VMEM((TOKENS, 3072), BF16),
            pltpu.VMEM((192, LENGTH), BF16),
            pltpu.VMEM((8, 192, 128), BF16),
            pltpu.VMEM((8, 192, 128), BF16),
            pltpu.VMEM((192, 128), BF16),
            pltpu.VMEM((9, 2, 4, 4, 2, 16, 512), BF16),
            Sum.scratch(),
            pltpu.VMEM((2, 4, 16, 128), F32),
            pltpu.VMEM((4, 2, 16, 128), F32),
            pltpu.VMEM((4, 16, 128), F32),
            pltpu.VMEM((4, 16, 128), F32),
            DMA((15,)), DMA((15,)),
            DMA((15,)), DMA((15,)),
            DMA((6,)), DMA((6,)),
            DMA((10,)), DMA((10,)),
            DMA((7,)), DMA((7,)),
            DMA((15,)), DMA((15,)),
            DMA((15,)),
        ],
        compiler_params=pltpu.CompilerParams(collective_id=2, has_side_effects=True, vmem_limit_bytes=62 * MIB),
        name="backward_attention",
    )(gm, q_all, k_all, v_all, q_t, k_t, o_t, log_total, grad_first, sm,
      x_far, first_low, mixed, act, gs, gfl, gp, g_far)


def unpack_kernel(out, heads, small, o_qkv, o_out, o_in, o_back, o_bin, *vectors):
    for i, vector in enumerate(vectors):
        vector[...] = small[i : i + 1, :]
    o_bin[...] = jnp.concatenate([small[i : i + 1, :] for i in range(8, 12)], axis=1)

    def unit(u):
        return out[u].reshape(128, 1024).astype(F32)

    o_out[...] = unit(0)
    for j in range(4):
        value = unit(1 + j)
        o_in[:, 512 * j : 512 * j + 512] = value[:, 0:512]
        o_in[:, 2048 + 512 * j : 2560 + 512 * j] = value[:, 512:1024]
        o_back[128 * j : 128 * j + 128, :] = unit(5 + j)
    for i in range(3):
        part = slice(64 * i, 64 * i + 64)
        for p in range(8):
            both = jnp.concatenate([heads[2 * p, part, :], heads[2 * p + 1, part, :]], axis=0)
            o_qkv[:, 1024 * i + 128 * p : 1024 * i + 128 * p + 128] = both.astype(F32).T


def unpack(out, heads, small):
    shape = jax.ShapeDtypeStruct
    vmem = pl.BlockSpec(memory_space=pltpu.VMEM)
    return pl.pallas_call(
        unpack_kernel,
        out_shape=(shape((128, 3072), F32), shape((128, 1024), F32), shape((128, 4096), F32), shape((512, 1024), F32),
                   shape((1, 512), F32)) + (shape((1, 128), F32),) * 8,
        in_specs=[vmem] * 3,
        out_specs=(vmem,) * 13,
        compiler_params=pltpu.CompilerParams(vmem_limit_bytes=30 * MIB),
        name="unpack_gradients",
    )(out, heads, small)


def widened(values):
    return values.astype(F32)


def layer_norm(hidden, gain, offset):
    center = hidden - jnp.mean(hidden, axis=-1, keepdims=True)
    inverse = lax.rsqrt(jnp.mean(center * center, axis=-1, keepdims=True) + EPSILON)
    normed = center * inverse
    return (normed * gain + offset, normed, inverse)


def norm_back(upstream, normed, inverse, gain):
    scaled = upstream * gain
    return inverse * (
        scaled
        - jnp.mean(scaled, axis=-1, keepdims=True)
        - normed * jnp.mean(scaled * normed, axis=-1, keepdims=True)
    )


def gelu_value(inputs):
    return 0.5 * inputs * (1.0 + jax.scipy.special.erf(inputs * ROOT_HALF))


def gelu_slope(inputs):
    return (
        0.5 * (1.0 + jax.scipy.special.erf(inputs * ROOT_HALF))
        + inputs * jnp.exp(-0.5 * inputs * inputs) * INV_ROOT_TWO_PI
    )


def shards(layer_input, cotangent, w_qkv, b_q, b_v, w_out, b_out, g_attn, beta_attn, w_in, b_in, w_back, b_back,
           g_mlp, beta_mlp):
    width = layer_input.shape[-1]
    small = jnp.concatenate(
        [jnp.stack([b_q, b_v, b_out, g_attn, beta_attn, b_back, g_mlp, beta_mlp]), b_in.reshape(4, 128),
         jnp.zeros((4, 128), BF16)]
    )
    rows = layer_input.reshape(-1, width)
    (q_all, k_all, v_all, q_t, k_t, o_t, log_total, mixed, smalls, x_all, g_out, g_in, g_back, g_qkv) = forward(
        rows, small, w_qkv, w_out, w_in, w_back
    )
    g_qkv = g_qkv.reshape(width, 3 * width)
    smalls = widened(smalls)
    _, _, bout, gattn, battn, bback, gmlp, bmlp = (smalls[:, i].reshape(width) for i in range(8))
    bin_ = smalls[:, 8:12].reshape(4 * width)

    first_sum = rows + dot(mixed, g_out) + bout
    first_out, first_normed, first_inverse = layer_norm(first_sum, gattn, battn)
    first_low = first_out.astype(BF16)
    pre_act = dot(first_low, g_in) + bin_
    activated = gelu_value(pre_act).astype(BF16)
    second_sum = first_out + dot(activated, g_back) + bback
    output, second_normed, second_inverse = layer_norm(second_sum, gmlp, bmlp)

    upstream = cotangent.reshape(-1, width)
    grad_g_mlp = jnp.sum(upstream * second_normed, axis=0)
    grad_beta_mlp = jnp.sum(upstream, axis=0)
    grad_second = norm_back(upstream, second_normed, second_inverse, gmlp)
    grad_b_back = jnp.sum(grad_second, axis=0)
    grad_second_low = grad_second.astype(BF16)
    grad_pre = dot_nt(grad_second_low, g_back) * gelu_slope(pre_act)
    grad_b_in = jnp.sum(grad_pre, axis=0)
    grad_pre_low = grad_pre.astype(BF16)
    grad_first_out = grad_second + dot_nt(grad_pre_low, g_in)
    grad_g_attn = jnp.sum(grad_first_out * first_normed, axis=0)
    grad_beta_attn = jnp.sum(grad_first_out, axis=0)
    grad_first = norm_back(grad_first_out, first_normed, first_inverse, gattn)
    grad_b_out = jnp.sum(grad_first, axis=0)
    grad_first_low = grad_first.astype(BF16)
    grad_mixed = dot_nt(grad_first_low, g_out).astype(BF16)

    blank = jnp.zeros((width,), F32)
    sm = jnp.stack(
        [blank, blank, grad_b_out, grad_g_attn, grad_beta_attn, grad_b_back, grad_g_mlp, grad_beta_mlp]
    )
    sm = jnp.concatenate(
        [sm.reshape(8, 8, 128).transpose(1, 0, 2), grad_b_in.reshape(8, 4, 128), jnp.zeros((8, 4, 128), F32)], axis=1
    ).reshape(2, 4, 16, 128)
    grad_input, owned, heads, own_small = backward(
        grad_mixed, q_all, k_all, v_all, q_t, k_t, o_t, log_total, grad_first, sm,
        x_all, first_low, mixed, activated, grad_second_low, grad_first_low, grad_pre_low, g_qkv
    )
    o_qkv, o_out, o_in, o_back, o_bin, *vectors = unpack(owned, heads, own_small)
    vectors = [vector.reshape(128) for vector in vectors]
    return (
        output.reshape(layer_input.shape),
        grad_input.reshape(layer_input.shape),
        o_qkv,
        vectors[0],
        vectors[1],
        o_out,
        vectors[2],
        vectors[3],
        vectors[4],
        o_in,
        o_bin.reshape(512),
        o_back,
        vectors[5],
        vectors[6],
        vectors[7],
    )


def solution(mesh):
    big, mat, vec = P("fsdp", "ctx", None), P("fsdp", None), P("fsdp")
    params = (mat, vec, vec, mat, vec, vec, vec, mat, vec, mat, vec, vec, vec)
    return jax.shard_map(
        shards, mesh=mesh, in_specs=(big, big) + params, out_specs=(big, big) + params, check_vma=False
    )
```

```python
import jax
import jax.numpy as jnp
from jax import lax
from jax.experimental import pallas as pl
from jax.experimental.pallas import tpu as pltpu
from jax.sharding import PartitionSpec as P

EPSILON = 1e-05
ROOT_HALF = 0.7071067811865476
INV_ROOT_TWO_PI = 0.3989422804014327
BF16 = jnp.bfloat16
F32 = jnp.float32
MESH = pl.DeviceIdType.MESH
MIB = 2**20


def place():
    fsdp, ctx = lax.axis_index("fsdp"), lax.axis_index("ctx")
    return (lax.rem(ctx // 2, 2) * 2 + fsdp // 4, lax.rem(fsdp, 4), ctx // 4, lax.rem(ctx, 2))


def device_at(x, y, z, core):
    x, y, z, core = (lax.rem(x + 4, 4), lax.rem(y + 4, 4), lax.rem(z + 4, 4), lax.rem(core, 2))
    return {"fsdp": lax.rem(x, 2) * 4 + y, "ctx": z * 4 + (x // 2) * 2 + core}


def greet(devices):
    barrier = pltpu.get_barrier_semaphore()
    for device in devices:
        pl.semaphore_signal(barrier, inc=1, device_id=device, device_id_type=MESH)
    pl.semaphore_wait(barrier, len(devices))


def remote(src, dst, send, recv, device):
    return pltpu.make_async_remote_copy(
        src_ref=src, dst_ref=dst, send_sem=send, recv_sem=recv, device_id=device, device_id_type=MESH
    )


BLOCK = 256
TOKENS = 192
LENGTH = 3072
DMA = pltpu.SemaphoreType.DMA


def peers():
    fsdp, me = lax.axis_index("fsdp"), lax.axis_index("ctx")
    return me, [(lax.rem(me + d, 16), {"fsdp": fsdp, "ctx": lax.rem(me + d, 16)}) for d in range(1, 16)]


def exchange(src, dst, me, others, sends, recvs, local):
    copies = []
    for i, (other, device) in enumerate(others):
        copy = remote(src.at[other], dst.at[me], sends.at[i], recvs.at[i], device)
        copy.start()
        copies.append(copy)
    mine = pltpu.make_async_copy(src.at[me], dst.at[me], local)
    mine.start()
    return copies + [mine]


def wait_all(copies):
    for copy in copies:
        copy.wait()


def dot(a, b):
    return jnp.dot(a, b, preferred_element_type=F32)


def dot_nt(a, b):
    return lax.dot_general(a, b, (((1,), (1,)), ((), ())), preferred_element_type=F32)


def dot_tn(a, b):
    return lax.dot_general(a, b, (((0,), (0,)), ((), ())), preferred_element_type=F32)


def beside(a, b):
    return jnp.concatenate([a, b], axis=1)


def flipped(value):
    return value.astype(F32).T.astype(BF16)


def block_span(i, size):
    return pl.ds(pl.multiple_of(i * size, size), size)


class Gather:
    def __init__(self, sources, fulls, chunks, sems, at, pending):
        self.sources, self.fulls, self.chunks, self.pending = sources, fulls, chunks, pending
        self.sems = sems
        x, y, z, core = at
        self.y, self.core, self.low = y, core, lax.rem(x, 2)
        self.up, self.down = device_at(x, y + 1, z, core), device_at(x, y - 1, z, core)
        self.xs = [device_at(x + 1, y, z, core), device_at(x - 1, y, z, core)]
        self.sibling = device_at(x, y, z, core + 1)
        self.copies = {}

    def shard_rows(self, array):
        return self.sources[array].shape[0]

    def rows(self, c, block, way=None):
        array, first, count = self.chunks[c]
        rows = self.shard_rows(array)
        start = block * rows + self.core * (rows // 2) + first
        if way is not None:
            count = count // 2
            start = start + way * count
        return pl.ds(pl.multiple_of(start, 16), count)

    def block(self, e, far=False):
        side = 1 - self.low if far else self.low
        return side * 4 + lax.rem(self.y - e + 4, 4)

    def own(self, array, local):
        rows = self.shard_rows(array)
        copy = pltpu.make_async_copy(
            self.sources[array], self.fulls[array].at[block_span(self.block(0), rows)], local
        )
        copy.start()
        return copy

    def go(self, key, kind, c, slot, src, rows, device):
        full = self.fulls[self.chunks[c][0]]
        sends, recvs = self.sems[2 * kind : 2 * kind + 2]
        copy = remote(full.at[rows] if src is None else src, full.at[rows], sends.at[c, slot], recvs.at[c, slot], device)
        copy.start()
        self.copies[key, c, slot] = copy
        self.pending.append(copy)

    def start(self, c):
        source = self.sources[self.chunks[c][0]]
        mine = self.block(0)
        self.go("y", 0, c, 0, source.at[self.rows(c, 0)], self.rows(c, mine), self.up)
        self.go("y", 0, c, 1, source.at[self.rows(c, 0)], self.rows(c, mine), self.down)

    def start_x(self, c):
        source = self.sources[self.chunks[c][0]]
        mine = self.block(0)
        for way in (0, 1):
            self.go("x", 1, c, way, source.at[self.rows(c, 0, way)], self.rows(c, mine, way), self.xs[way])

    def along_x(self, c, e, way):
        self.go("x", 1, c, 2 * e + way, None, self.rows(c, self.block(e), way), self.xs[way])

    def to_core(self, c, slot, rows):
        self.go("c", 2, c, slot, None, rows, self.sibling)

    def relay(self, c):
        for slot, e, device in ((0, 1, self.up), (1, 3, self.down)):
            self.copies["y", c, slot].wait_recv()
            self.go("y", 0, c, 2 + slot, None, self.rows(c, self.block(e), slot), device)
            for way in (0, 1):
                self.along_x(c, e, way)
            self.to_core(c, slot, self.rows(c, self.block(e)))

    def last(self, c):
        for way in (0, 1):
            self.copies["y", c, 2 + way].wait_recv()
            self.along_x(c, 2, way)
        self.to_core(c, 2, self.rows(c, self.block(2)))

    def share(self, c):
        for e in (0, 1, 3, 2):
            for way in (0, 1):
                self.copies["x", c, 2 * e + way].wait_recv()
                self.to_core(c, 3 + 2 * e + way, self.rows(c, self.block(e, True), way))

    def settle(self, c):
        for slot in range(11):
            self.copies["c", c, slot].wait_recv()

    @staticmethod
    def scratch(n):
        return (DMA((n, 4)),) * 2 + (DMA((n, 8)),) * 2 + (DMA((n, 11)),) * 2


class PlaneGather:
    def __init__(self, source, full, sems, at, pending):
        x, y, z, core = at
        self.full, self.sems, self.at, self.pending = full, sems, at, pending
        self.source = source.at[pl.ds(pl.multiple_of(core * 64 + z * 16, 16), 16)]
        self.xs = [device_at(x + 1, y, z, core), device_at(x - 1, y, z, core)]
        self.ys = [device_at(x, y + 1, z, core), device_at(x, y - 1, z, core), device_at(x, y + 2, z, core)]
        self.zs = [device_at(x, y, z + 1, core), device_at(x, y, z - 1, core)]
        self.sibling = device_at(x, y, z, core + 1)
        self.moves = {}

    def go(self, slot, src, dst, device):
        copy = remote(src, dst, self.sems[0].at[slot], self.sems[1].at[slot], device)
        copy.start()
        self.moves[slot] = copy
        self.pending.append(copy)

    def block(self, e):
        x, y, z, core = self.at
        return self.full.at[lax.rem(x, 2) * 4 + lax.rem(y - e + 4, 4), core, z]

    def start(self, local):
        self.own = pltpu.make_async_copy(self.source, self.block(0), local)
        self.own.start()
        for slot in range(3):
            self.go(slot, self.source, self.block(0), self.ys[slot])
        self.go(3, self.source, self.block(0), self.xs[0])

    def along_x(self):
        for slot, e in ((0, 1), (1, 3), (2, 2)):
            self.moves[slot].wait_recv()
            self.go(3 + e, self.block(e), self.block(e), self.xs[e % 2])

    def along_z(self):
        _, _, z, core = self.at
        self.own.wait()
        for slot in range(3, 7):
            self.moves[slot].wait_recv()
        ref = self.full.at[:, core, z]
        for slot in range(2):
            self.go(7 + slot, ref, ref, self.zs[slot])
        self.go(10, ref, ref, self.sibling)

    def relay(self):
        _, _, z, core = self.at
        for slot, d in ((0, 3), (1, 1)):
            self.moves[7 + slot].wait_recv()
            ref = self.full.at[pl.ds(4 * slot, 4), core, lax.rem(z + d, 4)]
            self.go(9 + 5 * slot, ref, ref, self.zs[slot])
            ref = self.full.at[:, core, lax.rem(z + d, 4)]
            self.go(11 + slot, ref, ref, self.sibling)

    def to_core(self):
        _, _, z, core = self.at
        for slot in (9, 14):
            self.moves[slot].wait_recv()
        ref = self.full.at[:, core, lax.rem(z + 2, 4)]
        self.go(13, ref, ref, self.sibling)

    def settle(self):
        for slot in range(10, 14):
            self.moves[slot].wait_recv()

    @staticmethod
    def scratch():
        return (DMA((15,)),) * 2


CHUNKS = ((1, 0, 32), (1, 32, 32), (2, 0, 128), (2, 128, 128), (0, 0, 64))


def forward_kernel(x_in, small, w_qkv, w_out, w_in, w_back,
                   q_all, k_all, v_all, q_t, k_t, o_t, log_total, mixed, smalls, x_out, g_out, g_in, g_back, g_qkv,
                   x_all, tiles, w_got, w_head, v_t, o_send, o_got, scores_a, scores_b, high_a, high_b,
                   g_sems, q_sems, s_s, s_r, h_s, h_r, n_s, n_r, b_s, b_r, local):
    x, y, z, core = place()
    me, others = peers()
    low, high = lax.rem(x, 2), x // 2
    shard = low * 4 + y
    sibling = device_at(x, y, z, core + 1)
    pending, locals_ = [], []

    def begin(copy):
        copy.start()
        pending.append(copy)
        return copy

    def keep(src, dst, slot):
        copy = pltpu.make_async_copy(src, dst, local.at[slot])
        copy.start()
        return copy

    tile_copies = [
        keep(w_qkv.at[:, block_span(8 * i + me // 2, 128)], tiles.at[i], i) for i in range(3)
    ]
    x_all[me] = x_in[...].astype(BF16)
    across = [
        (lax.rem(low + a, 2), d) for a in (0, 1) for d in range(4) if (a, d) != (0, 0)
    ]
    across = [device_at(high * 2 + a, y + d, z, core) for a, d in across]
    greet([device for _, device in others] + across + [device_at(high * 2 - 1 + 3 * low, y, z, core)])

    def index(dz, dh, dk=0):
        return lax.rem(z + dz + 4, 4) * 4 + lax.rem(high + dh, 2) * 2 + lax.rem(core + dk, 2)

    up, down = device_at(x, y, z + 1, core), device_at(x, y, z - 1, core)
    first_half, second_half = pl.ds(0, 96), pl.ds(96, 96)

    def pass_on(slot, block, device, rows=None):
        ref = x_all.at[block] if rows is None else x_all.at[block, rows]
        return begin(remote(ref, ref, h_s.at[slot], h_r.at[slot], device))

    def share_rows(slot, block):
        ref = x_all.at[block]
        return begin(remote(ref, ref, n_s.at[slot], n_r.at[slot], sibling))

    moves = {1: pass_on(1, me, up), 2: pass_on(2, me, down), 0: pass_on(0, me, device_at(x + 2, y, z, core))}
    nears = [share_rows(7, me)]

    odd = lax.rem(me, 2) == 1
    for copy in tile_copies:
        copy.wait()

    def column_half(value):
        return jnp.where(odd, value[:, 64:128], value[:, 0:64])

    parts = [column_half(tiles[i].astype(F32)) for i in range(3)]
    w_got[shard, 0:128, :] = beside(parts[0], parts[1]).astype(BF16)
    w_got[shard, 128:192, :] = beside(parts[2][0:64], parts[2][64:128]).astype(BF16)
    w_got[shard, 192:208, :] = small[...]
    head_copies = []
    for i, device in enumerate(across):
        ref = w_got.at[shard]
        head_copies.append(begin(remote(ref, ref, s_s.at[i], s_r.at[i], device)))

    whole = Gather((w_out, w_in, w_back), (g_out, g_in, g_back), CHUNKS, g_sems, (x, y, z, core), pending)
    plane = PlaneGather(w_qkv, g_qkv, q_sems, (x, y, z, core), pending)
    plane.start(local.at[3])
    for c in range(2):
        whole.start(c)
        whole.start_x(c)
    for array in range(3):
        locals_.append(whole.own(array, local.at[4 + array]))

    for copy in head_copies:
        copy.wait_recv()
    for f in range(8):
        span = slice(128 * f, 128 * f + 128)
        w_head[span, 0:128] = w_got[f, 0:128, :]
        w_head[128 * f : 128 * f + 64, 128:192] = w_got[f, 128:192, 0:64]
        w_head[128 * f + 64 : 128 * f + 128, 128:192] = w_got[f, 128:192, 64:128]
        smalls[f] = w_got[f, 192:208, :]
    bias = w_got[me // 2, 192:208, :].astype(F32)
    bias = jnp.concatenate(
        [column_half(bias[0:1]), jnp.zeros((1, 64), F32), column_half(bias[1:2])], axis=1
    )
    scale = jnp.where(lax.broadcasted_iota(jnp.int32, (1, 192), 1) < 64, 0.125, 1.0)

    def project(block):
        value = ((dot(x_all[block], w_head[:, 0:192]) + bias) * scale).astype(BF16)
        rows = pl.ds(pl.multiple_of(block * TOKENS, 64), TOKENS)
        q_all[rows, :] = value[:, 0:64]
        k_all[rows, :] = value[:, 64:128]
        v_all[rows, :] = value[:, 128:192]

    project(me)
    moves[1].wait_recv()
    moves[4] = pass_on(4, index(-1, 0), up, first_half)
    moves[2].wait_recv()
    moves[5] = pass_on(5, index(1, 0), down, second_half)
    moves[0].wait_recv()
    moves[6] = pass_on(6, index(0, 1), up)
    moves[7] = pass_on(7, index(0, 1), down)
    nears += [share_rows(0, index(-1, 0)), share_rows(1, index(1, 0)), share_rows(2, index(0, 1))]
    plane.along_x()
    project(index(-1, 0))
    project(index(1, 0))
    project(index(0, 1))
    nears[0].wait_recv()
    project(index(0, 0, 1))
    whole.relay(0)
    whole.start(2)
    whole.start_x(2)
    moves[4].wait_recv()
    moves[5].wait_recv()
    nears.append(share_rows(3, index(2, 0)))
    project(index(2, 0))
    moves[6].wait_recv()
    moves[8] = pass_on(8, index(-1, 1), up, first_half)
    moves[7].wait_recv()
    moves[9] = pass_on(9, index(1, 1), down, second_half)
    nears += [share_rows(4, index(-1, 1)), share_rows(5, index(1, 1))]
    whole.relay(1)
    whole.start(3)
    whole.start_x(3)
    whole.last(0)
    for i, spot in enumerate(((-1, 0), (1, 0), (0, 1), (2, 0))):
        nears[1 + i].wait_recv()
        project(index(*spot, 1))
    project(index(-1, 1))
    project(index(1, 1))
    for i, spot in enumerate(((-1, 1), (1, 1))):
        nears[5 + i].wait_recv()
        project(index(*spot, 1))
    moves[8].wait_recv()
    moves[9].wait_recv()
    nears.append(share_rows(6, index(2, 1)))
    project(index(2, 1))
    nears[7].wait_recv()
    project(index(2, 1, 1))
    kept = keep(x_all, x_out, 7)
    whole.relay(2)
    whole.last(1)
    whole.start(4)
    whole.start_x(4)
    whole.share(0)
    plane.along_z()

    for i in range(LENGTH // BLOCK):
        span = slice(BLOCK * i, BLOCK * i + BLOCK)
        q_t[:, span] = flipped(q_all[span, :])
        k_t[:, span] = flipped(k_all[span, :])
        v_t[0:64, span] = flipped(v_all[span, :])
    v_t[64:80, :] = jnp.ones((16, LENGTH), BF16)

    def make_scores(i, scores, highest):
        value = dot(k_all[...], q_t[:, block_span(i, BLOCK)])
        scores[...] = value
        highest[...] = jnp.max(value, axis=0, keepdims=True)

    def mix(i, scores, highest):
        span = block_span(i, BLOCK)
        out = dot(v_t[...], jnp.exp(scores[...] - highest[...]).astype(BF16))
        total = out[64:65]
        o_t[:, span] = (out[0:64] / total).astype(BF16)
        log_total[:, span] = highest[...] + jnp.log(total)

    def two_blocks(i, _):
        make_scores(2 * i + 1, scores_b, high_b)
        mix(2 * i, scores_a, high_a)
        make_scores(jnp.minimum(2 * i + 2, LENGTH // BLOCK - 1), scores_a, high_a)
        mix(2 * i + 1, scores_b, high_b)
        return 0

    make_scores(0, scores_a, high_a)
    lax.fori_loop(0, 1, two_blocks, 0)
    whole.relay(3)
    whole.last(2)
    whole.share(1)
    lax.fori_loop(1, 2, two_blocks, 0)
    plane.relay()
    whole.relay(4)
    whole.last(3)
    whole.share(2)
    lax.fori_loop(2, 4, two_blocks, 0)
    plane.to_core()
    whole.last(4)
    whole.share(3)
    lax.fori_loop(4, 6, two_blocks, 0)
    for j in range(16):
        part = o_t[:, j * 192 : (j + 1) * 192].astype(F32)
        o_send[j] = jnp.concatenate([part[:, 0:96], part[:, 96:192]], axis=0).T.astype(BF16)
    copies = exchange(o_send, o_got, me, others, b_s, b_r, local.at[8])
    whole.share(4)
    wait_all(copies)
    for p in range(8):
        a, b = o_got[2 * p].astype(F32), o_got[2 * p + 1].astype(F32)
        span = slice(128 * p, 128 * p + 128)
        mixed[0:96, span] = beside(a[:, 0:64], b[:, 0:64]).astype(BF16)
        mixed[96:192, span] = beside(a[:, 64:128], b[:, 64:128]).astype(BF16)
    for c in range(len(CHUNKS)):
        whole.settle(c)
    plane.settle()
    for copy in pending:
        copy.wait_send()
    wait_all(locals_)
    kept.wait()


def forward(x_in, small, w_qkv, w_out, w_in, w_back):
    vmem, far = pl.BlockSpec(memory_space=pltpu.VMEM), pl.BlockSpec(memory_space=pl.ANY)
    n = len(CHUNKS)
    shape = jax.ShapeDtypeStruct
    return pl.pallas_call(
        forward_kernel,
        out_shape=(
            shape((LENGTH, 64), BF16),
            shape((LENGTH, 64), BF16),
            shape((LENGTH, 64), BF16),
            shape((64, LENGTH), BF16),
            shape((64, LENGTH), BF16),
            shape((64, LENGTH), BF16),
            shape((1, LENGTH), F32),
            shape((TOKENS, 1024), BF16),
            shape((8, 16, 128), BF16),
            shape((16, TOKENS, 1024), BF16),
            shape((1024, 1024), BF16),
            shape((1024, 4096), BF16),
            shape((4096, 1024), BF16),
            shape((8, 2, 4, 16, 3072), BF16),
        ),
        in_specs=[vmem] * 6,
        out_specs=(vmem,) * 9 + (far,) * 5,
        scratch_shapes=[
            pltpu.VMEM((16, TOKENS, 1024), BF16),
            pltpu.VMEM((3, 128, 128), BF16),
            pltpu.VMEM((8, 208, 128), BF16),
            pltpu.VMEM((1024, 256), BF16),
            pltpu.VMEM((80, LENGTH), BF16),
            pltpu.VMEM((16, 96, 128), BF16),
            pltpu.VMEM((16, 96, 128), BF16),
            pltpu.VMEM((LENGTH, BLOCK), F32),
            pltpu.VMEM((LENGTH, BLOCK), F32),
            pltpu.VMEM((1, BLOCK), F32),
            pltpu.VMEM((1, BLOCK), F32),
            Gather.scratch(n),
            PlaneGather.scratch(),
            DMA((7,)), DMA((7,)),
            DMA((10,)), DMA((10,)),
            DMA((8,)), DMA((8,)),
            DMA((15,)), DMA((15,)),
            DMA((10,)),
        ],
        compiler_params=pltpu.CompilerParams(collective_id=1, has_side_effects=True, vmem_limit_bytes=60 * MIB),
        name="forward_attention",
    )(x_in, small, w_qkv, w_out, w_in, w_back)


TURNS = (2, 1, 0, 1, 0, 1, 2, 1, 0)
PIECES = (((4, 4), (2, 4, 2), (2, 4, 2)), ((4,), (2, 2), (4,)), ((), (), ()))


class Sum:
    def __init__(self, acc, bufs, final, out, sems, at, pending):
        self.acc, self.bufs, self.final, self.out = acc, bufs, final, out
        self.sems, self.at, self.pending = sems, at, pending
        self.mine = block_span(at[3], 512)
        self.sibling = device_at(*at[:3], at[3] + 1)
        self.copies = {}

    def line(self, axis, d):
        to = list(self.at[:3])
        to[axis] = lax.rem(to[axis] + d, 4)
        return to[axis], device_at(*to, self.at[3])

    def piece(self, stage, u, c):
        turn = TURNS[u]
        if stage == 0:
            ref = self.acc.at[u]
            if turn == 0:
                return ref.at[lax.rem(c, 2), :, :, c // 2]
            return ref.at[:, c] if turn == 1 else ref.at[:, :, c]
        ref = self.piece(stage - 1, u, self.at[(turn + stage - 1) % 3])
        if (turn + stage) % 3 == 0:
            return ref.at[lax.rem(c, 2), c // 2] if turn == 1 else ref.at[lax.rem(c, 2), :, c // 2]
        return ref.at[:, c] if turn == 1 else ref.at[c]

    def buffer(self, stage, u):
        turn = TURNS[u]
        return self.bufs[stage][turn].at[TURNS[:u].count(turn)]

    def start(self, stage, *units):
        sends, recvs = self.sems[2 * stage : 2 * stage + 2]
        for u in units:
            axis = (TURNS[u] + stage) % 3
            for d in (1, 3, 2):
                c, device = self.line(axis, d)
                copy = remote(
                    self.piece(stage, u, c),
                    self.buffer(stage, u).at[d - 1],
                    sends.at[u, d - 1],
                    recvs.at[u, d - 1],
                    device,
                )
                copy.start()
                self.copies[stage, u, d] = copy
                self.pending.append(copy)

    def finish(self, stage, *units):
        for u in units:
            for d in (1, 3, 2):
                self.copies[stage, u, d].wait_recv()
            own = self.piece(stage, u, self.at[(TURNS[u] + stage) % 3])
            buf = self.buffer(stage, u)
            total = own[...].astype(F32) + buf[0].astype(F32) + buf[1].astype(F32) + buf[2].astype(F32)
            if stage == 2:
                self.final[u] = total.astype(BF16)
            else:
                own[...] = total.astype(BF16)
                self.start(stage + 1, u)

    def go(self, key, slot, src, dst, device):
        sends, recvs = self.sems[6:8] if key == "far" else self.sems[8:10]
        copy = remote(src, dst, sends.at[slot], recvs.at[slot], device)
        copy.start()
        self.copies[key, slot] = copy
        self.pending.append(copy)

    def spot(self, dz, dh):
        x, y, z, core = self.at
        return self.out.at[:, lax.rem(z + dz, 4), lax.rem(x // 2 + dh, 2), :, self.mine]

    def spread(self, local):
        mine = self.spot(0, 0)
        self.go("far", 0, self.final, mine, self.line(0, 2)[1])
        for d in (1, 3, 2):
            self.go("far", d, self.final, mine, self.line(2, d)[1])
        self.go("near", 0, self.final, mine, self.sibling)
        own = pltpu.make_async_copy(self.final, mine, local)
        own.start()
        own.wait()

    def relay(self):
        self.copies["far", 0].wait_recv()
        ref = self.spot(0, 1)
        for d in (1, 3, 2):
            self.go("far", 3 + d, ref, ref, self.line(2, d)[1])
        self.go("near", 1, ref, ref, self.sibling)

    def share(self):
        for dh in (0, 1):
            for d in (1, 3, 2):
                self.copies["far", 3 * dh + d].wait_recv()
                ref = self.spot(4 - d, dh)
                self.go("near", 1 + 3 * dh + d, ref, ref, self.sibling)

    def end(self):
        for slot in range(8):
            self.copies["near", slot].wait_recv()

    @staticmethod
    def scratch():
        bufs = tuple(
            tuple(
                pltpu.VMEM((TURNS.count(turn), 3) + shapes[turn] + (16, 512), BF16) for turn in range(3)
            )
            for shapes in PIECES
        )
        n = len(TURNS)
        return (
            bufs,
            pltpu.VMEM((n, 16, 512), BF16),
            (DMA((n, 3)),) * 6 + (DMA((7,)),) * 2 + (DMA((8,)),) * 2,
        )


def backward_kernel(gm, q_all, k_all, v_all, q_t, k_t, o_t, log_total, grad_first, sm_in,
                    x_far, first_low, mixed, act, gs, gfl, gp, g_far,
                    grad_input, out, qkv_out, sm_out,
                    x_all, g_qkv, sm, back, send, do_got, do_all, do_t, delta, dq_t, dk, dv,
                    lhs, rhs, gproj, head_t, head_send, head_got, head_sum, acc, sum_a, s0, s1, s2, s3,
                    a_s, a_r, b_s, b_r, n_s, n_r, t_s, t_r, h_s, h_r, p_s, p_r, local):
    x, y, z, core = at = place()
    me, others = peers()
    low = lax.rem(x, 2)
    shard = low * 4 + y
    sibling = device_at(x, y, z, core + 1)
    pending = []

    def keep(src, dst, slot):
        copy = pltpu.make_async_copy(src, dst, local.at[slot])
        copy.start()
        return copy

    for h in range(16):
        part = gm[:, 64 * h : 64 * h + 64].astype(F32)
        send[h, 0:96, :] = beside(part[0:96], part[96:192]).astype(BF16)
    across = [(a, d) for a in (0, 1) for d in range(4) if (a, d) != (0, 0)]
    across = [
        (lax.rem(low + a, 2) * 4 + lax.rem(y + d, 4), device_at(x // 2 * 2 + lax.rem(low + a, 2), y + d, z, core))
        for a, d in across
    ]
    greet([device for _, device in others] + [device for _, device in across]
          + [device_at(x // 2 * 2 - 1 + 3 * low, y, z, core)])
    a_copies = exchange(send.at[:, 0:96], do_got, me, others, a_s, a_r, local.at[0])

    near = []
    upper, lower = pl.ds(0, TOKENS), pl.ds(TOKENS, TOKENS)
    moves = [
        (mixed, None, lhs, 1024, 1024),
        (gfl, 512, rhs, 512, 512),
        (first_low, None, lhs, 0, 1024),
        (gp, 2048, rhs, 1024, 2048),
        (act, None, lhs, 2048, 4096),
        (gs, 512, rhs, 0, 512),
    ]
    for i, (src, cols, dst, first, count) in enumerate(moves):
        own = src if cols is None else src.at[:, block_span(core, cols)]
        other = src if cols is None else src.at[:, block_span(1 - core, cols)]
        span = pl.ds(first, count)
        copy = remote(other, dst.at[lower, span], n_s.at[i], n_r.at[i], sibling)
        copy.start()
        near.append((copy, keep(own, dst.at[upper, span], 1 + i)))
        pending.append(copy)
    x_copy = keep(x_far, x_all, 7)
    g_copy = keep(g_far, g_qkv, 8)
    dk[...] = jnp.zeros_like(dk)
    dv[...] = jnp.zeros_like(dv)
    sums = Sum(acc, sum_a[0], sum_a[1], out, sum_a[2], at, pending)

    def arrive(*which):
        for i in which:
            near[i][0].wait_recv()
            near[i][1].wait()

    def product(unit, first, column):
        for side in range(2):
            value = dot_tn(lhs[:, first + 512 * side : first + 512 * side + 512], rhs[:, column : column + 512])
            acc[unit, side] = value.astype(BF16).reshape(4, 4, 2, 16, 512)
        sums.start(0, unit)

    arrive(0, 1)
    product(0, 1024, 512)
    arrive(2, 3)
    for j in range(4):
        product(1 + j, 0, 1024 + 512 * j)
    arrive(4, 5)
    for j in range(4):
        for side in range(2):
            left = jnp.concatenate(
                [lhs[:, 2048 + 512 * f + 128 * j : 2176 + 512 * f + 128 * j] for f in range(4 * side, 4 * side + 4)],
                axis=1,
            )
            acc[5 + j, side] = dot_tn(left, rhs[:, 0:512]).astype(BF16).reshape(4, 4, 2, 16, 512)
        sums.start(0, 5 + j)

    wait_all(a_copies)
    for j in range(16):
        span = slice(j * 192, (j + 1) * 192)
        do_all[j * 192 : j * 192 + 96, :] = do_got[j, :, 0:64]
        do_all[j * 192 + 96 : j * 192 + 192, :] = do_got[j, :, 64:128]
        pair = do_got[j].astype(F32).T
        flat = beside(pair[0:64], pair[64:128])
        do_t[:, span] = flat.astype(BF16)
        delta[:, span] = jnp.sum(flat * o_t[:, span].astype(F32), axis=0, keepdims=True)

    def block(i, _):
        span = block_span(i, BLOCK)
        prob = jnp.exp(dot(k_all[...], q_t[:, span]) - log_total[:, span])
        grad_prob = dot(v_all[...], do_t[:, span])
        dv[...] += dot(prob.astype(BF16), do_all[span, :])
        grad_scores = (prob * (grad_prob - delta[:, span])).astype(BF16)
        dk[...] += dot(grad_scores, q_all[span, :])
        dq_t[:, span] = dot(k_t[...], grad_scores) * 0.125
        return 0

    lax.fori_loop(0, 5, block, 0)
    sums.finish(0, 0, 1)
    lax.fori_loop(5, 9, block, 0)
    sums.finish(0, 2, 3)
    lax.fori_loop(9, 12, block, 0)
    sum_q = jnp.zeros((1, 64), F32)
    for j in range(16):
        span = slice(j * 192, (j + 1) * 192)
        dq = dq_t[:, span].T
        sum_q = sum_q + jnp.sum(dq, axis=0, keepdims=True)
        send[j, 0:192, :] = beside(dq, dk[span, :]).astype(BF16)
        send[j, 192:288, :] = beside(
            dv[j * 192 : j * 192 + 96, :], dv[j * 192 + 96 : j * 192 + 192, :]
        ).astype(BF16)
    b_copies = exchange(send, back, me, others, b_s, b_r, local.at[0])
    sums.finish(0, 4, 5)

    for i in range(LENGTH // BLOCK):
        span = slice(BLOCK * i, BLOCK * i + BLOCK)
        head_t[0:64, span] = dq_t[:, span].astype(BF16)
        head_t[64:128, span] = dk[span, :].T.astype(BF16)
        head_t[128:192, span] = dv[span, :].T.astype(BF16)
    x_copy.wait()
    head = dot(head_t[...], x_all[...].reshape(LENGTH, 1024))
    for f in range(8):
        head_send[f] = head[:, 128 * f : 128 * f + 128].astype(BF16)
    head_copies = []
    for i, (to, device) in enumerate(across):
        copy = remote(head_send.at[to], head_got.at[shard], h_s.at[i], h_r.at[i], device)
        copy.start()
        head_copies.append(copy)
    head_copies.append(keep(head_send.at[shard], head_got.at[shard], 9))

    sm[...] = sm_in[...]
    odd = lax.rem(me, 2) == 1
    blank = jnp.zeros((1, 64), F32)
    owner = me // 2
    for i, value in enumerate((sum_q, jnp.sum(dv[...], axis=0, keepdims=True))):
        sm[owner // 4, lax.rem(owner, 4), i : i + 1, :] = jnp.where(odd, beside(blank, value), beside(value, blank))
    t_copy = remote(sm, s0, t_s.at[0], t_r.at[0], sibling)
    t_copy.start()

    def small_start(stage, axis, piece, buf):
        copies = []
        for d in (1, 2, 3):
            c, device = sums.line(axis, d)
            slot = 1 + 3 * stage + d - 1
            copies.append(remote(piece(c), buf.at[at[axis]], t_s.at[slot], t_r.at[slot], device))
            copies[-1].start()
        return copies + [keep(piece(at[axis]), buf.at[at[axis]], 10 + stage)]

    sums.finish(0, 6, 7, 8)
    sums.finish(1, 0, 1, 2, 3)
    t_copy.wait()
    s0[...] = s0[...] + sm[...]
    small = small_start(0, 1, lambda c: s0.at[:, c], s1)
    wait_all(head_copies)
    total = head_got[0].astype(F32)
    for f in range(1, 8):
        total = total + head_got[f].astype(F32)
    head_sum[...] = total.astype(BF16)
    plane = [(dh, dz) for dh in (0, 1) for dz in (1, 3, 2, 0) if (dh, dz) != (0, 0)]
    p_own = keep(head_sum, qkv_out.at[me], 13)
    p_copies, p_near = [], []
    for i, (dh, dz) in enumerate(plane):
        copy = remote(
            head_sum, qkv_out.at[me], p_s.at[i], p_r.at[i], device_at(x + 2 * dh, y, z + dz, core)
        )
        copy.start()
        p_copies.append(copy)
        pending.append(copy)
    p_near.append(remote(head_sum, qkv_out.at[me], p_s.at[7], p_r.at[7], sibling))
    p_near[0].start()
    sums.finish(1, 4, 5, 6, 7, 8)
    wait_all(small)
    s0[:, 0] = s1[0] + s1[1] + s1[2] + s1[3]
    small = small_start(1, 0, lambda c: s0.at[lax.rem(c, 2), 0], s2)
    sums.finish(2, *range(9))
    sums.spread(local.at[14])
    wait_all(b_copies)
    for p in range(8):
        a, b = back[2 * p].astype(F32), back[2 * p + 1].astype(F32)
        for i, part in enumerate((slice(0, 64), slice(64, 128))):
            cols = slice(1024 * i + 128 * p, 1024 * i + 128 * p + 128)
            gproj[:, cols] = beside(a[0:192, part], b[0:192, part]).astype(BF16)
            gproj[96 * i : 96 * i + 96, 2048 + 128 * p : 2176 + 128 * p] = beside(
                a[192:288, part], b[192:288, part]
            ).astype(BF16)
    sums.relay()
    wait_all(small)
    s0[0, 1] = s2[0] + s2[1] + s2[2] + s2[3]
    small = small_start(2, 2, lambda c: s0.at[0, 1], s3)
    for i, (dh, dz) in enumerate(plane):
        p_copies[i].wait_recv()
        ref = qkv_out.at[lax.rem(z - dz + 4, 4) * 4 + lax.rem(x // 2 + dh, 2) * 2 + core]
        copy = remote(ref, ref, p_s.at[8 + i], p_r.at[8 + i], sibling)
        copy.start()
        p_near.append(copy)
    g_copy.wait()
    grad_input[...] = grad_first[...] + dot_nt(gproj[...], g_qkv[...])
    wait_all(small)
    sm_out[...] = s3[0] + s3[1] + s3[2] + s3[3]
    sums.share()
    p_own.wait()
    wait_all(p_near)
    sums.end()
    for copy in pending:
        copy.wait_send()


def backward(gm, q_all, k_all, v_all, q_t, k_t, o_t, log_total, grad_first, sm,
             x_far, first_low, mixed, act, gs, gfl, gp, g_far):
    vmem, far = pl.BlockSpec(memory_space=pltpu.VMEM), pl.BlockSpec(memory_space=pl.ANY)
    shape = jax.ShapeDtypeStruct
    return pl.pallas_call(
        backward_kernel,
        out_shape=(
            shape((TOKENS, 1024), F32),
            shape((9, 4, 2, 16, 1024), BF16),
            shape((16, 192, 128), BF16),
            shape((16, 128), F32),
        ),
        in_specs=[vmem] * 10 + [far] * 8,
        out_specs=(vmem,) * 4,
        scratch_shapes=[
            pltpu.VMEM((16, TOKENS, 1024), BF16),
            pltpu.VMEM((1024, 3072), BF16),
            pltpu.VMEM((2, 4, 16, 128), F32),
            pltpu.VMEM((16, 288, 128), BF16),
            pltpu.VMEM((16, 288, 128), BF16),
            pltpu.VMEM((16, 96, 128), BF16),
            pltpu.VMEM((LENGTH, 64), BF16),
            pltpu.VMEM((64, LENGTH), BF16),
            pltpu.VMEM((1, LENGTH), F32),
            pltpu.VMEM((64, LENGTH), F32),
            pltpu.VMEM((LENGTH, 64), F32),
            pltpu.VMEM((LENGTH, 64), F32),
            pltpu.VMEM((2 * TOKENS, 6144), BF16),
            pltpu.VMEM((2 * TOKENS, 3072), BF16),
            pltpu.VMEM((TOKENS, 3072), BF16),
            pltpu.VMEM((192, LENGTH), BF16),
            pltpu.VMEM((8, 192, 128), BF16),
            pltpu.VMEM((8, 192, 128), BF16),
            pltpu.VMEM((192, 128), BF16),
            pltpu.VMEM((9, 2, 4, 4, 2, 16, 512), BF16),
            Sum.scratch(),
            pltpu.VMEM((2, 4, 16, 128), F32),
            pltpu.VMEM((4, 2, 16, 128), F32),
            pltpu.VMEM((4, 16, 128), F32),
            pltpu.VMEM((4, 16, 128), F32),
            DMA((15,)), DMA((15,)),
            DMA((15,)), DMA((15,)),
            DMA((6,)), DMA((6,)),
            DMA((10,)), DMA((10,)),
            DMA((7,)), DMA((7,)),
            DMA((15,)), DMA((15,)),
            DMA((15,)),
        ],
        compiler_params=pltpu.CompilerParams(collective_id=2, has_side_effects=True, vmem_limit_bytes=62 * MIB),
        name="backward_attention",
    )(gm, q_all, k_all, v_all, q_t, k_t, o_t, log_total, grad_first, sm,
      x_far, first_low, mixed, act, gs, gfl, gp, g_far)


def unpack_kernel(out, heads, small, o_qkv, o_out, o_in, o_back, o_bin, *vectors):
    for i, vector in enumerate(vectors):
        vector[...] = small[i : i + 1, :]
    o_bin[...] = jnp.concatenate([small[i : i + 1, :] for i in range(8, 12)], axis=1)

    def unit(u):
        return out[u].reshape(128, 1024).astype(F32)

    o_out[...] = unit(0)
    for j in range(4):
        value = unit(1 + j)
        o_in[:, 512 * j : 512 * j + 512] = value[:, 0:512]
        o_in[:, 2048 + 512 * j : 2560 + 512 * j] = value[:, 512:1024]
        o_back[128 * j : 128 * j + 128, :] = unit(5 + j)
    for i in range(3):
        part = slice(64 * i, 64 * i + 64)
        for p in range(8):
            both = jnp.concatenate([heads[2 * p, part, :], heads[2 * p + 1, part, :]], axis=0)
            o_qkv[:, 1024 * i + 128 * p : 1024 * i + 128 * p + 128] = both.astype(F32).T


def unpack(out, heads, small):
    shape = jax.ShapeDtypeStruct
    vmem = pl.BlockSpec(memory_space=pltpu.VMEM)
    return pl.pallas_call(
        unpack_kernel,
        out_shape=(shape((128, 3072), F32), shape((128, 1024), F32), shape((128, 4096), F32), shape((512, 1024), F32),
                   shape((1, 512), F32)) + (shape((1, 128), F32),) * 8,
        in_specs=[vmem] * 3,
        out_specs=(vmem,) * 13,
        compiler_params=pltpu.CompilerParams(vmem_limit_bytes=30 * MIB),
        name="unpack_gradients",
    )(out, heads, small)


def widened(values):
    return values.astype(F32)


def layer_norm(hidden, gain, offset):
    center = hidden - jnp.mean(hidden, axis=-1, keepdims=True)
    inverse = lax.rsqrt(jnp.mean(center * center, axis=-1, keepdims=True) + EPSILON)
    normed = center * inverse
    return (normed * gain + offset, normed, inverse)


def norm_back(upstream, normed, inverse, gain):
    scaled = upstream * gain
    return inverse * (
        scaled
        - jnp.mean(scaled, axis=-1, keepdims=True)
        - normed * jnp.mean(scaled * normed, axis=-1, keepdims=True)
    )


def gelu_value(inputs):
    return 0.5 * inputs * (1.0 + jax.scipy.special.erf(inputs * ROOT_HALF))


def gelu_slope(inputs):
    return (
        0.5 * (1.0 + jax.scipy.special.erf(inputs * ROOT_HALF))
        + inputs * jnp.exp(-0.5 * inputs * inputs) * INV_ROOT_TWO_PI
    )


def shards(layer_input, cotangent, w_qkv, b_q, b_v, w_out, b_out, g_attn, beta_attn, w_in, b_in, w_back, b_back,
           g_mlp, beta_mlp):
    width = layer_input.shape[-1]
    small = jnp.concatenate(
        [jnp.stack([b_q, b_v, b_out, g_attn, beta_attn, b_back, g_mlp, beta_mlp]), b_in.reshape(4, 128),
         jnp.zeros((4, 128), BF16)]
    )
    rows = layer_input.reshape(-1, width)
    (q_all, k_all, v_all, q_t, k_t, o_t, log_total, mixed, smalls, x_all, g_out, g_in, g_back, g_qkv) = forward(
        rows, small, w_qkv, w_out, w_in, w_back
    )
    g_qkv = g_qkv.reshape(width, 3 * width)
    smalls = widened(smalls)
    _, _, bout, gattn, battn, bback, gmlp, bmlp = (smalls[:, i].reshape(width) for i in range(8))
    bin_ = smalls[:, 8:12].reshape(4 * width)

    first_sum = rows + dot(mixed, g_out) + bout
    first_out, first_normed, first_inverse = layer_norm(first_sum, gattn, battn)
    first_low = first_out.astype(BF16)
    pre_act = dot(first_low, g_in) + bin_
    activated = gelu_value(pre_act).astype(BF16)
    second_sum = first_out + dot(activated, g_back) + bback
    output, second_normed, second_inverse = layer_norm(second_sum, gmlp, bmlp)

    upstream = cotangent.reshape(-1, width)
    grad_g_mlp = jnp.sum(upstream * second_normed, axis=0)
    grad_beta_mlp = jnp.sum(upstream, axis=0)
    grad_second = norm_back(upstream, second_normed, second_inverse, gmlp)
    grad_b_back = jnp.sum(grad_second, axis=0)
    grad_second_low = grad_second.astype(BF16)
    grad_pre = dot_nt(grad_second_low, g_back) * gelu_slope(pre_act)
    grad_b_in = jnp.sum(grad_pre, axis=0)
    grad_pre_low = grad_pre.astype(BF16)
    grad_first_out = grad_second + dot_nt(grad_pre_low, g_in)
    grad_g_attn = jnp.sum(grad_first_out * first_normed, axis=0)
    grad_beta_attn = jnp.sum(grad_first_out, axis=0)
    grad_first = norm_back(grad_first_out, first_normed, first_inverse, gattn)
    grad_b_out = jnp.sum(grad_first, axis=0)
    grad_first_low = grad_first.astype(BF16)
    grad_mixed = dot_nt(grad_first_low, g_out).astype(BF16)

    blank = jnp.zeros((width,), F32)
    sm = jnp.stack(
        [blank, blank, grad_b_out, grad_g_attn, grad_beta_attn, grad_b_back, grad_g_mlp, grad_beta_mlp]
    )
    sm = jnp.concatenate(
        [sm.reshape(8, 8, 128).transpose(1, 0, 2), grad_b_in.reshape(8, 4, 128), jnp.zeros((8, 4, 128), F32)], axis=1
    ).reshape(2, 4, 16, 128)
    grad_input, owned, heads, own_small = backward(
        grad_mixed, q_all, k_all, v_all, q_t, k_t, o_t, log_total, grad_first, sm,
        x_all, first_low, mixed, activated, grad_second_low, grad_first_low, grad_pre_low, g_qkv
    )
    o_qkv, o_out, o_in, o_back, o_bin, *vectors = unpack(owned, heads, own_small)
    vectors = [vector.reshape(128) for vector in vectors]
    return (
        output.reshape(layer_input.shape),
        grad_input.reshape(layer_input.shape),
        o_qkv,
        vectors[0],
        vectors[1],
        o_out,
        vectors[2],
        vectors[3],
        vectors[4],
        o_in,
        o_bin.reshape(512),
        o_back,
        vectors[5],
        vectors[6],
        vectors[7],
    )


def solution(mesh):
    big, mat, vec = P("fsdp", "ctx", None), P("fsdp", None), P("fsdp")
    params = (mat, vec, vec, mat, vec, vec, vec, mat, vec, mat, vec, vec, vec)
    return jax.shard_map(
        shards, mesh=mesh, in_specs=(big, big) + params, out_specs=(big, big) + params, check_vma=False
    )
```
